128 devices in a mesh: ep: 16 (over z, x), tp: 8 (over y, core).
Axes of the slice: x: 4, y: 4, z: 4, core: 2. Of those that a mesh axis runs over, the one named last changes fastest.
Arguments:
- tokens: bfloat16 [2048, 2880], P('ep'), may hold values from -6 to 6
- seq_lengths: int32 [16, 2], replicated, may hold values from 0 to 128, as said below
- expert_ids: int32 [2048, 4], P('ep'), may hold values from 0 to 15, all different within a row; in each aligned block of 128 rows (0 to 127, 128 to 255, ...) at most 48 rows name the same one
- first_gain: float32 [2880], replicated, may hold values from 0.5 to 1.5
- query_weight: bfloat16 [2880, 4096], P(None, 'tp'), may hold values from -0.109375 to 0.109375
- key_matrix: bfloat16 [2880, 512], P(None, 'tp'), may hold values from -0.109375 to 0.109375
- value_matrix: bfloat16 [2880, 512], P(None, 'tp'), may hold values from -0.109375 to 0.109375
- query_bias: float32 [4096], P('tp'), may hold values from -2 to 2
- key_offset_bias: float32 [512], P('tp'), may hold values from -2 to 2
- value_offset_bias: float32 [512], P('tp'), may hold values from -2 to 2
- head_sink_logits: float32 [64], P('tp'), may hold values from 1 to 4
- output_weight: bfloat16 [4096, 2880], P('tp'), may hold values from -0.75 to 0.75
- output_bias: float32 [2880], replicated, may hold values from -2 to 2
- second_gain: float32 [2880], replicated, may hold values from 0.5 to 1.5
- router_weight: bfloat16 [2880, 16], replicated, may hold values from -0.0546875 to 0.0546875
- router_bias: float32 [16], replicated, may hold values from -1 to 1
- expert_gateup: bfloat16 [16, 2, 2880, 2880], P('ep', None, None, 'tp'), may hold values from -0.109375 to 0.109375
- gateup_bias: float32 [16, 2, 2880], P('ep', None, 'tp'), may hold values from -1 to 1
- expert_down: bfloat16 [16, 2880, 2880], P('ep', 'tp'), may hold values from -0.109375 to 0.109375
- down_bias: float32 [16, 2880], P('ep'), may hold values from -1 to 1
- cotangent: bfloat16 [2048, 2880], P('ep'), may hold values from -6 to 6
Outputs:
- layer_output: bfloat16 [2048, 2880], P('ep')
- grad_tokens: float32 [2048, 2880], P('ep')
- grad_first_gain: float32 [2880], replicated
- grad_query_weight: float32 [2880, 4096], P(None, 'tp')
- grad_key_weight: float32 [2880, 512], P(None, 'tp')
- grad_value_weight: float32 [2880, 512], P(None, 'tp')
- grad_query_bias: float32 [4096], P('tp')
- grad_key_bias: float32 [512], P('tp')
- grad_value_bias: float32 [512], P('tp')
- grad_sink_logits: float32 [64], P('tp')
- grad_output_weight: float32 [4096, 2880], P('tp')
- grad_output_bias: float32 [2880], replicated
- grad_second_gain: float32 [2880], replicated
- grad_router_weight: float32 [2880, 16], replicated
- grad_router_bias: float32 [16], replicated
- grad_expert_gateup: float32 [16, 2, 2880, 2880], P('ep', None, None, 'tp')
- grad_gateup_bias: float32 [16, 2, 2880], P('ep', None, 'tp')
- grad_expert_down: float32 [16, 2880, 2880], P('ep', 'tp')
- grad_down_bias: float32 [16, 2880], P('ep')
The draws below stay inside these ranges and needn't reach their ends.
Inputs may be any that keep to these rules, and one draw needn't show every extreme that they name: `seq_lengths`: for each token group, entry 0 is more than half of 128 and the two entries sum to at most 128; the rows after both sequences form a third one. Some group holds a single sequence of 128 tokens. `expert_ids`: each row names 4 different experts; among the 128 rows of one token group no expert is named more than 48 times, a bound that some block reaches.
All inputs are finite; a program needn't handle non-finite values.
Results may differ from the reference program's by a relative error of at most 0.023.
Values may be sent and summed in bfloat16 or wider, within the bound.
A program may use at most 192 MiB of HBM per device.

```python
import math
from functools import partial
import jax
import jax.numpy as jnp
import numpy as np
from jax import lax

MODEL_DIM = 2880
QUERY_HEADS = 64
KEY_VALUE_HEADS = 8
HEAD_SIZE = 64
FF = 2880
TOPK = 4
TOK_DEV = 128
TOKENS = 2048
EXPERTS = 16
CAP = 48
N_EP = 16


def draw_seq_lengths(key, part):
    key = jax.random.fold_in(key, 11)
    first_key, second_key, pick_key = jax.random.split(key, 3)
    first_length = jax.random.randint(first_key, (N_EP,), TOK_DEV // 2 + 1, TOK_DEV + 1)
    chosen_group = jax.random.randint(pick_key, (), 0, N_EP)
    first_length = jnp.where(jnp.arange(N_EP) == chosen_group, TOK_DEV, first_length)
    second_length = jax.random.randint(second_key, (N_EP,), 0, 1 << 20) % (TOK_DEV - first_length + 1)
    return jnp.stack([first_length, second_length], axis=1).astype(jnp.int32)


def steps_of(stream_key, extent, shards, least, largest):
    def one(position, parts):
        heights = jax.random.uniform(jax.random.fold_in(jax.random.fold_in(stream_key, 6), position), (parts,), jnp.float32, least / len(shards), largest / len(shards))
        return jnp.repeat(jnp.exp(heights), extent[position] // parts).reshape((-1,) + (1,) * (len(extent) - position - 1))

    level = one(*shards[0])
    for cut in shards[1:]:
        level = level * one(*cut)
    return level


def assign_block(rng, own, number, rows, amount, top, reach, slope):
    order = jax.random.permutation(rng, amount)
    crowded, ordinary = portions_of(amount, rows * top, reach, slope, True), portions_of(amount, rows * top, reach, slope, False)
    places = jnp.arange(amount)

    def named(lengths, rotation):
        used = int((lengths > 0).sum())
        fixed = max(1, used // 4)
        shifted = fixed + (places - fixed + rotation * (used - fixed)) % max(1, amount - fixed)
        return jnp.zeros((amount,), jnp.int32).at[order[jnp.where(places < fixed, places, shifted)]].set(jnp.asarray(lengths, jnp.int32))

    lengths = jnp.where(number % 4 == 0, named(crowded, number // 4), named(ordinary, number - number // 4 - 1))
    mixed = jax.random.permutation(jax.random.fold_in(own, 3), amount)
    donor, sink = mixed[0:amount // 2 * 2:2], mixed[1:amount // 2 * 2:2]
    margin = jnp.minimum(lengths[donor] - 1, reach - lengths[sink]) // 2
    margin = jnp.where((donor == order[0]) | (sink == order[0]) | (lengths[sink] == 0), 0, jnp.maximum(margin, 0))
    shifted = jax.random.randint(jax.random.fold_in(own, 4), (amount // 2,), 0, 1 << 20) % (margin + 1)
    lengths = lengths.at[donor].add(-shifted).at[sink].add(shifted)
    items = jnp.searchsorted(jnp.cumsum(lengths), jnp.arange(rows * top), side="right").astype(jnp.int32)
    listing = items.reshape(top, rows).T
    listing = listing[jax.random.permutation(jax.random.fold_in(own, 1), rows)]
    rotation = jax.random.randint(jax.random.fold_in(own, 2), (rows, 1), 0, top)
    return jnp.take_along_axis(listing, (jnp.arange(top)[None, :] + rotation) % top, axis=1)


def portions_of(number_of, total, reach, slope, full):
    weights = [(1 << 20) // math.isqrt(rank ** slope) + 1 for rank in range(1, number_of + 1)]
    largest = reach if full else min(reach, max(-(-total // number_of), total * weights[0] // sum(weights)))
    least = 1 if total - largest >= number_of - 1 else 0
    counts, surplus = [largest] + [least] * (number_of - 1), total - largest - least * (number_of - 1)
    while surplus > 0:
        movable = [i for i in range(1, number_of) if counts[i] < largest] or [i for i in range(1, number_of) if counts[i] < reach]
        pool, left = sum([weights[i] for i in movable]), surplus
        for i in movable:
            more = min(reach - counts[i], max(1, left * weights[i] // pool), surplus)
            counts[i] = counts[i] + more
            surplus = surplus - more
    return np.array(counts)


def noise(own_key, dims, deviation, most, shards=(), kind=jnp.bfloat16):
    result = deviation * jax.random.normal(own_key, dims, jnp.float32)
    if shards:
        result = result * steps_of(own_key, dims, shards, -0.22, 0.18)
    return jnp.clip(result, -most, most).astype(kind)


def setup_inputs(seed: int = 0) -> dict:
    key_list = jax.random.split(jax.random.key(seed), 22)
    tokens = noise(key_list[0], (TOKENS, MODEL_DIM), 1.0, 6.0, ((0, 16),))
    seq_lengths = draw_seq_lengths(jax.random.fold_in(key_list[21], 71), 0)
    expert_ids_keys = jax.random.split(jax.random.fold_in(key_list[2], 1), TOKENS // TOK_DEV)
    expert_ids_turns = jax.random.permutation(jax.random.fold_in(key_list[2], 3), TOKENS // TOK_DEV)
    expert_ids = jax.vmap(lambda own, number: assign_block(jax.random.fold_in(key_list[2], 2), own, number, TOK_DEV, EXPERTS, TOPK, CAP, 2))(expert_ids_keys, expert_ids_turns).reshape((TOKENS, TOPK))
    first_gain = jnp.clip(1.0 + 0.1 * jax.random.normal(key_list[3], (MODEL_DIM,), jnp.float32), 0.5, 1.5)
    query_weight = noise(key_list[4], (MODEL_DIM, QUERY_HEADS * HEAD_SIZE), MODEL_DIM ** -0.5, 0.109375, ((1, 8),))
    key_matrix = noise(key_list[5], (MODEL_DIM, KEY_VALUE_HEADS * HEAD_SIZE), MODEL_DIM ** -0.5, 0.109375, ((1, 8),))
    value_matrix = noise(key_list[6], (MODEL_DIM, KEY_VALUE_HEADS * HEAD_SIZE), MODEL_DIM ** -0.5, 0.109375, ((1, 8),))
    query_bias = noise(key_list[7], (QUERY_HEADS * HEAD_SIZE,), 0.3, 2.0, ((0, 8),), jnp.float32)
    key_offset_bias = noise(key_list[8], (KEY_VALUE_HEADS * HEAD_SIZE,), 0.3, 2.0, ((0, 8),), jnp.float32)
    value_offset_bias = noise(key_list[9], (KEY_VALUE_HEADS * HEAD_SIZE,), 0.3, 2.0, ((0, 8),), jnp.float32)
    head_sink_logits = jnp.clip(1.0 + 3.0 * jax.random.uniform(key_list[10], (QUERY_HEADS,), jnp.float32) ** steps_of(key_list[10], (QUERY_HEADS,), ((0, 8),), -0.2, 0.2), 1.0, 4.0)
    output_weight = noise(key_list[11], (QUERY_HEADS * HEAD_SIZE, MODEL_DIM), (QUERY_HEADS * HEAD_SIZE // 64) ** -0.5, 0.75, ((0, 8),))
    output_bias = noise(key_list[12], (MODEL_DIM,), 0.3, 2.0, (), jnp.float32)
    second_gain = jnp.clip(1.0 + 0.1 * jax.random.normal(key_list[13], (MODEL_DIM,), jnp.float32), 0.5, 1.5)
    router_weight = noise(key_list[14], (MODEL_DIM, EXPERTS), (4 * MODEL_DIM) ** -0.5, 0.0546875)
    router_bias = noise(key_list[15], (EXPERTS,), 0.2, 1.0, (), jnp.float32)
    expert_gateup = noise(key_list[16], (EXPERTS, 2, MODEL_DIM, FF), MODEL_DIM ** -0.5, 0.109375, ((0, 16), (3, 8)))
    gateup_bias = noise(key_list[17], (EXPERTS, 2, FF), 0.15, 1.0, ((0, 16), (2, 8)), jnp.float32)
    expert_down = noise(key_list[18], (EXPERTS, FF, MODEL_DIM), FF ** -0.5, 0.109375, ((0, 16), (1, 8)))
    down_bias = noise(key_list[19], (EXPERTS, MODEL_DIM), 0.15, 1.0, ((0, 16),), jnp.float32)
    cotangent = noise(key_list[20], (TOKENS, MODEL_DIM), 1.0, 6.0, ((0, 16),))
    return {"tokens": tokens, "seq_lengths": seq_lengths, "expert_ids": expert_ids, "first_gain": first_gain, "query_weight": query_weight, "key_matrix": key_matrix, "value_matrix": value_matrix, "query_bias": query_bias, "key_offset_bias": key_offset_bias, "value_offset_bias": value_offset_bias, "head_sink_logits": head_sink_logits, "output_weight": output_weight, "output_bias": output_bias, "second_gain": second_gain, "router_weight": router_weight, "router_bias": router_bias, "expert_gateup": expert_gateup, "gateup_bias": gateup_bias, "expert_down": expert_down, "down_bias": down_bias, "cotangent": cotangent}


EPS = 1e-05
THETA = 150000.0
LIMIT = 7.0
ALPHA = 1.702
NEGATIVE = -1e+30

@jax.custom_vjp
def lowered_copy(v):
    return lax.optimization_barrier(v.astype(jnp.bfloat16)).astype(jnp.float32)

@jax.custom_vjp
def lowered_backward(v):
    return v

def low_keep(v):
    return (lowered_copy(v), None)

def low_pass(kept, grad):
    return (grad,)

def back_keep(v):
    return (v, None)

def back_low(kept, grad):
    return (lowered_copy(grad),)
lowered_copy.defvjp(low_keep, low_pass)
lowered_backward.defvjp(back_keep, back_low)

def matrix_multiply(left, right):
    return jnp.dot(left, right, precision=lax.Precision.HIGHEST)

def rms_norm(value_rows, gain_vector):
    return value_rows * lax.rsqrt(lax.optimization_barrier(jnp.mean(value_rows * value_rows, axis=-1, keepdims=True)) + EPS) * gain_vector

def angles_of(positions, head_width):
    exponent = jnp.arange(head_width // 2, dtype=jnp.float32) * (2.0 / head_width)
    frequency = jnp.power(THETA, -exponent)
    return positions.astype(jnp.float32)[:, None] * frequency[None, :]

def apply_rotary(value_rows, rotary_angles):
    half_width = value_rows.shape[-1] // 2
    cosine = jnp.cos(rotary_angles)[:, None, :]
    sine_part = jnp.sin(rotary_angles)[:, None, :]
    first_half = value_rows[..., :half_width]
    second_half = value_rows[..., half_width:]
    return jnp.concatenate([first_half * cosine - second_half * sine_part, second_half * cosine + first_half * sine_part], axis=-1)

def layout(lengths_row, count_of_rows):
    row_index = jnp.arange(count_of_rows, dtype=jnp.int32)
    first_end = lengths_row[0]
    second_end = lengths_row[0] + lengths_row[1]
    document = (row_index >= first_end).astype(jnp.int32) + (row_index >= second_end).astype(jnp.int32)
    doc_start = jnp.where(document == 0, 0, jnp.where(document == 1, first_end, second_end)).astype(jnp.int32)
    return (row_index - doc_start, document)

def log_totals(scores, sink_logit_column):
    highest = jnp.maximum(lax.optimization_barrier(jnp.max(scores, axis=-1)), sink_logit_column)
    total = jnp.exp(sink_logit_column - highest) + lax.optimization_barrier(jnp.sum(jnp.exp(scores - highest[..., None]), axis=-1))
    return highest + jnp.log(total)

def gate_weights(logits, chosen):
    picked = lax.optimization_barrier(jnp.sum(chosen * logits[:, None, :], axis=-1))
    highest = lax.optimization_barrier(jnp.max(picked, axis=-1, keepdims=True))
    raised = jnp.exp(picked - highest)
    return raised / lax.optimization_barrier(jnp.sum(raised, axis=-1, keepdims=True))

def activate(gate_pre, up_pre):
    capped_gate = LIMIT - jax.nn.softplus(LIMIT - gate_pre)
    capped_up = LIMIT * jnp.tanh(up_pre / LIMIT)
    return (capped_up + 1.0) * capped_gate * jax.nn.sigmoid(ALPHA * capped_gate)

def slot_ranks(expert_ids):
    count_of_rows, top_count = expert_ids.shape
    chosen = (expert_ids[:, :, None] == jnp.arange(EXPERTS, dtype=jnp.int32)[None, None, :]).astype(jnp.int32)
    blocks = chosen.reshape(count_of_rows // TOK_DEV, TOK_DEV * top_count, EXPERTS)
    before = jnp.cumsum(blocks, axis=1, dtype=jnp.int32) - blocks
    return lax.optimization_barrier(jnp.sum(before * blocks, axis=-1, dtype=jnp.int32)).reshape(count_of_rows, top_count)

def attend(normalized_input, positions, document, weights):
    query_weight, key_matrix, value_matrix, query_bias, key_offset_bias, value_offset_bias, head_sink_logits = weights
    count_of_rows = normalized_input.shape[0]
    heads_per_group = QUERY_HEADS // KEY_VALUE_HEADS
    query_unrotated = lowered_backward(matrix_multiply(normalized_input, query_weight) + query_bias).reshape(count_of_rows, QUERY_HEADS, HEAD_SIZE)
    key_unrotated = lowered_backward(matrix_multiply(normalized_input, key_matrix) + key_offset_bias).reshape(count_of_rows, KEY_VALUE_HEADS, HEAD_SIZE)
    value_rows = lowered_backward(lowered_copy(matrix_multiply(normalized_input, value_matrix) + value_offset_bias)).reshape(count_of_rows, KEY_VALUE_HEADS, HEAD_SIZE)
    rotary_angles = angles_of(positions, HEAD_SIZE)
    query_rows = lowered_copy(apply_rotary(query_unrotated, rotary_angles)).reshape(count_of_rows, KEY_VALUE_HEADS, heads_per_group, HEAD_SIZE)
    key_rot = lowered_copy(apply_rotary(key_unrotated, rotary_angles))
    scores = lowered_backward(HEAD_SIZE ** (-0.5) * jnp.einsum('qhgd,khd->hgqk', query_rows, key_rot, precision=lax.Precision.HIGHEST))
    row_index = jnp.arange(count_of_rows)
    allowed = (document[:, None] == document[None, :]) & (row_index[None, :] <= row_index[:, None])
    scores = jnp.where(allowed[None, None], scores, NEGATIVE)
    sink_logit_column = head_sink_logits.reshape(KEY_VALUE_HEADS, heads_per_group)[:, :, None]
    log_total = log_totals(scores, sink_logit_column)
    probabilities = lowered_copy(jnp.exp(scores - log_total[..., None]))
    head_values = jnp.einsum('hgqk,khd->qhgd', probabilities, value_rows, precision=lax.Precision.HIGHEST)
    return lowered_backward(lowered_copy(head_values.reshape(count_of_rows, QUERY_HEADS * HEAD_SIZE)))

def expert_block(item):
    expert_rows, gateup_pair, bias_pair, down_matrix, bias_row = item
    gate_pre = lowered_backward(matrix_multiply(expert_rows, gateup_pair[0]) + bias_pair[0])
    up_pre = lowered_backward(matrix_multiply(expert_rows, gateup_pair[1]) + bias_pair[1])
    hidden = lowered_copy(activate(gate_pre, up_pre))
    return lowered_backward(lowered_copy(matrix_multiply(hidden, down_matrix) + bias_row))

def reference(tokens, seq_lengths, expert_ids, first_gain, query_weight, key_matrix, value_matrix, query_bias, key_offset_bias, value_offset_bias, head_sink_logits, output_weight, output_bias, second_gain, router_weight, router_bias, expert_gateup, gateup_bias, expert_down, down_bias, cotangent):
    device_count = TOKENS // TOK_DEV
    slot_rank = slot_ranks(expert_ids)
    device = (jnp.arange(TOKENS, dtype=jnp.int32) // TOK_DEV)[:, None]
    target = ((expert_ids * device_count + device) * CAP + slot_rank).reshape(-1).astype(jnp.int32)
    chosen = (expert_ids[:, :, None] == jnp.arange(EXPERTS, dtype=jnp.int32)[None, None, :]).astype(jnp.float32)
    positions, documents = jax.vmap(partial(layout, count_of_rows=TOK_DEV))(seq_lengths)

    def forward(inputs, gain_one, weight_query, weight_key, weight_value, bias_query, bias_key, bias_value, sink_values, weight_output, bias_output, gain_two, weight_router, bias_router, weight_gateup, bias_gateup, weight_down, bias_down):
        normalized_input = lowered_copy(rms_norm(inputs, gain_one))
        attention_weights = (weight_query, weight_key, weight_value, bias_query, bias_key, bias_value, sink_values)

        def group_attention(item):
            return attend(item[0], item[1], item[2], attention_weights)
        head_values = lax.map(jax.checkpoint(group_attention), (normalized_input.reshape(N_EP, TOK_DEV, MODEL_DIM), positions, documents))
        attended = lowered_backward(matrix_multiply(head_values.reshape(TOKENS, QUERY_HEADS * HEAD_SIZE), weight_output) + bias_output)
        mixed = inputs + attended
        second = lowered_copy(rms_norm(mixed, gain_two))
        logits = matrix_multiply(second, weight_router) + bias_router
        gate_share = gate_weights(logits, chosen)
        routed = lowered_backward(jnp.broadcast_to(second[:, None, :], (TOKENS, TOPK, MODEL_DIM))).reshape(TOKENS * TOPK, MODEL_DIM)
        buffer = jnp.zeros((EXPERTS * device_count * CAP, MODEL_DIM), jnp.float32).at[target].add(routed)
        results = lax.map(jax.checkpoint(expert_block), (buffer.reshape(EXPERTS, device_count * CAP, MODEL_DIM), weight_gateup, bias_gateup, weight_down, bias_down))
        picked = results.reshape(EXPERTS * device_count * CAP, MODEL_DIM)[target].reshape(TOKENS, TOPK, MODEL_DIM)
        return mixed + lax.optimization_barrier(jnp.sum(gate_share[:, :, None] * picked, axis=1))
    output, backward = jax.vjp(forward, tokens.astype(jnp.float32), first_gain, query_weight.astype(jnp.float32), key_matrix.astype(jnp.float32), value_matrix.astype(jnp.float32), query_bias, key_offset_bias, value_offset_bias, head_sink_logits, output_weight.astype(jnp.float32), output_bias, second_gain, router_weight.astype(jnp.float32), router_bias, expert_gateup.astype(jnp.float32), gateup_bias, expert_down.astype(jnp.float32), down_bias)
    grads = backward(cotangent.astype(jnp.float32))
    return (output.astype(jnp.bfloat16), grads[0], grads[1], grads[2], grads[3], grads[4], grads[5], grads[6], grads[7], grads[8], grads[9], grads[10], grads[11], grads[12], grads[13], grads[14], grads[15], grads[16], grads[17])
```

```python
from functools import partial

import jax
import jax.numpy as jnp
from jax import lax
from jax.experimental import pallas as pl
from jax.experimental.pallas import tpu as pltpu
from jax.sharding import PartitionSpec as P

HEAD_SIZE = 64
EPS = 1e-05
THETA = 150000.0
LIMIT = 7.0
ALPHA = 1.702
NEGATIVE = -1e30

D = 2880
FF_LOCAL = 360
SHARE = 384
BLOCKS = 8
WIDE = SHARE * BLOCKS
ROWS = 128
EXPERTS = 16
CAP = 48
SLOTS = EXPERTS * CAP
HALF = SLOTS // 2
QUARTER = SLOTS // 4
MESH = pl.DeviceIdType.MESH
F32 = jnp.float32
BF16 = jnp.bfloat16
HIGHEST = lax.Precision.HIGHEST


def product(left, right):
    return jnp.dot(left, right, preferred_element_type=F32)


def contract_rows(left, right):
    return lax.dot_general(left, right, (((0,), (0,)), ((), ())), preferred_element_type=F32)


def against_rows(left, right):
    return lax.dot_general(left, right, (((1,), (1,)), ((), ())), preferred_element_type=F32)


def exact_against_rows(left, right):
    return lax.dot_general(
        left, right, (((1,), (1,)), ((), ())), preferred_element_type=F32, precision=HIGHEST
    )


def rms_norm(value_rows, gain_vector):
    return (
        value_rows
        * lax.rsqrt(jnp.mean(value_rows * value_rows, axis=-1, keepdims=True) + EPS)
        * gain_vector
    )


def angles_of(positions, head_width):
    exponent = jnp.arange(head_width // 2, dtype=F32) * (2.0 / head_width)
    frequency = jnp.power(THETA, -exponent)
    return positions.astype(F32)[:, None] * frequency[None, :]


def apply_rotary(value_rows, rotary_angles):
    half_width = value_rows.shape[-1] // 2
    cosine = jnp.cos(rotary_angles)[:, None, :]
    sine_part = jnp.sin(rotary_angles)[:, None, :]
    first_half = value_rows[..., :half_width]
    second_half = value_rows[..., half_width:]
    return jnp.concatenate(
        [
            first_half * cosine - second_half * sine_part,
            second_half * cosine + first_half * sine_part,
        ],
        axis=-1,
    )


def layout(lengths_row, count_of_rows):
    row_index = jnp.arange(count_of_rows, dtype=jnp.int32)
    first_end = lengths_row[0]
    second_end = lengths_row[0] + lengths_row[1]
    document = (row_index >= first_end).astype(jnp.int32) + (row_index >= second_end).astype(
        jnp.int32
    )
    doc_start = jnp.where(document == 0, 0, jnp.where(document == 1, first_end, second_end))
    return (row_index - doc_start, document)


def log_totals(scores, sink_logit_column):
    highest = jnp.maximum(jnp.max(scores, axis=-1), sink_logit_column)
    total = jnp.exp(sink_logit_column - highest) + jnp.sum(
        jnp.exp(scores - highest[..., None]), axis=-1
    )
    return highest + jnp.log(total)


class Place:
    def __init__(self):
        self.ep = lax.axis_index("ep")
        self.tp = lax.axis_index("tp")
        self.z, self.x = self.ep // 4, self.ep % 4
        self.y, self.core = self.tp // 2, self.tp % 2

    def sibling(self):
        return (self.ep, self.y * 2 + (1 - self.core))

    def along_y(self, step):
        return (self.ep, lax.rem(self.y + step, 4) * 2 + self.core)

    def along_tp(self, step):
        return (self.ep, lax.rem(self.tp + step, 8))

    def along_ep(self, k):
        z = lax.rem(self.z + k // 4, 4)
        x = lax.rem(self.x + k % 4, 4)
        return (z * 4 + x, self.tp)

    def back_ep(self, k):
        z = lax.rem(self.z + 4 - k // 4, 4)
        x = lax.rem(self.x + 4 - k % 4, 4)
        return (z * 4 + x, self.tp)


class Sender:
    def __init__(self, send_sems, recv_sems):
        self.send_sems, self.recv_sems = send_sems, recv_sems
        self.used = 0
        self.open = []

    def start(self, source, target, device):
        n = self.used
        self.used += 1
        copy = pltpu.make_async_remote_copy(
            src_ref=source,
            dst_ref=target,
            send_sem=self.send_sems.at[n],
            recv_sem=self.recv_sems.at[n],
            device_id=device,
            device_id_type=MESH,
        )
        copy.start()
        self.open.append(copy)
        return n

    def arrived(self, n, target):
        pltpu.make_async_remote_copy(
            src_ref=target,
            dst_ref=target,
            send_sem=self.send_sems.at[n],
            recv_sem=self.recv_sems.at[n],
            device_id=Place().sibling(),
            device_id_type=MESH,
        ).wait_recv()

    def finish(self):
        for copy in self.open:
            copy.wait_send()
        self.open = []


def column_of(row):
    return jnp.transpose(jnp.broadcast_to(row, (128, 128)))


def wide(columns, width=SHARE):
    return jnp.concatenate([columns] * (width // 128), axis=1)


def share_blocks(part, emit):
    for q in range(BLOCKS):
        lo = q * SHARE
        width = min(SHARE, D - lo)
        block = part(lo, width)
        if width < SHARE:
            block = jnp.concatenate(
                [block, jnp.zeros((block.shape[0], SHARE - width), block.dtype)], axis=1
            )
        emit(q, block)


def reduce_columns(me, send, part, from_sibling, sums, from_y):
    order = (2, 1, 3, 0)
    ticket = []
    for i, step in enumerate(order):
        y = lax.rem(me.y + step, 4)
        ticket.append(
            send.start(part.at[y * 2 + 1 - me.core], from_sibling.at[i], me.sibling())
        )
    landed = []
    for i, step in enumerate(order):
        y = lax.rem(me.y + step, 4)
        send.arrived(ticket[i], from_sibling.at[i])
        total = part[y * 2 + me.core].astype(F32) + from_sibling[i].astype(F32)
        if step:
            sums[i] = total.astype(BF16)
            landed.append(send.start(sums.at[i], from_y.at[i], me.along_y(step)))
    for i, n in enumerate(landed):
        send.arrived(n, from_y.at[i])
        total = total + from_y[i].astype(F32)
    return total


def exchange(me, send, own, others):
    tickets = [send.start(own, others.at[i - 1], me.along_tp(i)) for i in range(1, 8)]
    total = own[...]
    for i, n in enumerate(tickets):
        send.arrived(n, others.at[i])
        total = total + others[i]
    return total


def gather_columns(me, send, blocks):
    own = blocks.at[me.tp]
    to_y = [send.start(own, own, me.along_y(step)) for step in (2, 1, 3)]
    to_sibling = [send.start(own, own, me.sibling())]
    for n, step in zip(to_y, (2, 1, 3)):
        block = blocks.at[lax.rem(me.y + 4 - step, 4) * 2 + me.core]
        send.arrived(n, block)
        to_sibling.append(send.start(block, block, me.sibling()))
    for n, step in zip(to_sibling, (0, 2, 1, 3)):
        send.arrived(n, blocks.at[lax.rem(me.y + 4 - step, 4) * 2 + 1 - me.core])


def greet_tp(me):
    barrier = pltpu.get_barrier_semaphore()
    for i in range(1, 8):
        pl.semaphore_signal(barrier, inc=1, device_id=me.along_tp(i), device_id_type=MESH)
    return lambda: pl.semaphore_wait(barrier, 7)


def greet_all(me):
    barrier = pltpu.get_barrier_semaphore()
    for i in range(1, 8):
        pl.semaphore_signal(barrier, inc=1, device_id=me.along_tp(i), device_id_type=MESH)
    for k in range(1, 16):
        pl.semaphore_signal(barrier, inc=1, device_id=me.along_ep(k), device_id_type=MESH)
    return lambda: pl.semaphore_wait(barrier, 22)


def attend_kernel(
    heads, weight, inputs, vectors, router, router_bias, chosen,
    second, mixed_out, stat_out,
    part, from_sibling, sums, from_y, stat, stats, send_sems, recv_sems,
):
    me = Place()
    send = Sender(send_sems, recv_sems)
    all_here = greet_tp(me)
    rows = heads[...]

    def emit(q, block):
        part[q] = block.astype(BF16)

    share_blocks(lambda lo, width: product(rows, weight[:, lo : lo + width]), emit)
    all_here()
    attended = reduce_columns(me, send, part, from_sibling, sums, from_y)
    mixed = inputs[...] + attended + vectors[0:1, :]
    mixed_out[...] = mixed
    raised = mixed * vectors[1:2, :]
    stat[0:16, :] = against_rows(router[...], raised.astype(BF16))
    stat[16:24, :] = exact_against_rows(jnp.ones((8, SHARE), F32), mixed * mixed)
    total = exchange(me, send, stat, stats)
    scale = lax.rsqrt(total[16:17, :] * (1.0 / D) + EPS)
    second[...] = (raised * wide(column_of(scale))).astype(BF16)
    plain = total[0:16, :] * scale
    logits = plain + router_bias[...]
    taken = chosen[...] > 0.5
    highest = jnp.max(jnp.where(taken, logits, NEGATIVE), axis=0, keepdims=True)
    lifted = jnp.where(taken, jnp.exp(jnp.where(taken, logits, highest) - highest), 0.0)
    stat_out[0:16, :] = lifted / jnp.sum(lifted, axis=0, keepdims=True)
    stat_out[16:32, :] = plain
    stat_out[32:40, :] = jnp.broadcast_to(scale, (8, 128))
    send.finish()


def attend_end(heads, weight, inputs, vectors, router, router_bias, chosen):
    return pl.pallas_call(
        attend_kernel,
        out_shape=(
            jax.ShapeDtypeStruct((ROWS, SHARE), BF16),
            jax.ShapeDtypeStruct((ROWS, SHARE), F32),
            jax.ShapeDtypeStruct((40, 128), F32),
        ),
        in_specs=[pl.BlockSpec(memory_space=pltpu.VMEM)] * 7,
        out_specs=(pl.BlockSpec(memory_space=pltpu.VMEM),) * 3,
        scratch_shapes=[
            pltpu.VMEM((8, ROWS, SHARE), BF16),
            pltpu.VMEM((4, ROWS, SHARE), BF16),
            pltpu.VMEM((3, ROWS, SHARE), BF16),
            pltpu.VMEM((3, ROWS, SHARE), BF16),
            pltpu.VMEM((24, 128), F32),
            pltpu.VMEM((7, 24, 128), F32),
            pltpu.SemaphoreType.DMA((14,)),
            pltpu.SemaphoreType.DMA((14,)),
        ],
        compiler_params=pltpu.CompilerParams(
            collective_id=1, has_side_effects=True, vmem_limit_bytes=40 * 2**20
        ),
        name="attend_end",
    )(heads, weight, inputs, vectors, router, router_bias, chosen)


def activation_parts(gate_pre, up_pre):
    lowered = LIMIT - gate_pre
    cap = jnp.maximum(lowered, 0.0) + jnp.log(1.0 + jnp.exp(-jnp.abs(lowered)))
    capped_gate = LIMIT - cap
    tanh = jnp.tanh(up_pre * (1.0 / LIMIT))
    capped_up = LIMIT * tanh
    sigmoid = 1.0 / (1.0 + jnp.exp(-ALPHA * capped_gate))
    return lowered, capped_gate, tanh, capped_up, sigmoid


def expert_kernel(
    second, mixed, stat, selector, selector_t, cotangent, cot_own, gateup, down, gateup_bias, down_bias,
    router, vectors,
    rows_out, cots_out, scaled_out, grad_gate_out, grad_up_out, gate_cols_out,
    grad_att_out, layer_out, small_out, bias_out,
    R, C, weights, staged, staged_c, gates_send, gates, gate_pre, up_pre, hidden,
    to_sibling, kept, from_sibling, sums, results, from_y, home, wire, from_y_small, stat_own, stats,
    both, send_sems, recv_sems, local_sems,
):
    me = Place()
    send = Sender(send_sems, recv_sems)
    all_here = greet_all(me)
    load = pltpu.make_async_copy(gateup, weights.at[:, 0:D, :], local_sems.at[0])
    load.start()
    weights[:, D:, :] = jnp.zeros((2, WIDE - D, FF_LOCAL), BF16)
    staged[...] = product(selector[...], second[...]).astype(BF16)
    staged_c[...] = product(selector[...], cot_own[...]).astype(BF16)
    for k in range(EXPERTS):
        row = jnp.broadcast_to(stat[k : k + 1, :], (8, 128))
        picked = exact_against_rows(row, selector[k * CAP : (k + 1) * CAP, :].astype(F32))
        gates_send[k] = jnp.concatenate([picked, jnp.zeros((8, 128 - CAP), F32)], axis=1)
    all_here()

    def scatter(source, target):
        tickets = [None]
        for k in range(1, EXPERTS):
            lines = pl.ds(k * CAP, CAP)
            tickets.append(
                send.start(source.at[lines], target.at[me.tp, lines], me.along_ep(k))
            )
        target[me.tp, 0:CAP, :] = source[0:CAP, :]
        return tickets

    rows_in = scatter(staged, R)
    gates_in = [None]
    for k in range(1, EXPERTS):
        gates_in.append(send.start(gates_send.at[k], gates.at[k], me.along_ep(k)))
    gates[0] = gates_send[0]
    cots_in = scatter(staged_c, C)

    steps = (1, 3, 2)

    def spread(buffer, tickets, j):
        lines = pl.ds(j * QUARTER, QUARTER)
        for k in range(4 * j, 4 * j + 4):
            if k:
                send.arrived(tickets[k], buffer.at[me.tp, pl.ds(k * CAP, CAP)])
        own = buffer.at[me.tp, lines]
        return [send.start(own, own, me.along_y(s)) for s in steps] + [
            send.start(own, own, me.sibling())
        ]

    def pass_on(buffer, tickets, j):
        lines = pl.ds(j * QUARTER, QUARTER)
        sent = [tickets[3]]
        for n, s in zip(tickets, steps):
            block = buffer.at[lax.rem(me.y + 4 - s, 4) * 2 + me.core, lines]
            send.arrived(n, block)
            sent.append(send.start(block, block, me.sibling()))
        return sent

    def complete(buffer, tickets, j):
        lines = pl.ds(j * QUARTER, QUARTER)
        for n, s in zip(tickets, (0,) + steps):
            send.arrived(n, buffer.at[lax.rem(me.y + 4 - s, 4) * 2 + 1 - me.core, lines])

    a, b = [None] * 4, [None] * 4
    a[0] = spread(R, rows_in, 0)
    a[1] = spread(R, rows_in, 1)
    a[0] = pass_on(R, a[0], 0)
    a[2] = spread(R, rows_in, 2)
    a[1] = pass_on(R, a[1], 1)
    a[3] = spread(R, rows_in, 3)
    a[2] = pass_on(R, a[2], 2)
    for j in range(4):
        b[j] = spread(C, cots_in, j)
    complete(R, a[0], 0)
    complete(R, a[1], 1)
    load.wait()

    def lines_of(h):
        return pl.ds(h * HALF, HALF)

    def forward(h):
        lines = lines_of(h)
        gate_pre[lines, :] = jnp.broadcast_to(gateup_bias[0:1, :], (HALF, FF_LOCAL))
        up_pre[lines, :] = jnp.broadcast_to(gateup_bias[1:2, :], (HALF, FF_LOCAL))

        @pl.loop(0, 4)
        def _(y):
            block = jnp.concatenate([R[2 * y, lines, :], R[2 * y + 1, lines, :]], axis=1)
            span = pl.ds(pl.multiple_of(y * 2 * SHARE, 2 * SHARE), 2 * SHARE)
            gate_pre[lines, :] += product(block, weights[0, span, :])
            up_pre[lines, :] += product(block, weights[1, span, :])

        _, capped_gate, _, capped_up, sigmoid = activation_parts(
            gate_pre[lines, :], up_pre[lines, :]
        )
        hidden[lines, :] = ((capped_up + 1.0) * capped_gate * sigmoid).astype(BF16)

        def out_block(q):
            span = pl.ds(pl.multiple_of(q * SHARE, SHARE), SHARE)
            return product(hidden[lines, :], down[:, span]) + down_bias[pl.ds(q, 1), :]

        sent = []
        for y in range(4):
            to_sibling[0, y, lines, :] = out_block(2 * y + 1 - me.core).astype(BF16)
            sent.append(
                send.start(
                    to_sibling.at[0, y, lines], from_sibling.at[0, y, lines], me.sibling()
                )
            )
        for y in range(4):
            kept[0, y, lines, :] = out_block(2 * y + me.core).astype(BF16)
        return sent

    def results_home(h, sent):
        lines = lines_of(h)
        for y in range(4):
            send.arrived(sent[y], from_sibling.at[0, y, lines])
            sums[0, y, lines, :] = (
                kept[0, y, lines, :].astype(F32) + from_sibling[0, y, lines, :].astype(F32)
            ).astype(BF16)
        tickets = []
        for k in range(8 * h, 8 * h + 8):
            span = pl.ds(k * CAP, CAP)
            if k:
                tickets.append(
                    send.start(sums.at[0, :, span], results.at[:, span], me.back_ep(k))
                )
            else:
                tickets.append(None)
                results[:, 0:CAP, :] = sums[0, :, 0:CAP, :]
        return tickets

    sent_0 = forward(0)
    a[3] = pass_on(R, a[3], 3)
    b[0] = pass_on(C, b[0], 0)
    complete(R, a[2], 2)
    complete(R, a[3], 3)
    rows_copy = pltpu.make_async_copy(R, rows_out, local_sems.at[1])
    rows_copy.start()
    sent_1 = forward(1)
    back = results_home(0, sent_0)
    for j in (1, 2, 3):
        b[j] = pass_on(C, b[j], j)
    back = back + results_home(1, sent_1)
    for k in range(1, EXPERTS):
        send.arrived(gates_in[k], gates.at[k])
    gate_rows = jnp.concatenate(
        [gates[:, 0, :], jnp.zeros((128 - EXPERTS, 128), F32)], axis=0
    )
    gate_cols = jnp.transpose(gate_rows)

    def gate_column(h):
        return jnp.concatenate(
            [gate_cols[0:CAP, k : k + 1] for k in range(8 * h, 8 * h + 8)], axis=0
        )

    def backward(h):
        lines = lines_of(h)
        gate = gate_column(h)
        high = gate.astype(BF16)
        low = (gate - high.astype(F32)).astype(BF16)
        place = lax.broadcasted_iota(jnp.int32, (HALF, 128), 1)
        gate_cols_out[lines, :] = jnp.where(
            place == 0,
            high.astype(F32),
            jnp.where(place == 1, low.astype(F32), 0.0),
        ).astype(BF16)

        def step(y, total):
            block = jnp.concatenate([C[2 * y, lines, :], C[2 * y + 1, lines, :]], axis=1)
            span = pl.ds(pl.multiple_of(y * 2 * SHARE, 2 * SHARE), 2 * SHARE)
            return total + against_rows(block, down[:, span])

        grad_hidden = gate * lax.fori_loop(0, 4, step, jnp.zeros((HALF, FF_LOCAL), F32))
        lowered, capped_gate, tanh, capped_up, sigmoid = activation_parts(
            gate_pre[lines, :], up_pre[lines, :]
        )
        scaled_out[lines, :] = (gate * hidden[lines, :].astype(F32)).astype(BF16)
        slope = (capped_up + 1.0) * (
            sigmoid + ALPHA * capped_gate * sigmoid * (1.0 - sigmoid)
        )
        grad_gate_out[lines, :] = (
            grad_hidden * slope * (1.0 / (1.0 + jnp.exp(-lowered)))
        ).astype(BF16)
        grad_up_out[lines, :] = (
            grad_hidden * capped_gate * sigmoid * (1.0 - tanh * tanh)
        ).astype(BF16)

        def back_block(q):
            span = pl.ds(pl.multiple_of(q * SHARE, SHARE), SHARE)
            return against_rows(grad_gate_out[lines, :], weights[0, span, :]) + against_rows(
                grad_up_out[lines, :], weights[1, span, :]
            )

        sent = []
        for s in (2, 1, 3, 0):
            y = lax.rem(me.y + s, 4)
            to_sibling[1, s, lines, :] = back_block(2 * y + 1 - me.core).astype(BF16)
            sent.append(
                send.start(
                    to_sibling.at[1, s, lines], from_sibling.at[1, s, lines], me.sibling()
                )
            )
        landed = []
        for s, n in zip((2, 1, 3, 0), sent):
            y = lax.rem(me.y + s, 4)
            block = back_block(2 * y + me.core)
            send.arrived(n, from_sibling.at[1, s, lines])
            total = block + from_sibling[1, s, lines, :].astype(F32)
            if s:
                sums[1, s, lines, :] = total.astype(BF16)
                landed.append(
                    send.start(
                        sums.at[1, s, lines], from_y.at[s - 1, lines], me.along_y(s)
                    )
                )
            else:
                kept[1, 0, lines, :] = total.astype(BF16)
        return landed

    def grads_home(h, landed):
        lines = lines_of(h)
        total = kept[1, 0, lines, :].astype(F32)
        for s, n in zip((2, 1, 3), landed):
            send.arrived(n, from_y.at[s - 1, lines])
            total = total + from_y[s - 1, lines, :].astype(F32)
        sums[1, 0, lines, :] = total.astype(BF16)
        tickets = []
        for k in range(8 * h, 8 * h + 8):
            span = pl.ds(k * CAP, CAP)
            if k:
                tickets.append(
                    send.start(sums.at[1, 0, span], home.at[span], me.back_ep(k))
                )
            else:
                tickets.append(None)
                home[0:CAP, :] = sums[1, 0, 0:CAP, :]
        return tickets

    complete(C, b[0], 0)
    complete(C, b[1], 1)
    landed_0 = backward(0)
    complete(C, b[2], 2)
    complete(C, b[3], 3)
    cots_copy = pltpu.make_async_copy(C, cots_out, local_sems.at[2])
    cots_copy.start()
    landed_1 = backward(1)
    home_in = grads_home(0, landed_0)
    home_in = home_in + grads_home(1, landed_1)

    for k in range(1, EXPERTS):
        send.arrived(back[k], results.at[:, pl.ds(k * CAP, CAP)])
    spread_gates = jnp.concatenate(
        [jnp.broadcast_to(stat[k : k + 1, :], (CAP, 128)) for k in range(EXPERTS)], axis=0
    )
    weighted = selector[...].astype(F32) * spread_gates
    high = weighted.astype(BF16)
    low = (weighted - high.astype(F32)).astype(BF16)
    pairs = jnp.zeros((SLOTS, ROWS), F32)
    to_y = []
    for s in (2, 1, 3, 0):
        y = lax.rem(me.y + s, 4)
        block = results[y]
        pairs = pairs + against_rows(block, cotangent[2 * y + me.core])
        mine = contract_rows(high, block) + contract_rows(low, block)
        if s:
            wire[s - 1] = mine.astype(BF16)
            to_y.append(send.start(wire.at[s - 1], from_y_small.at[s - 1], me.along_y(s)))
    pairs = pairs * selector[...].astype(F32)
    for k in range(EXPERTS):
        stat_own[k : k + 1, :] = jnp.sum(pairs[k * CAP : (k + 1) * CAP], axis=0, keepdims=True)
    for k in range(1, EXPERTS):
        send.arrived(home_in[k], home.at[pl.ds(k * CAP, CAP)])
    returned = product(selector_t[...], home[...])
    gain = vectors[1:2, :]
    scale = wide(column_of(stat[32:33, :]))
    normal = mixed[...] * scale
    stat_own[16:24, :] = exact_against_rows(
        jnp.ones((8, SHARE), F32), returned * gain * normal
    )
    total = exchange(me, send, stat_own, stats)
    gate_share = stat[0:16, :]
    grad_gates = total[0:16, :]
    grad_logits = gate_share * (
        grad_gates - jnp.sum(gate_share * grad_gates, axis=0, keepdims=True)
    )
    inner = total[16:17, :] + jnp.sum(grad_logits * stat[16:32, :], axis=0, keepdims=True)
    grad_second = returned + lax.dot_general(
        grad_logits,
        router[...].astype(F32),
        (((0,), (0,)), ((), ())),
        preferred_element_type=F32,
        precision=HIGHEST,
    )
    final = cot_own[...].astype(F32)
    grad_mixed = final + scale * (
        gain * grad_second - normal * wide(column_of(inner * (1.0 / D)))
    )
    grad_att = grad_mixed.astype(BF16)
    for s, n in zip((2, 1, 3), to_y):
        send.arrived(n, from_y_small.at[s - 1])
        mine = mine + from_y_small[s - 1].astype(F32)
    both[me.tp, 0:ROWS, :] = grad_att
    both[me.tp, ROWS:, :] = (mixed[...] + mine).astype(BF16)
    small_out[0:16, :] = lax.dot_general(
        grad_logits,
        second[...].astype(F32),
        (((1,), (0,)), ((), ())),
        preferred_element_type=F32,
        precision=HIGHEST,
    )
    small_out[16:17, :] = jnp.sum(grad_second * normal, axis=0, keepdims=True)
    small_out[17:18, :] = jnp.sum(grad_att.astype(F32), axis=0, keepdims=True)
    small_out[18:24, :] = jnp.zeros((6, SHARE), F32)
    bias_out[...] = grad_logits
    gather_columns(me, send, both)
    grad_att_out[...] = both[:, 0:ROWS, :]
    layer_out[...] = both[:, ROWS:, :]
    rows_copy.wait()
    cots_copy.wait()
    send.finish()


def experts(*operands):
    vmem = pl.BlockSpec(memory_space=pltpu.VMEM)
    hbm = pl.BlockSpec(memory_space=pl.ANY)
    shape = jax.ShapeDtypeStruct
    count = 256
    return pl.pallas_call(
        expert_kernel,
        out_shape=(
            shape((8, SLOTS, SHARE), BF16),
            shape((8, SLOTS, SHARE), BF16),
            shape((SLOTS, FF_LOCAL), BF16),
            shape((SLOTS, FF_LOCAL), BF16),
            shape((SLOTS, FF_LOCAL), BF16),
            shape((SLOTS, 128), BF16),
            shape((8, ROWS, SHARE), BF16),
            shape((8, ROWS, SHARE), BF16),
            shape((24, SHARE), F32),
            shape((16, 128), F32),
        ),
        in_specs=[vmem] * 7 + [hbm] + [vmem] * 5,
        out_specs=(hbm, hbm) + (vmem,) * 8,
        scratch_shapes=[
            pltpu.VMEM((8, SLOTS, SHARE), BF16),
            pltpu.VMEM((8, SLOTS, SHARE), BF16),
            pltpu.VMEM((2, WIDE, FF_LOCAL), BF16),
            pltpu.VMEM((SLOTS, SHARE), BF16),
            pltpu.VMEM((SLOTS, SHARE), BF16),
            pltpu.VMEM((EXPERTS, 8, 128), F32),
            pltpu.VMEM((EXPERTS, 8, 128), F32),
            pltpu.VMEM((SLOTS, FF_LOCAL), F32),
            pltpu.VMEM((SLOTS, FF_LOCAL), F32),
            pltpu.VMEM((SLOTS, FF_LOCAL), BF16),
            pltpu.VMEM((2, 4, SLOTS, SHARE), BF16),
            pltpu.VMEM((2, 4, SLOTS, SHARE), BF16),
            pltpu.VMEM((2, 4, SLOTS, SHARE), BF16),
            pltpu.VMEM((2, 4, SLOTS, SHARE), BF16),
            pltpu.VMEM((4, SLOTS, SHARE), BF16),
            pltpu.VMEM((3, SLOTS, SHARE), BF16),
            pltpu.VMEM((SLOTS, SHARE), BF16),
            pltpu.VMEM((3, ROWS, SHARE), BF16),
            pltpu.VMEM((3, ROWS, SHARE), BF16),
            pltpu.VMEM((24, 128), F32),
            pltpu.VMEM((7, 24, 128), F32),
            pltpu.VMEM((8, 2 * ROWS, SHARE), BF16),
            pltpu.SemaphoreType.DMA((count,)),
            pltpu.SemaphoreType.DMA((count,)),
            pltpu.SemaphoreType.DMA((3,)),
        ],
        compiler_params=pltpu.CompilerParams(
            collective_id=2, has_side_effects=True, vmem_limit_bytes=60 * 2**20
        ),
        name="experts",
    )(*operands)


def expert_grads_kernel(rows, cots, scaled, grad_gate, grad_up, gate_cols, gateup, down, bias):
    gateup[0] = contract_rows(rows[0], grad_gate[...])
    gateup[1] = contract_rows(rows[0], grad_up[...])
    down[...] = contract_rows(scaled[...], cots[0])
    bias[0] = contract_rows(gate_cols[...], cots[0])[0:8]


def expert_grads(rows, cots, scaled, grad_gate, grad_up, gate_cols):
    whole = pl.BlockSpec((SLOTS, FF_LOCAL), lambda p: (0, 0))
    block = pl.BlockSpec((1, SLOTS, SHARE), lambda p: (p, 0, 0))
    shape = jax.ShapeDtypeStruct
    return pl.pallas_call(
        expert_grads_kernel,
        grid=(BLOCKS,),
        out_shape=(
            shape((2, D, FF_LOCAL), F32),
            shape((FF_LOCAL, D), F32),
            shape((BLOCKS, 8, SHARE), F32),
        ),
        in_specs=[block, block, whole, whole, whole, pl.BlockSpec((SLOTS, 128), lambda p: (0, 0))],
        out_specs=(
            pl.BlockSpec((2, SHARE, FF_LOCAL), lambda p: (0, p, 0)),
            pl.BlockSpec((FF_LOCAL, SHARE), lambda p: (0, p)),
            pl.BlockSpec((1, 8, SHARE), lambda p: (p, 0, 0)),
        ),
        compiler_params=pltpu.CompilerParams(vmem_limit_bytes=40 * 2**20),
        cost_estimate=pl.CostEstimate(
            flops=6 * SLOTS * D * FF_LOCAL, bytes_accessed=22_000_000, transcendentals=0
        ),
        name="expert_grads",
    )(rows, cots, scaled, grad_gate, grad_up, gate_cols)


def input_kernel(
    grad_query, grad_key, grad_value, query_weight, key_weight, value_weight, inputs, scale_row,
    vectors, grad_mixed,
    tokens_out, small_out,
    part, from_sibling, sums, from_y, stat, stats, blocks, send_sems, recv_sems,
):
    me = Place()
    send = Sender(send_sems, recv_sems)
    all_here = greet_tp(me)

    def grad(lo, width):
        return (
            against_rows(grad_query[...], query_weight[lo : lo + width, :])
            + against_rows(grad_key[...], key_weight[lo : lo + width, :])
            + against_rows(grad_value[...], value_weight[lo : lo + width, :])
        )

    def emit(q, block):
        part[q] = block.astype(BF16)

    share_blocks(grad, emit)
    all_here()
    grad_normed = reduce_columns(me, send, part, from_sibling, sums, from_y)
    scale = wide(column_of(scale_row[0:1, :]))
    normal = inputs[...] * scale
    raised = vectors[2:3, :] * grad_normed
    stat[...] = exact_against_rows(jnp.ones((8, SHARE), F32), raised * normal)
    total = exchange(me, send, stat, stats)
    tokens = grad_mixed[me.tp].astype(F32) + scale * (
        raised - normal * wide(column_of(total[0:1, :] * (1.0 / D)))
    )
    blocks[me.tp] = tokens.astype(BF16)
    small_out[...] = jnp.broadcast_to(
        jnp.sum(grad_normed * normal, axis=0, keepdims=True), (8, SHARE)
    )
    gather_columns(me, send, blocks)
    tokens_out[...] = blocks[...]
    send.finish()


def input_grad(*operands):
    return pl.pallas_call(
        input_kernel,
        out_shape=(
            jax.ShapeDtypeStruct((8, ROWS, SHARE), BF16),
            jax.ShapeDtypeStruct((8, SHARE), F32),
        ),
        in_specs=[pl.BlockSpec(memory_space=pltpu.VMEM)] * 10,
        out_specs=(pl.BlockSpec(memory_space=pltpu.VMEM),) * 2,
        scratch_shapes=[
            pltpu.VMEM((8, ROWS, SHARE), BF16),
            pltpu.VMEM((4, ROWS, SHARE), BF16),
            pltpu.VMEM((3, ROWS, SHARE), BF16),
            pltpu.VMEM((3, ROWS, SHARE), BF16),
            pltpu.VMEM((8, 128), F32),
            pltpu.VMEM((7, 8, 128), F32),
            pltpu.VMEM((8, ROWS, SHARE), BF16),
            pltpu.SemaphoreType.DMA((21,)),
            pltpu.SemaphoreType.DMA((21,)),
        ],
        compiler_params=pltpu.CompilerParams(
            collective_id=3, has_side_effects=True, vmem_limit_bytes=40 * 2**20
        ),
        name="input_grad",
    )(*operands)


def joined(blocks):
    return jnp.concatenate([blocks[q] for q in range(BLOCKS)], axis=1)[:, :D]


def shards(
    tokens,
    seq_lengths,
    expert_ids,
    first_gain,
    query_weight,
    key_matrix,
    value_matrix,
    query_bias,
    key_offset_bias,
    value_offset_bias,
    head_sink_logits,
    output_weight,
    output_bias,
    second_gain,
    router_weight,
    router_bias,
    expert_gateup,
    gateup_bias,
    expert_down,
    down_bias,
    cotangent,
):
    tp_place = lax.axis_index("tp")
    ep_place = lax.axis_index("ep")
    place_z, place_x = ep_place // 4, ep_place % 4
    heads_local = query_weight.shape[1] // HEAD_SIZE
    score_scale = HEAD_SIZE ** (-0.5)

    def own_columns(array):
        padded = jnp.pad(array, ((0, 0), (0, WIDE - D)))
        return lax.dynamic_slice_in_dim(padded, tp_place * SHARE, SHARE, 1)

    distance = jnp.arange(EXPERTS)
    expert_of = ((place_z + distance // 4) % 4) * 4 + (place_x + distance % 4) % 4
    turn = (expert_of[:, None] == jnp.arange(EXPERTS)[None, :]).astype(F32)
    chosen = jnp.sum(
        (expert_ids.T[:, None, :] == expert_of[None, :, None]).astype(F32), axis=0
    )
    earlier = (jnp.arange(ROWS)[:, None] < jnp.arange(ROWS)[None, :]).astype(BF16)
    rank = product(chosen.astype(BF16), earlier).astype(jnp.int32)
    at_slot = (rank[:, None, :] == jnp.arange(CAP)[None, :, None]) & (chosen[:, None, :] > 0.5)
    selector = at_slot.astype(BF16).reshape(SLOTS, ROWS)
    selector_t = selector.T
    vectors = own_columns(
        jnp.concatenate(
            [
                output_bias[None],
                second_gain[None],
                first_gain[None],
                jnp.zeros((5, D), F32),
            ]
        )
    )
    router_t = own_columns(product(turn.astype(BF16), router_weight.T).astype(BF16))
    router_bias_turned = jnp.broadcast_to(
        jnp.sum(turn * router_bias[None, :], axis=1, keepdims=True), (EXPERTS, ROWS)
    )
    cot_blocks = jnp.pad(cotangent, ((0, 0), (0, WIDE - D))).reshape(ROWS, BLOCKS, SHARE)
    cot_blocks = cot_blocks.transpose(1, 0, 2)
    cot_own = own_columns(cotangent)
    down = jnp.pad(expert_down[0], ((0, 0), (0, WIDE - D)))
    first_slice = jnp.where(tp_place == 0, 1.0, 0.0).astype(F32)
    down_bias_blocks = jnp.pad(first_slice * down_bias[0], (0, WIDE - D)).reshape(BLOCKS, SHARE)
    gateup_bias_local = jnp.pad(gateup_bias[0], ((0, 6), (0, 0)))

    lengths_row = lax.dynamic_index_in_dim(seq_lengths, ep_place, 0, keepdims=False)
    positions, document = layout(lengths_row, ROWS)
    rotary_angles = angles_of(positions, HEAD_SIZE)
    row_index = jnp.arange(ROWS)
    allowed = (document[:, None] == document[None, :]) & (row_index[None, :] <= row_index[:, None])
    sink_logit_column = head_sink_logits[:, None]
    inputs = tokens.astype(F32)
    first_scale = lax.rsqrt(jnp.mean(inputs * inputs, axis=-1) + EPS)
    normed_low = (inputs * first_scale[:, None] * first_gain).astype(BF16)
    all_normed = lax.all_gather(normed_low, "ep", axis=0, tiled=True)
    query_unrotated = product(normed_low, query_weight) + query_bias
    key_unrotated = product(normed_low, key_matrix) + key_offset_bias
    value_low = (product(normed_low, value_matrix) + value_offset_bias).astype(BF16)

    def rotate_both(query_in, key_in):
        return (
            apply_rotary(query_in.reshape(ROWS, heads_local, HEAD_SIZE), rotary_angles),
            apply_rotary(key_in.reshape(ROWS, 1, HEAD_SIZE), rotary_angles),
        )

    rotated, rotate_back = jax.vjp(rotate_both, query_unrotated, key_unrotated)
    query_low = rotated[0].astype(BF16)
    key_low = rotated[1].astype(BF16)[:, 0]

    def masked_scores():
        raw_scores = (
            jnp.einsum("qgd,kd->gqk", query_low, key_low, preferred_element_type=F32) * score_scale
        )
        return jnp.where(allowed[None], raw_scores, NEGATIVE)

    scores = masked_scores()
    log_total = log_totals(scores, sink_logit_column)
    probs_low = jnp.exp(scores - log_total[..., None]).astype(BF16)
    head_values = jnp.einsum("gqk,kd->qgd", probs_low, value_low, preferred_element_type=F32)
    heads_low = head_values.reshape(ROWS, heads_local * HEAD_SIZE).astype(BF16)
    all_heads = lax.all_gather(heads_low, "ep", axis=0, tiled=True)

    second, mixed, stat = attend_end(
        heads_low,
        output_weight,
        own_columns(inputs),
        vectors,
        router_t,
        router_bias_turned,
        chosen,
    )
    (
        expert_rows, cot_rows, scaled_hidden, grad_gate, grad_up, gate_cols,
        grad_att_blocks, layer_blocks, small, grad_logits,
    ) = experts(
        second, mixed, stat, selector, selector_t, cot_blocks, cot_own, expert_gateup[0], down,
        gateup_bias_local, down_bias_blocks, router_t, vectors,
    )
    grad_gateup, grad_down, grad_down_bias = expert_grads(
        expert_rows, cot_rows, scaled_hidden, grad_gate, grad_up, gate_cols
    )
    grad_gateup_bias = jnp.stack(
        [jnp.sum(grad_gate.astype(F32), axis=0), jnp.sum(grad_up.astype(F32), axis=0)]
    )[None]
    grad_down_bias = (grad_down_bias[:, 0] + grad_down_bias[:, 1]).reshape(1, WIDE)[:, :D]
    layer_output = joined(layer_blocks)
    grad_attended = joined(grad_att_blocks)
    all_grad_attended = lax.all_gather(grad_attended, "ep", axis=0, tiled=True)
    grad_output_weight = contract_rows(all_heads, all_grad_attended)

    grad_heads = (
        against_rows(grad_attended, output_weight).astype(BF16).reshape(ROWS, heads_local, HEAD_SIZE)
    )
    probs_full = jnp.exp(masked_scores() - log_total[..., None])
    grad_probs = jnp.einsum("qgd,kd->gqk", grad_heads, value_low, preferred_element_type=F32)
    row_delta = jnp.sum(probs_full * grad_probs, axis=-1)
    grad_scores = (probs_full * (grad_probs - row_delta[..., None])).astype(BF16)
    grad_sinks = -jnp.sum(jnp.exp(sink_logit_column - log_total) * row_delta, axis=-1)
    grad_values_low = jnp.einsum(
        "gqk,qgd->kd", probs_low, grad_heads, preferred_element_type=F32
    ).astype(BF16)
    grad_query_rot = (
        jnp.einsum("gqk,kd->qgd", grad_scores, key_low, preferred_element_type=F32) * score_scale
    )
    grad_key_rot = (
        jnp.einsum("gqk,qgd->kd", grad_scores, query_low, preferred_element_type=F32) * score_scale
    )
    grad_query_pre, grad_key_pre = rotate_back((grad_query_rot, grad_key_rot[:, None, :]))
    grad_query_low = grad_query_pre.astype(BF16)
    grad_key_low = grad_key_pre.astype(BF16)
    grad_heads_all = jnp.concatenate([grad_query_low, grad_key_low, grad_values_low], axis=1)
    all_grad_heads = lax.all_gather(grad_heads_all, "ep", axis=0, tiled=True)

    token_blocks, first_small = input_grad(
        grad_query_low,
        grad_key_low,
        grad_values_low,
        query_weight,
        key_matrix,
        value_matrix,
        own_columns(inputs),
        jnp.broadcast_to(first_scale[None, :], (8, ROWS)),
        vectors,
        grad_att_blocks,
    )
    grad_tokens = joined(token_blocks).astype(F32)
    grad_qkv_weight = contract_rows(all_normed, all_grad_heads)
    width = heads_local * HEAD_SIZE
    own_router = contract_rows(turn, small[:16])
    pieces = jnp.concatenate([own_router, small[16:18], first_small[:1]], axis=0)
    lines = jnp.concatenate(
        [
            pieces.reshape(-1),
            jnp.sum(grad_heads_all.astype(F32), axis=0),
            grad_sinks,
            jnp.sum(turn * jnp.sum(grad_logits, axis=1)[:, None], axis=0),
        ]
    )
    lines = lax.psum(lines, "ep")
    count = 19 * SHARE
    across = lax.all_gather(lines[:count].reshape(19, SHARE), "tp", axis=1, tiled=True)[:, :D]
    heads_sum = lines[count : count + width + 2 * HEAD_SIZE]
    rest = lines[count + width + 2 * HEAD_SIZE :]
    return (
        layer_output,
        grad_tokens,
        across[18],
        grad_qkv_weight[:, :width],
        grad_qkv_weight[:, width : width + HEAD_SIZE],
        grad_qkv_weight[:, width + HEAD_SIZE :],
        heads_sum[:width],
        heads_sum[width : width + HEAD_SIZE],
        heads_sum[width + HEAD_SIZE :],
        rest[:heads_local],
        grad_output_weight,
        across[17],
        across[16],
        across[:16].T,
        rest[heads_local:],
        grad_gateup[None],
        grad_gateup_bias,
        grad_down[None],
        grad_down_bias,
    )


def solution(mesh):
    in_specs = (
        P("ep", None),
        P(),
        P("ep", None),
        P(),
        P(None, "tp"),
        P(None, "tp"),
        P(None, "tp"),
        P("tp"),
        P("tp"),
        P("tp"),
        P("tp"),
        P("tp", None),
        P(),
        P(),
        P(),
        P(),
        P("ep", None, None, "tp"),
        P("ep", None, "tp"),
        P("ep", "tp", None),
        P("ep", None),
        P("ep", None),
    )
    out_specs = (
        P("ep", None),
        P("ep", None),
        P(),
        P(None, "tp"),
        P(None, "tp"),
        P(None, "tp"),
        P("tp"),
        P("tp"),
        P("tp"),
        P("tp"),
        P("tp", None),
        P(),
        P(),
        P(),
        P(),
        P("ep", None, None, "tp"),
        P("ep", None, "tp"),
        P("ep", "tp", None),
        P("ep", None),
    )
    return jax.shard_map(shards, mesh=mesh, in_specs=in_specs, out_specs=out_specs, check_vma=False)
```

```python
from functools import partial

import jax
import jax.numpy as jnp
from jax import lax
from jax.experimental import pallas as pl
from jax.experimental.pallas import tpu as pltpu
from jax.sharding import PartitionSpec as P

HEAD_SIZE = 64
EPS = 1e-05
THETA = 150000.0
LIMIT = 7.0
ALPHA = 1.702
NEGATIVE = -1e30

D = 2880
FF_LOCAL = 360
SHARE = 384
BLOCKS = 8
WIDE = SHARE * BLOCKS
ROWS = 128
EXPERTS = 16
CAP = 48
SLOTS = EXPERTS * CAP
HALF = SLOTS // 2
HEADS = 8
QUARTER = SLOTS // 4
MESH = pl.DeviceIdType.MESH
F32 = jnp.float32
BF16 = jnp.bfloat16
HIGHEST = lax.Precision.HIGHEST


def product(left, right):
    return jnp.dot(left, right, preferred_element_type=F32)


def contract_rows(left, right):
    return lax.dot_general(left, right, (((0,), (0,)), ((), ())), preferred_element_type=F32)


def against_rows(left, right):
    return lax.dot_general(left, right, (((1,), (1,)), ((), ())), preferred_element_type=F32)


def exact(left, right, left_dim=1, right_dim=0):
    return lax.dot_general(
        left,
        right,
        (((left_dim,), (right_dim,)), ((), ())),
        preferred_element_type=F32,
        precision=HIGHEST,
    )


def row_sums(columns):
    return exact(jnp.ones((8, columns.shape[1]), F32), columns, 1, 1)


class Place:
    def __init__(self):
        self.ep = lax.axis_index("ep")
        self.tp = lax.axis_index("tp")
        self.z, self.x = self.ep // 4, self.ep % 4
        self.y, self.core = self.tp // 2, self.tp % 2

    def sibling(self):
        return (self.ep, self.y * 2 + (1 - self.core))

    def along_y(self, step):
        return (self.ep, lax.rem(self.y + step, 4) * 2 + self.core)

    def along_tp(self, step):
        return (self.ep, lax.rem(self.tp + step, 8))

    def along_ep(self, k):
        z = lax.rem(self.z + k // 4, 4)
        x = lax.rem(self.x + k % 4, 4)
        return (z * 4 + x, self.tp)

    def back_ep(self, k):
        z = lax.rem(self.z + 4 - k // 4, 4)
        x = lax.rem(self.x + 4 - k % 4, 4)
        return (z * 4 + x, self.tp)

    def greet(self, tp, ep):
        barrier = pltpu.get_barrier_semaphore()
        partners = [self.along_tp(i) for i in range(1, 8) if tp]
        partners += [self.along_ep(k) for k in range(1, 16) if ep]
        for device in partners:
            pl.semaphore_signal(barrier, inc=1, device_id=device, device_id_type=MESH)
        return lambda: pl.semaphore_wait(barrier, len(partners))


class Sender:
    def __init__(self, me, send_sems, recv_sems):
        self.me, self.send_sems, self.recv_sems = me, send_sems, recv_sems
        self.used = 0
        self.open = []

    def start(self, source, target, device):
        n = self.used
        self.used += 1
        copy = pltpu.make_async_remote_copy(
            src_ref=source,
            dst_ref=target,
            send_sem=self.send_sems.at[n],
            recv_sem=self.recv_sems.at[n],
            device_id=device,
            device_id_type=MESH,
        )
        copy.start()
        self.open.append(copy)
        return n

    def arrived(self, n, target):
        pltpu.make_async_remote_copy(
            src_ref=target,
            dst_ref=target,
            send_sem=self.send_sems.at[n],
            recv_sem=self.recv_sems.at[n],
            device_id=self.me.sibling(),
            device_id_type=MESH,
        ).wait_recv()

    def finish(self):
        for copy in self.open:
            copy.wait_send()
        self.open = []


class GroupGather:
    def __init__(self, me, send, buffer, lines, shared):
        self.me, self.send, self.buffer, self.shared = me, send, buffer, shared
        self.size = lines // (4 if shared else 2)
        self.first, self.then, self.passed = {}, {}, {}

    def span(self, part, core):
        start = part * self.size
        if self.shared:
            start = core * (2 * self.size) + start
        return pl.ds(pl.multiple_of(start, 16), self.size)

    def own(self, part):
        return self.span(part, self.me.core)

    def begin(self):
        for d in (1, 2, 3):
            for part, k in ((0, d), (1, 4 * d)):
                span = self.own(part)
                self.first[part, d] = self.send.start(
                    self.buffer.at[0, span], self.buffer.at[k, span], self.me.along_ep(k)
                )

    def spread(self):
        for part in (0, 1):
            span = self.own(part)
            for d in (1, 2, 3):
                k = d if part == 0 else 4 * d
                self.send.arrived(self.first[part, d], self.buffer.at[k, span])
        for d in (1, 2, 3):
            span = self.own(0)
            self.then[0, d] = self.send.start(
                self.buffer.at[0:4, span],
                self.buffer.at[4 * d : 4 * d + 4, span],
                self.me.along_ep(4 * d),
            )
            span = self.own(1)
            self.then[1, d] = [
                self.send.start(
                    self.buffer.at[4 * i, span], self.buffer.at[4 * i + d, span], self.me.along_ep(d)
                )
                for i in range(4)
            ]

    def landed(self, j):
        if j == 0:
            return
        self.send.arrived(self.then[0, j], self.buffer.at[4 * j : 4 * j + 4, self.own(0)])
        for i in range(4):
            self.send.arrived(self.then[1, j][i], self.buffer.at[4 * i + j, self.own(1)])

    def groups(self, j):
        low = 1 if j == 0 else 0
        return [(0, slice(4 * j + low, 4 * j + 4))] + [(1, 4 * i + j) for i in range(low, 4)]

    def pass_on(self, j):
        self.passed[j] = []
        for part, slots in self.groups(j):
            block = self.buffer.at[slots, self.own(part)]
            self.passed[j].append(self.send.start(block, block, self.me.sibling()))

    def complete(self, j):
        for n, (part, slots) in zip(self.passed[j], self.groups(j)):
            self.send.arrived(n, self.buffer.at[slots, self.span(part, 1 - self.me.core)])


def column_of(row):
    return jnp.transpose(jnp.broadcast_to(row, (128, 128)))


def column_share(row):
    return jnp.concatenate([column_of(row[:, j : j + 128]) for j in range(0, SHARE, 128)], axis=0)


def share_blocks(part, emit):
    for q in range(BLOCKS):
        lo = q * SHARE
        width = min(SHARE, D - lo)
        block = part(lo, width)
        if width < SHARE:
            block = jnp.concatenate(
                [block, jnp.zeros((SHARE - width, block.shape[1]), block.dtype)], axis=0
            )
        emit(q, block)


def reduce_shares(me, send, part, from_sibling, sums, from_y):
    order = (2, 1, 3, 0)
    ticket = []
    for i, step in enumerate(order):
        y = lax.rem(me.y + step, 4)
        ticket.append(
            send.start(part.at[y * 2 + 1 - me.core], from_sibling.at[i], me.sibling())
        )
    landed = []
    for i, step in enumerate(order):
        y = lax.rem(me.y + step, 4)
        send.arrived(ticket[i], from_sibling.at[i])
        total = part[y * 2 + me.core].astype(F32) + from_sibling[i].astype(F32)
        if step:
            sums[i] = total.astype(BF16)
            landed.append(send.start(sums.at[i], from_y.at[i], me.along_y(step)))
    for i, n in enumerate(landed):
        send.arrived(n, from_y.at[i])
        total = total + from_y[i].astype(F32)
    return total


def exchange(me, send, own, others):
    tickets = [send.start(own, others.at[i - 1], me.along_tp(i)) for i in range(1, 8)]
    total = own[...]
    for i, n in enumerate(tickets):
        send.arrived(n, others.at[i])
        total = total + others[i]
    return total


def start_gather_shares(me, send, blocks):
    own = blocks.at[me.tp]
    to_y = [send.start(own, own, me.along_y(step)) for step in (2, 1, 3)]
    to_sibling = [send.start(own, own, me.sibling())]

    def end():
        for n, step in zip(to_y, (2, 1, 3)):
            block = blocks.at[lax.rem(me.y + 4 - step, 4) * 2 + me.core]
            send.arrived(n, block)
            to_sibling.append(send.start(block, block, me.sibling()))
        for n, step in zip(to_sibling, (0, 2, 1, 3)):
            send.arrived(n, blocks.at[lax.rem(me.y + 4 - step, 4) * 2 + 1 - me.core])

    return end


def vmem(count):
    return [pl.BlockSpec(memory_space=pltpu.VMEM)] * count


def hbm(count):
    return [pl.BlockSpec(memory_space=pl.ANY)] * count


def semaphores(count):
    return [pltpu.SemaphoreType.DMA((count,)), pltpu.SemaphoreType.DMA((count,))]


def params(number, megabytes):
    return pltpu.CompilerParams(
        collective_id=number, has_side_effects=True, vmem_limit_bytes=megabytes * 2**20
    )


shape = jax.ShapeDtypeStruct


def turned(me):
    k = lax.broadcasted_iota(jnp.int32, (EXPERTS, EXPERTS), 0)
    e = lax.broadcasted_iota(jnp.int32, (EXPERTS, EXPERTS), 1)
    name = ((me.z + (k >> 2)) & 3) * 4 + ((me.x + (k & 3)) & 3)
    return (name == e).astype(F32)


def rotate(pair, trig, back=False):
    first, last = pair[0:32], pair[32:64]
    cosine, sine = trig[0:32, :], trig[32:64, :]
    if back:
        sine = -sine
    return jnp.concatenate([first * cosine - last * sine, last * cosine + first * sine], axis=0)


def front_kernel(
    tokens, query_weight, key_weight, value_weight, output_weight, router, vectors, biases, sinks,
    router_bias, ids, trig, allowed,
    second, mixed_out, stat_out, selector, normed, queries, keys_values, heads, log_total, first_scale,
    router_out,
    padded, wide_normed, vecs, wide_router, part, from_sibling, sums, from_y, stat, stats,
    send_sems, recv_sems,
):
    me = Place()
    send = Sender(me, send_sems, recv_sems)
    all_here = me.greet(True, False)
    vecs[:, 0:D] = vectors[...]
    vecs[:, D:] = jnp.zeros((8, WIDE - D), F32)
    padded[0:D, :] = tokens[...]
    padded[D:, :] = jnp.zeros((WIDE - D, ROWS), BF16)

    def squares(j, total):
        lines = padded[pl.ds(pl.multiple_of(j * 96, 96), 96), :].astype(F32)
        return total + jnp.sum(lines * lines, axis=0, keepdims=True)

    scale = lax.rsqrt(lax.fori_loop(0, 30, squares, jnp.zeros((1, ROWS), F32)) * (1.0 / D) + EPS)
    first_scale[...] = jnp.broadcast_to(scale, (8, ROWS))

    @pl.loop(0, 23)
    def _(j):
        span = pl.ds(pl.multiple_of(j * 128, 128), 128)
        gain = column_of(vecs[2:3, span])
        wide_normed[span, :] = (padded[span, :].astype(F32) * scale * gain).astype(BF16)

    normed[...] = wide_normed[0:D, :]
    query_rows = contract_rows(normed[...], query_weight[...]) + biases[0:1, 0:512]
    both = jnp.concatenate(
        [product(key_weight[...], normed[...]), product(value_weight[...], normed[...])], axis=0
    ) + column_of(biases[0:1, 512:640])
    both = jnp.concatenate([rotate(both[0:64], trig), both[64:128]], axis=0)
    keys_values[...] = both.astype(BF16)
    key_rows = jnp.transpose(both)[:, 0:64].astype(BF16)
    for j in range(4):
        pair = jnp.transpose(query_rows[:, j * 128 : (j + 1) * 128])
        queries[j * 128 : j * 128 + 64, :] = rotate(pair[0:64], trig).astype(BF16)
        queries[j * 128 + 64 : j * 128 + 128, :] = rotate(pair[64:128], trig).astype(BF16)
    included = allowed[...] > 0.5
    for h in range(HEADS):
        scores = product(key_rows, queries[h * 64 : h * 64 + 64, :]) * (HEAD_SIZE**-0.5)
        scores = jnp.where(included, scores, NEGATIVE)
        sink = sinks[h : h + 1, :]
        highest = jnp.maximum(jnp.max(scores, axis=0, keepdims=True), sink)
        total = jnp.exp(sink - highest) + jnp.sum(
            jnp.exp(scores - highest), axis=0, keepdims=True
        )
        logs = highest + jnp.log(total)
        log_total[h : h + 1, :] = logs
        probs = jnp.exp(scores - logs).astype(BF16)
        heads[h * 64 : h * 64 + 64, :] = product(keys_values[64:128, :], probs).astype(BF16)

    def emit(q, block):
        part[q] = block.astype(BF16)

    share_blocks(lambda lo, width: product(output_weight[lo : lo + width, :], heads[...]), emit)

    turn = turned(me)
    wide_router[:, 0:D] = product(turn.astype(BF16), router[...]).astype(BF16)
    wide_router[:, D:] = jnp.zeros((EXPERTS, WIDE - D), BF16)
    k = lax.broadcasted_iota(jnp.int32, (EXPERTS, ROWS), 0)
    name = ((me.z + (k >> 2)) & 3) * 4 + ((me.x + (k & 3)) & 3)
    chosen = jnp.zeros((EXPERTS, ROWS), F32)
    for j in range(4):
        chosen = chosen + (name == ids[j : j + 1, :]).astype(F32)
    taken = chosen > 0.5
    before = lax.broadcasted_iota(jnp.int32, (ROWS, ROWS), 0) < lax.broadcasted_iota(
        jnp.int32, (ROWS, ROWS), 1
    )
    rank = product(chosen.astype(BF16), before.astype(F32).astype(BF16))
    rank = jnp.where(taken, rank, -1.0)
    place = lax.broadcasted_iota(jnp.int32, (CAP, ROWS), 0).astype(F32)
    for k in range(EXPERTS):
        selector[k * CAP : (k + 1) * CAP, :] = (
            (place == rank[k : k + 1, :]).astype(F32).astype(BF16)
        )
    mine = pl.ds(pl.multiple_of(me.tp * SHARE, SHARE), SHARE)
    share = vecs[:, mine]
    router_share = wide_router[:, mine]
    router_out[...] = router_share
    base = padded[mine, :].astype(F32) + column_share(share[0:1])
    gain = column_share(share[1:2])
    all_here()

    mixed = base + reduce_shares(me, send, part, from_sibling, sums, from_y)
    mixed_out[...] = mixed
    raised = mixed * gain
    stat[0:16, :] = product(router_share, raised.astype(BF16))
    stat[16:24, :] = jnp.broadcast_to(jnp.sum(mixed * mixed, axis=0, keepdims=True), (8, ROWS))
    total = exchange(me, send, stat, stats)
    scale = lax.rsqrt(total[16:17, :] * (1.0 / D) + EPS)
    second[...] = (raised * scale).astype(BF16)
    plain = total[0:16, :] * scale
    logits = plain + exact(turn, router_bias[...])
    highest = jnp.max(jnp.where(taken, logits, NEGATIVE), axis=0, keepdims=True)
    lifted = jnp.where(taken, jnp.exp(jnp.where(taken, logits, highest) - highest), 0.0)
    stat_out[0:16, :] = lifted / jnp.sum(lifted, axis=0, keepdims=True)
    stat_out[16:32, :] = plain
    stat_out[32:40, :] = jnp.broadcast_to(scale, (8, ROWS))
    send.finish()


def front(*operands):
    return pl.pallas_call(
        front_kernel,
        out_shape=(
            shape((SHARE, ROWS), BF16),
            shape((SHARE, ROWS), F32),
            shape((40, ROWS), F32),
            shape((SLOTS, ROWS), BF16),
            shape((D, ROWS), BF16),
            shape((512, ROWS), BF16),
            shape((128, ROWS), BF16),
            shape((512, ROWS), BF16),
            shape((8, ROWS), F32),
            shape((8, ROWS), F32),
            shape((EXPERTS, SHARE), BF16),
        ),
        in_specs=vmem(13),
        out_specs=tuple(vmem(11)),
        scratch_shapes=[
            pltpu.VMEM((WIDE, ROWS), BF16),
            pltpu.VMEM((WIDE, ROWS), BF16),
            pltpu.VMEM((8, WIDE), F32),
            pltpu.VMEM((EXPERTS, WIDE), BF16),
            pltpu.VMEM((8, SHARE, ROWS), BF16),
            pltpu.VMEM((4, SHARE, ROWS), BF16),
            pltpu.VMEM((3, SHARE, ROWS), BF16),
            pltpu.VMEM((3, SHARE, ROWS), BF16),
            pltpu.VMEM((24, ROWS), F32),
            pltpu.VMEM((7, 24, ROWS), F32),
            *semaphores(14),
        ],
        compiler_params=params(1, 40),
        name="front",
    )(*operands)


def activation_parts(gate_pre, up_pre):
    lowered = LIMIT - gate_pre
    cap = jnp.maximum(lowered, 0.0) + jnp.log(1.0 + jnp.exp(-jnp.abs(lowered)))
    capped_gate = LIMIT - cap
    tanh = jnp.tanh(up_pre * (1.0 / LIMIT))
    capped_up = LIMIT * tanh
    sigmoid = 1.0 / (1.0 + jnp.exp(-ALPHA * capped_gate))
    return lowered, capped_gate, tanh, capped_up, sigmoid


def expert_kernel(
    second, mixed, stat, selector, cotangent, gateup, down, tails, gateup_bias, down_bias, router, vectors,
    normed, heads,
    rows_out, cots_out, scaled_out, grad_gate_out, grad_up_out, gate_cols_out,
    grad_att_out, layer_out, small_out, grad_logits_out, normed_all, heads_all,
    R, C, weights, wide_cot, vecs, staged, staged_c, gates_send, gates, gate_pre, up_pre, hidden,
    to_sibling, kept, from_sibling, sums, results, from_y, home, wire, from_y_small, stat_own, stats,
    both, send_sems, recv_sems, local_sems,
):
    me = Place()
    send = Sender(me, send_sems, recv_sems)
    all_here = me.greet(True, True)
    last = 2816
    loads = [
        pltpu.make_async_copy(
            gateup.at[:, :, 0:last], weights.at[0:2, :, 0:last], local_sems.at[0]
        ),
        pltpu.make_async_copy(down.at[:, 0:last], weights.at[2, :, 0:last], local_sems.at[1]),
        pltpu.make_async_copy(tails, weights.at[:, :, last:], local_sems.at[2]),
    ]
    for load in loads:
        load.start()
    own_copies = [
        pltpu.make_async_copy(normed, normed_all.at[0], local_sems.at[3]),
        pltpu.make_async_copy(heads, heads_all.at[0], local_sems.at[4]),
    ]
    for copy in own_copies:
        copy.start()
    wide_cot[0:D, :] = cotangent[...]
    wide_cot[D:, :] = jnp.zeros((WIDE - D, ROWS), BF16)
    vecs[:, 0:D] = vectors[...]
    vecs[:, D:] = jnp.zeros((8, WIDE - D), F32)
    mine = pl.ds(pl.multiple_of(me.tp * SHARE, SHARE), SHARE)
    staged[...] = against_rows(selector[...], second[...]).astype(BF16)
    staged_c[...] = against_rows(selector[...], wide_cot[mine, :]).astype(BF16)
    for k in range(EXPERTS):
        row = jnp.broadcast_to(stat[k : k + 1, :], (8, 128))
        picked = exact(row, selector[k * CAP : (k + 1) * CAP, :].astype(F32), 1, 1)
        gates_send[k] = jnp.concatenate([picked, jnp.zeros((8, 128 - CAP), F32)], axis=1)
    all_here()

    def scatter(source, target):
        tickets = [None]
        for k in range(1, EXPERTS):
            lines = pl.ds(k * CAP, CAP)
            tickets.append(
                send.start(source.at[lines], target.at[me.tp, lines], me.along_ep(k))
            )
        target[me.tp, 0:CAP, :] = source[0:CAP, :]
        return tickets

    rows_in = scatter(staged, R)
    gates_in = [None]
    for k in range(1, EXPERTS):
        gates_in.append(send.start(gates_send.at[k], gates.at[k], me.along_ep(k)))
    gates[0] = gates_send[0]
    cots_in = scatter(staged_c, C)
    for copy in own_copies:
        copy.wait()
    all_normed = GroupGather(me, send, normed_all, D, True)
    all_heads = GroupGather(me, send, heads_all, 512, False)
    all_normed.begin()
    all_heads.begin()

    steps = (1, 3, 2)

    def spread(buffer, tickets, j):
        lines = pl.ds(j * QUARTER, QUARTER)
        for k in range(4 * j, 4 * j + 4):
            if k:
                send.arrived(tickets[k], buffer.at[me.tp, pl.ds(k * CAP, CAP)])
        own = buffer.at[me.tp, lines]
        return [send.start(own, own, me.along_y(s)) for s in steps] + [
            send.start(own, own, me.sibling())
        ]

    def pass_on(buffer, tickets, j):
        lines = pl.ds(j * QUARTER, QUARTER)
        sent = [tickets[3]]
        for n, s in zip(tickets, steps):
            block = buffer.at[lax.rem(me.y + 4 - s, 4) * 2 + me.core, lines]
            send.arrived(n, block)
            sent.append(send.start(block, block, me.sibling()))
        return sent

    def complete(buffer, tickets, j):
        lines = pl.ds(j * QUARTER, QUARTER)
        for n, s in zip(tickets, (0,) + steps):
            send.arrived(n, buffer.at[lax.rem(me.y + 4 - s, 4) * 2 + 1 - me.core, lines])

    a, b = [None] * 4, [None] * 4
    a[0] = spread(R, rows_in, 0)
    a[1] = spread(R, rows_in, 1)
    a[0] = pass_on(R, a[0], 0)
    a[2] = spread(R, rows_in, 2)
    a[1] = pass_on(R, a[1], 1)
    a[3] = spread(R, rows_in, 3)
    a[2] = pass_on(R, a[2], 2)
    for j in range(4):
        b[j] = spread(C, cots_in, j)
    all_normed.spread()
    all_heads.spread()
    complete(R, a[0], 0)
    complete(R, a[1], 1)
    for load in loads:
        load.wait()

    def lines_of(h):
        return pl.ds(h * HALF, HALF)

    def forward(h):
        lines = lines_of(h)
        gate_pre[lines, :] = jnp.broadcast_to(gateup_bias[0:1, :], (HALF, FF_LOCAL))
        up_pre[lines, :] = jnp.broadcast_to(gateup_bias[1:2, :], (HALF, FF_LOCAL))

        @pl.loop(0, 4)
        def _(y):
            block = jnp.concatenate([R[2 * y, lines, :], R[2 * y + 1, lines, :]], axis=1)
            span = pl.ds(pl.multiple_of(y * 2 * SHARE, 2 * SHARE), 2 * SHARE)
            gate_pre[lines, :] += against_rows(block, weights[0, :, span])
            up_pre[lines, :] += against_rows(block, weights[1, :, span])

        _, capped_gate, _, capped_up, sigmoid = activation_parts(
            gate_pre[lines, :], up_pre[lines, :]
        )
        hidden[lines, :] = ((capped_up + 1.0) * capped_gate * sigmoid).astype(BF16)

        def out_block(q):
            span = pl.ds(pl.multiple_of(q * SHARE, SHARE), SHARE)
            return product(hidden[lines, :], weights[2, :, span]) + down_bias[pl.ds(q, 1), :]

        sent = []
        for y in range(4):
            to_sibling[0, y, lines, :] = out_block(2 * y + 1 - me.core).astype(BF16)
            sent.append(
                send.start(
                    to_sibling.at[0, y, lines], from_sibling.at[0, y, lines], me.sibling()
                )
            )
        for y in range(4):
            kept[0, y, lines, :] = out_block(2 * y + me.core).astype(BF16)
        return sent

    def results_home(h, sent):
        lines = lines_of(h)
        for y in range(4):
            send.arrived(sent[y], from_sibling.at[0, y, lines])
            sums[0, y, lines, :] = (
                kept[0, y, lines, :].astype(F32) + from_sibling[0, y, lines, :].astype(F32)
            ).astype(BF16)
        tickets = []
        for k in range(8 * h, 8 * h + 8):
            span = pl.ds(k * CAP, CAP)
            if k:
                tickets.append(
                    send.start(sums.at[0, :, span], results.at[:, span], me.back_ep(k))
                )
            else:
                tickets.append(None)
                results[:, 0:CAP, :] = sums[0, :, 0:CAP, :]
        return tickets

    sent_0 = forward(0)
    a[3] = pass_on(R, a[3], 3)
    b[0] = pass_on(C, b[0], 0)
    complete(R, a[2], 2)
    complete(R, a[3], 3)
    rows_copy = pltpu.make_async_copy(R, rows_out, local_sems.at[5])
    rows_copy.start()
    sent_1 = forward(1)
    back = results_home(0, sent_0)
    for j in (1, 2, 3):
        b[j] = pass_on(C, b[j], j)
    back = back + results_home(1, sent_1)
    for k in range(1, EXPERTS):
        send.arrived(gates_in[k], gates.at[k])
    gate_rows = jnp.concatenate(
        [gates[:, 0, :], jnp.zeros((128 - EXPERTS, 128), F32)], axis=0
    )
    gate_cols = jnp.transpose(gate_rows)

    def gate_column(h):
        return jnp.concatenate(
            [gate_cols[0:CAP, k : k + 1] for k in range(8 * h, 8 * h + 8)], axis=0
        )

    def backward(h):
        lines = lines_of(h)
        gate = gate_column(h)
        high = gate.astype(BF16)
        low = (gate - high.astype(F32)).astype(BF16)
        place = lax.broadcasted_iota(jnp.int32, (HALF, 128), 1)
        gate_cols_out[lines, :] = jnp.where(
            place == 0,
            high.astype(F32),
            jnp.where(place == 1, low.astype(F32), 0.0),
        ).astype(BF16)

        def step(y, total):
            block = jnp.concatenate([C[2 * y, lines, :], C[2 * y + 1, lines, :]], axis=1)
            span = pl.ds(pl.multiple_of(y * 2 * SHARE, 2 * SHARE), 2 * SHARE)
            return total + against_rows(block, weights[2, :, span])

        grad_hidden = gate * lax.fori_loop(0, 4, step, jnp.zeros((HALF, FF_LOCAL), F32))
        lowered, capped_gate, tanh, capped_up, sigmoid = activation_parts(
            gate_pre[lines, :], up_pre[lines, :]
        )
        scaled_out[lines, :] = (gate * hidden[lines, :].astype(F32)).astype(BF16)
        slope = (capped_up + 1.0) * (
            sigmoid + ALPHA * capped_gate * sigmoid * (1.0 - sigmoid)
        )
        grad_gate_out[lines, :] = (
            grad_hidden * slope * (1.0 / (1.0 + jnp.exp(-lowered)))
        ).astype(BF16)
        grad_up_out[lines, :] = (
            grad_hidden * capped_gate * sigmoid * (1.0 - tanh * tanh)
        ).astype(BF16)

        def back_block(q):
            span = pl.ds(pl.multiple_of(q * SHARE, SHARE), SHARE)
            return product(grad_gate_out[lines, :], weights[0, :, span]) + product(
                grad_up_out[lines, :], weights[1, :, span]
            )

        sent = []
        for s in (2, 1, 3, 0):
            y = lax.rem(me.y + s, 4)
            to_sibling[1, s, lines, :] = back_block(2 * y + 1 - me.core).astype(BF16)
            sent.append(
                send.start(
                    to_sibling.at[1, s, lines], from_sibling.at[1, s, lines], me.sibling()
                )
            )
        landed = []
        for s, n in zip((2, 1, 3, 0), sent):
            y = lax.rem(me.y + s, 4)
            block = back_block(2 * y + me.core)
            send.arrived(n, from_sibling.at[1, s, lines])
            total = block + from_sibling[1, s, lines, :].astype(F32)
            if s:
                sums[1, s, lines, :] = total.astype(BF16)
                landed.append(
                    send.start(
                        sums.at[1, s, lines], from_y.at[s - 1, lines], me.along_y(s)
                    )
                )
            else:
                kept[1, 0, lines, :] = total.astype(BF16)
        return landed

    def grads_home(h, landed):
        lines = lines_of(h)
        total = kept[1, 0, lines, :].astype(F32)
        for s, n in zip((2, 1, 3), landed):
            send.arrived(n, from_y.at[s - 1, lines])
            total = total + from_y[s - 1, lines, :].astype(F32)
        sums[1, 0, lines, :] = total.astype(BF16)
        tickets = []
        for k in range(8 * h, 8 * h + 8):
            span = pl.ds(k * CAP, CAP)
            if k:
                tickets.append(
                    send.start(sums.at[1, 0, span], home.at[span], me.back_ep(k))
                )
            else:
                tickets.append(None)
                home[0:CAP, :] = sums[1, 0, 0:CAP, :]
        return tickets

    complete(C, b[0], 0)
    complete(C, b[1], 1)
    landed_0 = backward(0)
    complete(C, b[2], 2)
    complete(C, b[3], 3)
    cots_copy = pltpu.make_async_copy(C, cots_out, local_sems.at[6])
    cots_copy.start()
    landed_1 = backward(1)
    for j in range(4):
        all_normed.landed(j)
        all_normed.pass_on(j)
    home_in = grads_home(0, landed_0)
    home_in = home_in + grads_home(1, landed_1)

    for k in range(1, EXPERTS):
        send.arrived(back[k], results.at[:, pl.ds(k * CAP, CAP)])
    spread_gates = jnp.concatenate(
        [jnp.broadcast_to(stat[k : k + 1, :], (CAP, 128)) for k in range(EXPERTS)], axis=0
    )
    weighted = selector[...].astype(F32) * spread_gates
    high = weighted.astype(BF16)
    low = (weighted - high.astype(F32)).astype(BF16)
    pairs = jnp.zeros((SLOTS, ROWS), F32)
    to_y = []
    for s in (2, 1, 3, 0):
        q = lax.rem(me.y + s, 4) * 2 + me.core
        block = results[lax.rem(me.y + s, 4)]
        pairs = pairs + product(
            block, wide_cot[pl.ds(pl.multiple_of(q * SHARE, SHARE), SHARE), :]
        )
        total = contract_rows(block, high) + contract_rows(block, low)
        if s:
            wire[s - 1] = total.astype(BF16)
            to_y.append(send.start(wire.at[s - 1], from_y_small.at[s - 1], me.along_y(s)))
    moe_out = total
    pairs = pairs * selector[...].astype(F32)
    for k in range(EXPERTS):
        stat_own[k : k + 1, :] = jnp.sum(pairs[k * CAP : (k + 1) * CAP], axis=0, keepdims=True)
    share = vecs[:, mine]
    gain = column_share(share[1:2])
    scale = stat[32:33, :]
    normal = mixed[...] * scale
    for k in range(1, EXPERTS):
        send.arrived(home_in[k], home.at[pl.ds(k * CAP, CAP)])
    returned = contract_rows(home[...], selector[...])
    stat_own[16:24, :] = jnp.broadcast_to(
        jnp.sum(returned * gain * normal, axis=0, keepdims=True), (8, ROWS)
    )
    total = exchange(me, send, stat_own, stats)
    gate_share = stat[0:16, :]
    grad_gates = total[0:16, :]
    grad_logits = gate_share * (
        grad_gates - jnp.sum(gate_share * grad_gates, axis=0, keepdims=True)
    )
    inner = total[16:17, :] + jnp.sum(grad_logits * stat[16:32, :], axis=0, keepdims=True)
    grad_second = returned + exact(router[...].astype(F32), grad_logits, 0, 0)
    grad_mixed = wide_cot[mine, :].astype(F32) + scale * (
        gain * grad_second - normal * (inner * (1.0 / D))
    )
    grad_att = grad_mixed.astype(BF16)
    for s, n in zip((2, 1, 3), to_y):
        send.arrived(n, from_y_small.at[s - 1])
        moe_out = moe_out + from_y_small[s - 1].astype(F32)
    both[me.tp, 0:SHARE, :] = grad_att
    both[me.tp, SHARE:, :] = (mixed[...] + moe_out).astype(BF16)
    end_gather = start_gather_shares(me, send, both)
    small_out[0:16, :] = exact(grad_logits, second[...].astype(F32), 1, 1)
    small_out[16:24, :] = row_sums(grad_second * normal)
    small_out[24:32, :] = row_sums(grad_att.astype(F32))
    grad_logits_out[...] = grad_logits
    end_gather()
    for q in range(BLOCKS):
        width = min(SHARE, D - q * SHARE)
        grad_att_out[q * SHARE : q * SHARE + width, :] = both[q, 0:width, :]
        layer_out[q * SHARE : q * SHARE + width, :] = both[q, SHARE : SHARE + width, :]
    for j in (1, 2, 3):
        all_heads.landed(j)
    for j in range(4):
        all_normed.complete(j)
    rows_copy.wait()
    cots_copy.wait()
    send.finish()


def experts(*operands):
    return pl.pallas_call(
        expert_kernel,
        out_shape=(
            shape((8, SLOTS, SHARE), BF16),
            shape((8, SLOTS, SHARE), BF16),
            shape((SLOTS, FF_LOCAL), BF16),
            shape((SLOTS, FF_LOCAL), BF16),
            shape((SLOTS, FF_LOCAL), BF16),
            shape((SLOTS, 128), BF16),
            shape((D, ROWS), BF16),
            shape((D, ROWS), BF16),
            shape((32, SHARE), F32),
            shape((16, 128), F32),
            shape((16, D, ROWS), BF16),
            shape((16, 512, ROWS), BF16),
        ),
        in_specs=vmem(5) + hbm(3) + vmem(6),
        out_specs=tuple(hbm(2) + vmem(8) + hbm(2)),
        scratch_shapes=[
            pltpu.VMEM((8, SLOTS, SHARE), BF16),
            pltpu.VMEM((8, SLOTS, SHARE), BF16),
            pltpu.VMEM((3, FF_LOCAL, WIDE), BF16),
            pltpu.VMEM((WIDE, ROWS), BF16),
            pltpu.VMEM((8, WIDE), F32),
            pltpu.VMEM((SLOTS, SHARE), BF16),
            pltpu.VMEM((SLOTS, SHARE), BF16),
            pltpu.VMEM((EXPERTS, 8, 128), F32),
            pltpu.VMEM((EXPERTS, 8, 128), F32),
            pltpu.VMEM((SLOTS, FF_LOCAL), F32),
            pltpu.VMEM((SLOTS, FF_LOCAL), F32),
            pltpu.VMEM((SLOTS, FF_LOCAL), BF16),
            pltpu.VMEM((2, 4, SLOTS, SHARE), BF16),
            pltpu.VMEM((2, 4, SLOTS, SHARE), BF16),
            pltpu.VMEM((2, 4, SLOTS, SHARE), BF16),
            pltpu.VMEM((2, 4, SLOTS, SHARE), BF16),
            pltpu.VMEM((4, SLOTS, SHARE), BF16),
            pltpu.VMEM((3, SLOTS, SHARE), BF16),
            pltpu.VMEM((SLOTS, SHARE), BF16),
            pltpu.VMEM((3, SHARE, ROWS), BF16),
            pltpu.VMEM((3, SHARE, ROWS), BF16),
            pltpu.VMEM((24, 128), F32),
            pltpu.VMEM((7, 24, 128), F32),
            pltpu.VMEM((8, 2 * SHARE, ROWS), BF16),
            *semaphores(300),
            pltpu.SemaphoreType.DMA((7,)),
        ],
        compiler_params=params(2, 60),
        name="experts",
    )(*operands)


def expert_grads_kernel(rows, cots, scaled, grad_gate, grad_up, gate_cols, gateup, down, bias):
    gateup[0] = contract_rows(grad_gate[...], rows[0])
    gateup[1] = contract_rows(grad_up[...], rows[0])
    down[...] = contract_rows(scaled[...], cots[0])
    bias[0] = contract_rows(gate_cols[...], cots[0])[0:8]


def expert_grads(rows, cots, scaled, grad_gate, grad_up, gate_cols):
    whole = pl.BlockSpec((SLOTS, FF_LOCAL), lambda p: (0, 0))
    block = pl.BlockSpec((1, SLOTS, SHARE), lambda p: (p, 0, 0))
    return pl.pallas_call(
        expert_grads_kernel,
        grid=(BLOCKS,),
        out_shape=(
            shape((2, FF_LOCAL, D), F32),
            shape((FF_LOCAL, D), F32),
            shape((BLOCKS, 8, SHARE), F32),
        ),
        in_specs=[block, block, whole, whole, whole, pl.BlockSpec((SLOTS, 128), lambda p: (0, 0))],
        out_specs=(
            pl.BlockSpec((2, FF_LOCAL, SHARE), lambda p: (0, 0, p)),
            pl.BlockSpec((FF_LOCAL, SHARE), lambda p: (0, p)),
            pl.BlockSpec((1, 8, SHARE), lambda p: (p, 0, 0)),
        ),
        compiler_params=pltpu.CompilerParams(vmem_limit_bytes=40 * 2**20),
        cost_estimate=pl.CostEstimate(
            flops=6 * SLOTS * D * FF_LOCAL, bytes_accessed=22_000_000, transcendentals=0
        ),
        name="expert_grads",
    )(rows, cots, scaled, grad_gate, grad_up, gate_cols)


def back_kernel(
    grad_att, queries, keys_values, log_total, sinks, allowed, trig, output_weight, query_weight,
    key_weight, value_weight, tokens, first_scale, vectors, small, grad_logits, normed_all, heads_all,
    output_grad, query_grad, key_value_grad, tokens_out, small_all, small_own,
    N, H, G, Q, output_sum, query_sum, padded, vecs, wide_att, part, from_sibling, sums, from_y, stat, stats, blocks,
    line, lines_in, lines_all, send_sems, recv_sems, local_sems,
):
    me = Place()
    send = Sender(me, send_sems, recv_sems)
    all_here = me.greet(True, True)
    loads = [
        pltpu.make_async_copy(heads_all, H, local_sems.at[0]),
        pltpu.make_async_copy(normed_all, N, local_sems.at[1]),
    ]
    for load in loads:
        load.start()
    G[0] = grad_att[...]
    all_here()
    all_att = GroupGather(me, send, G, D, True)
    all_att.begin()

    head_rows = contract_rows(grad_att[...], output_weight[...])
    both = keys_values[...].astype(F32)
    row_pair = jnp.transpose(both).astype(BF16)
    key_rows, value_rows = row_pair[:, 0:64], row_pair[:, 64:128]
    included = allowed[...] > 0.5
    grad_keys = jnp.zeros((64, ROWS), F32)
    grad_values = jnp.zeros((64, ROWS), F32)
    sink_line = jnp.zeros((1, 128), F32)
    place = lax.broadcasted_iota(jnp.int32, (1, 128), 1)
    factor = HEAD_SIZE**-0.5
    for h in range(HEADS):
        if h % 2 == 0:
            pair = jnp.transpose(head_rows[:, h * 64 : h * 64 + 128]).astype(BF16)
        grad_head = pair[0:64] if h % 2 == 0 else pair[64:128]
        query = queries[h * 64 : h * 64 + 64, :]
        scores = jnp.where(included, product(key_rows, query) * factor, NEGATIVE)
        logs = log_total[h : h + 1, :]
        probs = jnp.exp(scores - logs)
        grad_probs = product(value_rows, grad_head)
        delta = jnp.sum(probs * grad_probs, axis=0, keepdims=True)
        grad_scores = (probs * (grad_probs - delta)).astype(BF16)
        sunk = -jnp.sum(jnp.exp(sinks[h : h + 1, :] - logs) * delta, axis=1, keepdims=True)
        sink_line = jnp.where(place == h, sunk, sink_line)
        grad_values = grad_values + against_rows(grad_head, probs.astype(BF16))
        grad_keys = grad_keys + against_rows(query, grad_scores)
        grad_query = product(keys_values[0:64, :], grad_scores) * factor
        Q[0, h * 64 : h * 64 + 64, :] = rotate(grad_query, trig, True).astype(BF16)
    Q[0, 512:576, :] = rotate(grad_keys * factor, trig, True).astype(BF16)
    Q[0, 576:640, :] = grad_values.astype(BF16)
    all_heads = GroupGather(me, send, Q, 640, False)
    all_heads.begin()
    all_att.spread()
    all_att.pass_on(0)

    def grad(lo, width):
        return (
            product(query_weight[lo : lo + width, :], Q[0, 0:512, :])
            + contract_rows(key_weight[:, lo : lo + width], Q[0, 512:576, :])
            + contract_rows(value_weight[:, lo : lo + width], Q[0, 576:640, :])
        )

    def emit(q, block):
        part[q] = block.astype(BF16)

    share_blocks(grad, emit)
    vecs[:, 0:D] = vectors[...]
    vecs[:, D:] = jnp.zeros((8, WIDE - D), F32)
    padded[0:D, :] = tokens[...]
    padded[D:, :] = jnp.zeros((WIDE - D, ROWS), BF16)
    wide_att[0:D, :] = grad_att[...]
    wide_att[D:, :] = jnp.zeros((WIDE - D, ROWS), BF16)
    mine = pl.ds(pl.multiple_of(me.tp * SHARE, SHARE), SHARE)
    gain = column_share(vecs[:, mine][2:3])
    scale = first_scale[0:1, :]
    normal = padded[mine, :].astype(F32) * scale
    grad_normed = reduce_shares(me, send, part, from_sibling, sums, from_y)
    all_heads.spread()
    raised = gain * grad_normed
    stat[...] = jnp.broadcast_to(jnp.sum(raised * normal, axis=0, keepdims=True), (8, ROWS))
    total = exchange(me, send, stat, stats)
    grad_tokens = wide_att[mine, :].astype(F32) + scale * (
        raised - normal * (total[0:1, :] * (1.0 / D))
    )
    blocks[me.tp] = grad_tokens.astype(BF16)
    end_gather = start_gather_shares(me, send, blocks)

    turn = turned(me)
    line[0:16, :] = exact(turn, small[0:16, :], 0, 0)
    line[16:17, :] = small[16:17, :]
    line[17:18, :] = small[24:25, :]
    line[18:19, :] = row_sums(grad_normed * normal)[0:1]
    spare = jnp.zeros((1, SHARE - 128), F32)
    router_bias = row_sums(exact(turn, grad_logits[...], 0, 0))[0:1]
    line[19:20, :] = jnp.concatenate([router_bias, jnp.zeros((1, SHARE - 16), F32)], axis=1)
    line[20:21, :] = jnp.concatenate([sink_line, spare], axis=1)
    head_sums = row_sums(Q[0].astype(F32))
    line[21:22, :] = head_sums[0:1, 0:SHARE]
    line[22:23, :] = jnp.concatenate(
        [head_sums[0:1, SHARE:640], jnp.zeros((1, 2 * SHARE - 640), F32)], axis=1
    )
    line[23:24, :] = jnp.zeros((1, SHARE), F32)
    tickets = [
        send.start(line, lines_in.at[k - 1], me.along_ep(k)) for k in range(1, EXPERTS)
    ]
    end_gather()
    tokens_out[...] = blocks[...]
    summed = line[...]
    for k, n in enumerate(tickets):
        send.arrived(n, lines_in.at[k])
        summed = summed + lines_in[k]
    lines_all[me.tp] = summed
    small_own[...] = summed
    end_lines = start_gather_shares(me, send, lines_all)

    for load in loads:
        load.wait()

    def slots(j, part):
        return [4 * j + i if part == 0 else 4 * i + j for i in range(4)]

    def att_step(j):
        for part in (0, 1):
            right = jnp.concatenate([H[k] for k in slots(j, part)], axis=1)

            @pl.loop(0, 2)
            def _(core):
                span = pl.ds(pl.multiple_of(core * 1440 + part * 720, 16), 720)
                left = jnp.concatenate([G[k, span, :] for k in slots(j, part)], axis=1)
                value = against_rows(left, right)
                if j:
                    value = value + output_sum[span, :]
                output_sum[span, :] = value

    def head_step(j):
        for part in (0, 1):
            half = slice(part * 320, part * 320 + 320)
            right = jnp.concatenate([Q[k, half, :] for k in slots(j, part)], axis=1)

            @pl.loop(0, 4)
            def _(r):
                span = pl.ds(pl.multiple_of(r * 720, 16), 720)
                left = jnp.concatenate([N[k, span, :] for k in slots(j, part)], axis=1)
                value = against_rows(left, right)
                if j:
                    value = value + query_sum[part, span, :]
                query_sum[part, span, :] = value

    for j in range(4):
        if j:
            all_att.landed(j)
            all_att.pass_on(j)
        all_att.complete(j)
        att_step(j)
        if j == 0:
            end_lines()
            small_all[...] = lines_all[...]
    output_grad[...] = output_sum[...].astype(BF16)
    for j in range(4):
        all_heads.landed(j)
        head_step(j)
    query_grad[...] = jnp.concatenate(
        [query_sum[0], query_sum[1, :, 0:192]], axis=1
    ).astype(BF16)
    key_value_grad[...] = query_sum[1, :, 192:320].astype(BF16)
    send.finish()


def back(*operands):
    return pl.pallas_call(
        back_kernel,
        out_shape=(
            shape((D, 512), BF16),
            shape((D, 512), BF16),
            shape((D, 128), BF16),
            shape((8, SHARE, ROWS), BF16),
            shape((8, 24, SHARE), F32),
            shape((24, SHARE), F32),
        ),
        in_specs=vmem(16) + hbm(2),
        out_specs=tuple(vmem(6)),
        scratch_shapes=[
            pltpu.VMEM((16, D, ROWS), BF16),
            pltpu.VMEM((16, 512, ROWS), BF16),
            pltpu.VMEM((16, D, ROWS), BF16),
            pltpu.VMEM((16, 640, ROWS), BF16),
            pltpu.VMEM((D, 512), F32),
            pltpu.VMEM((2, D, 320), F32),
            pltpu.VMEM((WIDE, ROWS), BF16),
            pltpu.VMEM((8, WIDE), F32),
            pltpu.VMEM((WIDE, ROWS), BF16),
            pltpu.VMEM((8, SHARE, ROWS), BF16),
            pltpu.VMEM((4, SHARE, ROWS), BF16),
            pltpu.VMEM((3, SHARE, ROWS), BF16),
            pltpu.VMEM((3, SHARE, ROWS), BF16),
            pltpu.VMEM((8, ROWS), F32),
            pltpu.VMEM((7, 8, ROWS), F32),
            pltpu.VMEM((8, SHARE, ROWS), BF16),
            pltpu.VMEM((24, SHARE), F32),
            pltpu.VMEM((15, 24, SHARE), F32),
            pltpu.VMEM((8, 24, SHARE), F32),
            *semaphores(160),
            pltpu.SemaphoreType.DMA((2,)),
        ],
        compiler_params=params(3, 63),
        name="back",
    )(*operands)


def layout(lengths_row):
    row_index = jnp.arange(ROWS, dtype=jnp.int32)
    first_end = lengths_row[0]
    second_end = lengths_row[0] + lengths_row[1]
    document = (row_index >= first_end).astype(jnp.int32) + (row_index >= second_end).astype(
        jnp.int32
    )
    doc_start = jnp.where(document == 0, 0, jnp.where(document == 1, first_end, second_end))
    return (row_index - doc_start, document)


def shards(
    tokens,
    seq_lengths,
    expert_ids,
    first_gain,
    query_weight,
    key_matrix,
    value_matrix,
    query_bias,
    key_offset_bias,
    value_offset_bias,
    head_sink_logits,
    output_weight,
    output_bias,
    second_gain,
    router_weight,
    router_bias,
    expert_gateup,
    gateup_bias,
    expert_down,
    down_bias,
    cotangent,
):
    tp_place = lax.axis_index("tp")
    ep_place = lax.axis_index("ep")
    lengths_row = lax.dynamic_index_in_dim(seq_lengths, ep_place, 0, keepdims=False)
    positions, document = layout(lengths_row)
    exponent = jnp.arange(HEAD_SIZE // 2, dtype=F32) * (2.0 / HEAD_SIZE)
    angles = jnp.power(THETA, -exponent)[:, None] * positions.astype(F32)[None, :]
    trig = jnp.concatenate([jnp.cos(angles), jnp.sin(angles)], axis=0)
    row_index = jnp.arange(ROWS)
    allowed = (
        (document[:, None] == document[None, :]) & (row_index[:, None] <= row_index[None, :])
    ).astype(F32)
    vectors = jnp.concatenate(
        [output_bias[None], second_gain[None], first_gain[None], jnp.zeros((5, D), F32)]
    )
    biases = jnp.broadcast_to(
        jnp.concatenate([query_bias, key_offset_bias, value_offset_bias])[None], (8, 640)
    )
    sinks = jnp.broadcast_to(head_sink_logits[:, None], (HEADS, 128))
    router_biases = jnp.broadcast_to(router_bias[:, None], (EXPERTS, 128))
    gateup_t = jnp.swapaxes(expert_gateup[0], 1, 2)
    down = expert_down[0]
    tails = jnp.pad(
        jnp.concatenate([gateup_t[:, :, 2816:], down[None, :, 2816:]]),
        ((0, 0), (0, 0), (0, WIDE - D)),
    )
    first_slice = jnp.where(tp_place == 0, 1.0, 0.0).astype(F32)
    down_bias_blocks = jnp.pad(first_slice * down_bias[0], (0, WIDE - D)).reshape(BLOCKS, SHARE)
    gateup_bias_local = jnp.pad(gateup_bias[0], ((0, 6), (0, 0)))
    (
        second, mixed, stat, selector, normed, queries, keys_values, heads, log_total, first_scale, router,
    ) = front(
        tokens.T, query_weight, key_matrix.T, value_matrix.T, output_weight.T, router_weight.T,
        vectors, biases, sinks, router_biases, expert_ids.T, trig, allowed,
    )
    (
        expert_rows, cot_rows, scaled_hidden, grad_gate, grad_up, gate_cols,
        grad_att, layer, small, grad_logits, normed_all, heads_all,
    ) = experts(
        second, mixed, stat, selector, cotangent.T, gateup_t, down, tails, gateup_bias_local,
        down_bias_blocks, router, vectors, normed, heads,
    )
    output_grad, query_grad, key_value_grad, token_blocks, small_all, small_own = back(
        grad_att, queries, keys_values, log_total, sinks, allowed, trig, output_weight.T, query_weight,
        key_matrix.T, value_matrix.T, tokens.T, first_scale, vectors, small, grad_logits,
        normed_all, heads_all,
    )
    grad_gateup, grad_down, grad_down_bias = expert_grads(
        expert_rows, cot_rows, scaled_hidden, grad_gate, grad_up, gate_cols
    )
    grad_gateup_bias = jnp.stack(
        [jnp.sum(grad_gate.astype(F32), axis=0), jnp.sum(grad_up.astype(F32), axis=0)]
    )[None]
    grad_down_bias = (grad_down_bias[:, 0] + grad_down_bias[:, 1]).reshape(1, WIDE)[:, :D]
    grad_tokens = token_blocks.reshape(WIDE, ROWS)[:D].astype(F32).T
    across = small_all.transpose(1, 0, 2).reshape(24, WIDE)[:, :D]
    head_sums = small_own[21:23].reshape(2 * SHARE)
    return (
        layer.T,
        grad_tokens,
        across[18],
        query_grad.astype(F32),
        key_value_grad[:, 0:64].astype(F32),
        key_value_grad[:, 64:128].astype(F32),
        head_sums[0:512],
        head_sums[512:576],
        head_sums[576:640],
        small_own[20, 0:HEADS],
        output_grad.astype(F32).T,
        across[17],
        across[16],
        across[:16].T,
        small_own[19, 0:EXPERTS],
        jnp.swapaxes(grad_gateup, 1, 2)[None],
        grad_gateup_bias,
        grad_down[None],
        grad_down_bias,
    )


def solution(mesh):
    in_specs = (
        P("ep", None),
        P(),
        P("ep", None),
        P(),
        P(None, "tp"),
        P(None, "tp"),
        P(None, "tp"),
        P("tp"),
        P("tp"),
        P("tp"),
        P("tp"),
        P("tp", None),
        P(),
        P(),
        P(),
        P(),
        P("ep", None, None, "tp"),
        P("ep", None, "tp"),
        P("ep", "tp", None),
        P("ep", None),
        P("ep", None),
    )
    out_specs = (
        P("ep", None),
        P("ep", None),
        P(),
        P(None, "tp"),
        P(None, "tp"),
        P(None, "tp"),
        P("tp"),
        P("tp"),
        P("tp"),
        P("tp"),
        P("tp", None),
        P(),
        P(),
        P(),
        P(),
        P("ep", None, None, "tp"),
        P("ep", None, "tp"),
        P("ep", "tp", None),
        P("ep", None),
    )
    return jax.shard_map(shards, mesh=mesh, in_specs=in_specs, out_specs=out_specs, check_vma=False)
```

```python
import math

import jax
import jax.numpy as jnp
from jax import lax
from jax.experimental import pallas as pl
from jax.experimental.pallas import tpu as pltpu
from jax.sharding import PartitionSpec as P

HEAD_SIZE = 64
EPS = 1e-05
THETA = 150000.0
LIMIT = 7.0
ALPHA = 1.702
NEGATIVE = -1e30

D = 2880
FF_LOCAL = 360
SHARE = 384
BLOCKS = 8
WIDE = SHARE * BLOCKS
ROWS = 128
EXPERTS = 16
CAP = 48
SLOTS = EXPERTS * CAP
HALF = SLOTS // 2
HEADS = 8
QUARTER = SLOTS // 4
MESH = pl.DeviceIdType.MESH
F32 = jnp.float32
BF16 = jnp.bfloat16
HIGHEST = lax.Precision.HIGHEST


def product(left, right):
    return jnp.dot(left, right, preferred_element_type=F32)


def contract_rows(left, right):
    return lax.dot_general(left, right, (((0,), (0,)), ((), ())), preferred_element_type=F32)


def against_rows(left, right):
    return lax.dot_general(left, right, (((1,), (1,)), ((), ())), preferred_element_type=F32)


def exact(left, right, left_dim=1, right_dim=0):
    return lax.dot_general(
        left,
        right,
        (((left_dim,), (right_dim,)), ((), ())),
        preferred_element_type=F32,
        precision=HIGHEST,
    )


def row_sums(columns):
    return exact(jnp.ones((8, columns.shape[1]), F32), columns, 1, 1)


class Place:
    def __init__(self):
        self.ep = lax.axis_index("ep")
        self.tp = lax.axis_index("tp")
        self.z, self.x = self.ep // 4, self.ep % 4
        self.y, self.core = self.tp // 2, self.tp % 2

    def sibling(self):
        return (self.ep, self.y * 2 + (1 - self.core))

    def along_y(self, step):
        return (self.ep, lax.rem(self.y + step, 4) * 2 + self.core)

    def along_tp(self, step):
        return (self.ep, lax.rem(self.tp + step, 8))

    def along_ep(self, k):
        z = lax.rem(self.z + k // 4, 4)
        x = lax.rem(self.x + k % 4, 4)
        return (z * 4 + x, self.tp)

    def back_ep(self, k):
        z = lax.rem(self.z + 4 - k // 4, 4)
        x = lax.rem(self.x + 4 - k % 4, 4)
        return (z * 4 + x, self.tp)

    def greet(self, tp, ep):
        barrier = pltpu.get_barrier_semaphore()
        partners = [self.along_tp(i) for i in range(1, 8) if tp]
        partners += [self.along_ep(k) for k in range(1, 16) if ep]
        for device in partners:
            pl.semaphore_signal(barrier, inc=1, device_id=device, device_id_type=MESH)
        return lambda: pl.semaphore_wait(barrier, len(partners))


class Sender:
    def __init__(self, me, send_sems, recv_sems):
        self.me, self.send_sems, self.recv_sems = me, send_sems, recv_sems
        self.used = 0
        self.open = []

    def start(self, source, target, device):
        n = self.used
        self.used += 1
        copy = pltpu.make_async_remote_copy(
            src_ref=source,
            dst_ref=target,
            send_sem=self.send_sems.at[n],
            recv_sem=self.recv_sems.at[n],
            device_id=device,
            device_id_type=MESH,
        )
        copy.start()
        self.open.append(copy)
        return n

    def arrived(self, n, target):
        pltpu.make_async_remote_copy(
            src_ref=target,
            dst_ref=target,
            send_sem=self.send_sems.at[n],
            recv_sem=self.recv_sems.at[n],
            device_id=self.me.sibling(),
            device_id_type=MESH,
        ).wait_recv()

    def finish(self):
        for copy in self.open:
            copy.wait_send()
        self.open = []


class GroupGather:
    def __init__(self, me, send, buffer, lines, shared):
        self.me, self.send, self.buffer, self.shared = me, send, buffer, shared
        self.size = lines // (4 if shared else 2)
        self.cut = self.size // 32 * 16
        self.tickets, self.passed = {}, {}

    def span(self, part, core, piece=None):
        start = part * self.size
        if self.shared:
            start = core * (2 * self.size) + start
        size = self.size
        if piece == 0:
            size = self.cut
        if piece == 1:
            start, size = start + self.cut, size - self.cut
        return pl.ds(pl.multiple_of(start, 16), size)

    def groups(self, part, phase, j):
        unit = 1 if (part + phase) % 2 == 0 else 4
        if phase == 0:
            return [j * unit]
        if part == 0:
            return [slice(4 * j, 4 * j + 4)]
        return [4 * i + j for i in range(4)]

    def move(self, name, part, phase, source, target, piece=None):
        unit = 1 if (part + phase) % 2 == 0 else 4
        span = self.span(part, self.me.core, piece)
        step = (target - source) % 4
        self.tickets[name, part, phase] = [
            self.send.start(
                self.buffer.at[a, span], self.buffer.at[b, span], self.me.along_ep(unit * step)
            )
            for a, b in zip(self.groups(part, phase, source), self.groups(part, phase, target))
        ]

    def wait(self, name, part, phase, j, piece=None):
        span = self.span(part, self.me.core, piece)
        for n, slots in zip(self.tickets[name, part, phase], self.groups(part, phase, j)):
            self.send.arrived(n, self.buffer.at[slots, span])

    def begin(self, phase=0):
        for part in (0, 1):
            self.move("right", part, phase, 0, 1)
            self.move("left", part, phase, 0, 3)

    def relay(self, phase=0):
        for part in (0, 1):
            self.wait("right", part, phase, 1)
            self.move("far right", part, phase, 1, 2, 0)
            self.wait("left", part, phase, 3)
            self.move("far left", part, phase, 3, 2, 1)

    def meet(self, phase=0):
        for part in (0, 1):
            self.wait("far right", part, phase, 2, 0)
            self.wait("far left", part, phase, 2, 1)

    def shares(self, j):
        low = 1 if j == 0 else 0
        return [(0, slice(4 * j + low, 4 * j + 4))] + [(1, 4 * i + j) for i in range(low, 4)]

    def pass_on(self, j):
        self.passed[j] = []
        for part, slots in self.shares(j):
            block = self.buffer.at[slots, self.span(part, self.me.core)]
            self.passed[j].append(self.send.start(block, block, self.me.sibling()))

    def complete(self, j):
        for n, (part, slots) in zip(self.passed[j], self.shares(j)):
            self.send.arrived(n, self.buffer.at[slots, self.span(part, 1 - self.me.core)])


def column_of(row):
    return jnp.transpose(jnp.broadcast_to(row, (128, 128)))


def column_share(settings, first, me):
    return jnp.concatenate(
        [column_of(settings[pl.ds(first + me.tp * 3 + j, 1), :]) for j in range(3)], axis=0
    )


def share_blocks(part, emit):
    for q in range(BLOCKS):
        lo = q * SHARE
        width = min(SHARE, D - lo)
        block = part(lo, width)
        if width < SHARE:
            block = jnp.concatenate(
                [block, jnp.zeros((SHARE - width, block.shape[1]), block.dtype)], axis=0
            )
        emit(q, block)


def reduce_shares(me, send, part, from_sibling, sums, from_y):
    order = (2, 1, 3, 0)
    ticket = []
    for i, step in enumerate(order):
        y = lax.rem(me.y + step, 4)
        ticket.append(
            send.start(part.at[y * 2 + 1 - me.core], from_sibling.at[i], me.sibling())
        )
    landed = []
    for i, step in enumerate(order):
        y = lax.rem(me.y + step, 4)
        send.arrived(ticket[i], from_sibling.at[i])
        total = part[y * 2 + me.core].astype(F32) + from_sibling[i].astype(F32)
        if step:
            sums[i] = total.astype(BF16)
            landed.append(send.start(sums.at[i], from_y.at[i], me.along_y(step)))
    for i, n in enumerate(landed):
        send.arrived(n, from_y.at[i])
        total = total + from_y[i].astype(F32)
    return total


def exchange(me, send, own, others):
    tickets = [send.start(own, others.at[i - 1], me.along_tp(i)) for i in range(1, 8)]
    total = own[...]
    for i, n in enumerate(tickets):
        send.arrived(n, others.at[i])
        total = total + others[i]
    return total


def start_gather_shares(me, send, blocks):
    own = blocks.at[me.tp]
    to_y = [send.start(own, own, me.along_y(step)) for step in (2, 1, 3)]
    to_sibling = [send.start(own, own, me.sibling())]

    def end():
        for n, step in zip(to_y, (2, 1, 3)):
            block = blocks.at[lax.rem(me.y + 4 - step, 4) * 2 + me.core]
            send.arrived(n, block)
            to_sibling.append(send.start(block, block, me.sibling()))
        for n, step in zip(to_sibling, (0, 2, 1, 3)):
            send.arrived(n, blocks.at[lax.rem(me.y + 4 - step, 4) * 2 + 1 - me.core])

    return end


def vmem(count):
    return [pl.BlockSpec(memory_space=pltpu.VMEM)] * count


def hbm(count):
    return [pl.BlockSpec(memory_space=pl.ANY)] * count


def semaphores(count):
    return [pltpu.SemaphoreType.DMA((count,)), pltpu.SemaphoreType.DMA((count,))]


def params(number, megabytes):
    return pltpu.CompilerParams(
        collective_id=number, has_side_effects=True, vmem_limit_bytes=megabytes * 2**20
    )


shape = jax.ShapeDtypeStruct


OUTPUT_BIAS, SECOND_GAIN, FIRST_GAIN, HEAD_BIASES, ROUTER_BIAS, SINKS = 0, 24, 48, 72, 77, 78


def turned(me):
    k = lax.broadcasted_iota(jnp.int32, (EXPERTS, EXPERTS), 0)
    e = lax.broadcasted_iota(jnp.int32, (EXPERTS, EXPERTS), 1)
    name = ((me.z + (k >> 2)) & 3) * 4 + ((me.x + (k & 3)) & 3)
    return (name == e).astype(F32)


def rotate(pair, trig, back=False):
    first, last = pair[0:32], pair[32:64]
    cosine, sine = trig[0:32, :], trig[32:64, :]
    if back:
        sine = -sine
    return jnp.concatenate([first * cosine - last * sine, last * cosine + first * sine], axis=0)


def documents(index, first_end, second_end):
    return (index >= first_end).astype(jnp.int32) + (index >= second_end).astype(jnp.int32)


def activation_parts(gate_pre, up_pre):
    lowered = LIMIT - gate_pre
    cap = jnp.maximum(lowered, 0.0) + jnp.log(1.0 + jnp.exp(-jnp.abs(lowered)))
    capped_gate = LIMIT - cap
    tanh = jnp.tanh(up_pre * (1.0 / LIMIT))
    capped_up = LIMIT * tanh
    sigmoid = 1.0 / (1.0 + jnp.exp(-ALPHA * capped_gate))
    return lowered, capped_gate, tanh, capped_up, sigmoid


def layer_kernel(
    lengths, ids, settings, gateup_bias, down_bias,
    tokens, cotangent, query_weight, key_weight, value_weight, output_weight, router, gateup, down,
    queries, keys_values, log_total, first_scale, trig, allowed, scaled_out, grad_gate_out, grad_up_out,
    gate_cols_out, grad_att_out, layer_out, small_out, grad_logits_out,
    rows_out, cots_out, normed_all, heads_all,
    wide_tokens, wide_cot, wide_normed, wide_router, wq, wk, wv, wo, router_in, unpadded, weights, wide_bias,
    selector, heads, mixed, second, stat, part, part_sibling, part_sums, part_y, stat_own, stats,
    R, C, staged, staged_c, gates_send, gates, gate_pre, up_pre, hidden,
    to_sibling, from_sibling, sums, results, far_in, near_in, home, wire, from_y_small, blocks,
    send_sems, recv_sems, local_sems,
):
    me = Place()
    send = Sender(me, send_sems, recv_sems)
    all_here = me.greet(True, True)

    def load(source, target, n):
        copy = pltpu.make_async_copy(source, target, local_sems.at[n])
        copy.start()
        return copy

    load_cot = load(cotangent, wide_cot.at[0:D], 0)
    load_tokens = load(tokens, wide_tokens.at[0:D], 1)
    load_query = load(query_weight, wq, 2)
    load_pair = [load(key_weight, wk, 3), load(value_weight, wv, 4)]
    load_output = load(output_weight, wo, 5)
    load_router = load(router, router_in, 6)
    last = 2816
    load_experts = [
        load(gateup.at[:, :, 0:last], weights.at[0:2, :, 0:last], 7),
        load(down.at[:, 0:last], weights.at[2, :, 0:last], 8),
    ]
    load_tail = load(gateup.at[0], unpadded, 9)

    def keep_tail(n, copy):
        copy.wait()
        weights[n, :, last:] = jnp.concatenate(
            [unpadded[:, last:], jnp.zeros((FF_LOCAL, WIDE - D), BF16)], axis=1
        )

    mine = pl.ds(pl.multiple_of(me.tp * SHARE, SHARE), SHARE)
    for buffer in (wide_cot, wide_tokens):
        buffer[D:, :] = jnp.zeros((WIDE - D, ROWS), BF16)
    first_slice = jnp.where(me.tp == 0, 1.0, 0.0)
    wide_bias[:, 0:D] = down_bias[...] * first_slice
    wide_bias[:, D:] = jnp.zeros((1, WIDE - D), F32)

    k = lax.broadcasted_iota(jnp.int32, (EXPERTS, ROWS), 0)
    name = ((me.z + (k >> 2)) & 3) * 4 + ((me.x + (k & 3)) & 3)
    chosen = jnp.zeros((EXPERTS, ROWS), F32)
    for j in range(4):
        chosen = chosen + (name == ids[j : j + 1, :]).astype(F32)
    taken = chosen > 0.5
    column = lax.broadcasted_iota(jnp.int32, (ROWS, ROWS), 0)
    row = lax.broadcasted_iota(jnp.int32, (ROWS, ROWS), 1)
    rank = product(chosen.astype(BF16), (column < row).astype(F32).astype(BF16))
    rank = jnp.where(taken, rank, -1.0)
    place = lax.broadcasted_iota(jnp.int32, (CAP, ROWS), 0).astype(F32)
    for k in range(EXPERTS):
        selector[k * CAP : (k + 1) * CAP, :] = (
            (place == rank[k : k + 1, :]).astype(F32).astype(BF16)
        )
    load_cot.wait()
    staged_c[...] = against_rows(selector[...], wide_cot[mine, :]).astype(BF16)
    all_here()

    def scatter(source, target):
        tickets = [None]
        for k in range(1, EXPERTS):
            lines = pl.ds(k * CAP, CAP)
            tickets.append(
                send.start(source.at[lines], target.at[me.tp, lines], me.along_ep(k))
            )
        target[me.tp, 0:CAP, :] = source[0:CAP, :]
        return tickets

    def lines_at(j, piece=None):
        if piece is None:
            return pl.ds(j * QUARTER, QUARTER)
        return pl.ds(j * QUARTER + piece * (QUARTER // 2), QUARTER // 2)

    def back_y(buffer, step, lines, core):
        return buffer.at[lax.rem(me.y + 4 - step, 4) * 2 + core, lines]

    def spread(buffer, tickets, j):
        for k in range(4 * j, 4 * j + 4):
            if k:
                send.arrived(tickets[k], buffer.at[me.tp, pl.ds(k * CAP, CAP)])
        own = buffer.at[me.tp, lines_at(j)]
        return {
            1: send.start(own, own, me.along_y(1)),
            3: send.start(own, own, me.along_y(3)),
            "sibling": [send.start(own, own, me.sibling())],
        }

    def pass_on(buffer, tickets, j):
        for step, piece in ((1, 0), (3, 1)):
            block = back_y(buffer, step, lines_at(j), me.core)
            send.arrived(tickets[step], block)
            block_half = back_y(buffer, step, lines_at(j, piece), me.core)
            tickets[2, piece] = send.start(block_half, block_half, me.along_y(step))
            tickets["sibling"].append(send.start(block, block, me.sibling()))

    def pass_far(buffer, tickets, j):
        for piece in (0, 1):
            send.arrived(tickets[2, piece], back_y(buffer, 2, lines_at(j, piece), me.core))
        block = back_y(buffer, 2, lines_at(j), me.core)
        tickets["sibling"].append(send.start(block, block, me.sibling()))

    def complete(buffer, tickets, j):
        for n, step in zip(tickets["sibling"], (0, 1, 3, 2)):
            send.arrived(n, back_y(buffer, step, lines_at(j), 1 - me.core))

    cots_in = scatter(staged_c, C)

    load_tokens.wait()

    def squares(j, total):
        lines = wide_tokens[pl.ds(pl.multiple_of(j * 96, 96), 96), :].astype(F32)
        return total + jnp.sum(lines * lines, axis=0, keepdims=True)

    scale = lax.rsqrt(lax.fori_loop(0, 30, squares, jnp.zeros((1, ROWS), F32)) * (1.0 / D) + EPS)
    first_scale[...] = jnp.broadcast_to(scale, (8, ROWS))

    @pl.loop(0, 24)
    def _(j):
        span = pl.ds(pl.multiple_of(j * 128, 128), 128)
        gain = column_of(settings[pl.ds(FIRST_GAIN + j, 1), :])
        wide_normed[span, :] = (wide_tokens[span, :].astype(F32) * scale * gain).astype(BF16)

    keep_normed = load(wide_normed.at[0:D], normed_all.at[0], 10)
    first_end = lengths[me.ep, 0]
    second_end = first_end + lengths[me.ep, 1]
    index = lax.broadcasted_iota(jnp.int32, (1, ROWS), 1)
    document = documents(index, first_end, second_end)
    start = jnp.where(document == 0, 0, jnp.where(document == 1, first_end, second_end))
    positions = (index - start).astype(F32)
    exponent = lax.broadcasted_iota(jnp.int32, (32, ROWS), 0).astype(F32)
    angles = jnp.exp(exponent * (-math.log(THETA) / 32.0)) * positions
    trig[0:32, :] = jnp.cos(angles)
    trig[32:64, :] = jnp.sin(angles)
    included = (
        documents(column, first_end, second_end) == documents(row, first_end, second_end)
    ) & (column <= row)
    allowed[...] = included.astype(F32)
    load_query.wait()
    query_rows = contract_rows(wide_normed[0:D, :], wq[...])
    for copy in load_pair:
        copy.wait()
    both = jnp.concatenate(
        [product(wk[...], wide_normed[0:D, :]), product(wv[...], wide_normed[0:D, :])], axis=0
    ) + column_of(settings[HEAD_BIASES + 4 : HEAD_BIASES + 5, :])
    both = jnp.concatenate([rotate(both[0:64], trig), both[64:128]], axis=0)
    keys_values[...] = both.astype(BF16)
    key_rows = jnp.transpose(both)[:, 0:64].astype(BF16)
    for j in range(4):
        pair = jnp.transpose(query_rows[:, j * 128 : (j + 1) * 128]) + column_of(
            settings[HEAD_BIASES + j : HEAD_BIASES + j + 1, :]
        )
        queries[j * 128 : j * 128 + 64, :] = rotate(pair[0:64], trig).astype(BF16)
        queries[j * 128 + 64 : j * 128 + 128, :] = rotate(pair[64:128], trig).astype(BF16)
    b = [None] * 4
    b[0] = spread(C, cots_in, 0)
    b[1] = spread(C, cots_in, 1)
    keep_normed.wait()
    all_normed = GroupGather(me, send, normed_all, D, True)
    all_normed.begin()
    sinks = column_of(settings[SINKS : SINKS + 1, :])
    for h in range(HEADS):
        scores = product(key_rows, queries[h * 64 : h * 64 + 64, :]) * (HEAD_SIZE**-0.5)
        scores = jnp.where(included, scores, NEGATIVE)
        sink = sinks[h : h + 1, :]
        highest = jnp.maximum(jnp.max(scores, axis=0, keepdims=True), sink)
        total = jnp.exp(sink - highest) + jnp.sum(
            jnp.exp(scores - highest), axis=0, keepdims=True
        )
        logs = highest + jnp.log(total)
        log_total[h : h + 1, :] = logs
        probs = jnp.exp(scores - logs).astype(BF16)
        heads[h * 64 : h * 64 + 64, :] = product(keys_values[64:128, :], probs).astype(BF16)
    keep_heads = load(heads, heads_all.at[0], 11)
    load_output.wait()

    def emit(q, block):
        part[q] = block.astype(BF16)

    share_blocks(lambda lo, width: product(wo[lo : lo + width, :], heads[...]), emit)
    turn = turned(me)
    load_router.wait()
    wide_router[:, 0:D] = product(turn.astype(BF16), router_in[...]).astype(BF16)
    wide_router[:, D:] = jnp.zeros((EXPERTS, WIDE - D), BF16)
    router_share = wide_router[:, mine]
    base = wide_tokens[mine, :].astype(F32) + column_share(settings, OUTPUT_BIAS, me)
    gain = column_share(settings, SECOND_GAIN, me)
    mixed[...] = base + reduce_shares(me, send, part, part_sibling, part_sums, part_y)
    raised = mixed[...] * gain
    stat_own[0, 0:16, :] = product(router_share, raised.astype(BF16))
    stat_own[0, 16:24, :] = jnp.broadcast_to(
        jnp.sum(mixed[...] * mixed[...], axis=0, keepdims=True), (8, ROWS)
    )
    total = exchange(me, send, stat_own.at[0], stats.at[0:7])
    scale = lax.rsqrt(total[16:17, :] * (1.0 / D) + EPS)
    second[...] = (raised * scale).astype(BF16)
    staged[...] = against_rows(selector[...], second[...]).astype(BF16)
    rows_in = scatter(staged, R)
    plain = total[0:16, :] * scale
    logits = plain + exact(
        turn, column_of(settings[ROUTER_BIAS : ROUTER_BIAS + 1, :])[0:EXPERTS]
    )
    highest = jnp.max(jnp.where(taken, logits, NEGATIVE), axis=0, keepdims=True)
    lifted = jnp.where(taken, jnp.exp(jnp.where(taken, logits, highest) - highest), 0.0)
    stat[0:16, :] = lifted / jnp.sum(lifted, axis=0, keepdims=True)
    stat[16:32, :] = plain
    stat[32:40, :] = jnp.broadcast_to(scale, (8, ROWS))
    for k in range(EXPERTS):
        line = jnp.broadcast_to(stat[k : k + 1, :], (8, 128))
        picked = exact(line, selector[k * CAP : (k + 1) * CAP, :].astype(F32), 1, 1)
        gates_send[k] = jnp.concatenate([picked, jnp.zeros((8, 128 - CAP), F32)], axis=1)
    gates_in = [None]
    for k in range(1, EXPERTS):
        gates_in.append(send.start(gates_send.at[k], gates.at[k], me.along_ep(k)))
    gates[0] = gates_send[0]
    pass_on(C, b[0], 0)
    pass_on(C, b[1], 1)
    b[2] = spread(C, cots_in, 2)
    b[3] = spread(C, cots_in, 3)
    keep_tail(0, load_tail)
    load_tail = load(gateup.at[1], unpadded, 9)
    keep_heads.wait()
    all_heads = GroupGather(me, send, heads_all, 512, False)
    all_heads.begin()
    all_normed.relay()
    a = [None] * 4
    a[0] = spread(R, rows_in, 0)
    a[1] = spread(R, rows_in, 1)
    pass_far(C, b[0], 0)
    pass_far(C, b[1], 1)
    a[2] = spread(R, rows_in, 2)
    a[3] = spread(R, rows_in, 3)
    pass_on(C, b[2], 2)
    pass_on(C, b[3], 3)
    pass_on(R, a[0], 0)
    keep_tail(1, load_tail)
    load_tail = load(down, unpadded, 9)
    all_normed.meet()
    all_normed.begin(1)
    all_normed.pass_on(0)
    all_heads.relay()
    pass_on(R, a[1], 1)
    pass_far(R, a[0], 0)
    pass_on(R, a[2], 2)
    pass_far(R, a[1], 1)
    pass_far(C, b[2], 2)
    pass_far(C, b[3], 3)
    keep_tail(2, load_tail)
    for copy in load_experts:
        copy.wait()

    def lines_of(h):
        return pl.ds(h * HALF, HALF)

    def forward(h):
        lines = lines_of(h)
        gate_pre[lines, :] = jnp.broadcast_to(gateup_bias[0:1, :], (HALF, FF_LOCAL))
        up_pre[lines, :] = jnp.broadcast_to(gateup_bias[1:2, :], (HALF, FF_LOCAL))

        @pl.loop(0, 4)
        def _(y):
            block = jnp.concatenate([R[2 * y, lines, :], R[2 * y + 1, lines, :]], axis=1)
            span = pl.ds(pl.multiple_of(y * 2 * SHARE, 2 * SHARE), 2 * SHARE)
            gate_pre[lines, :] += against_rows(block, weights[0, :, span])
            up_pre[lines, :] += against_rows(block, weights[1, :, span])

        _, capped_gate, _, capped_up, sigmoid = activation_parts(
            gate_pre[lines, :], up_pre[lines, :]
        )
        hidden[lines, :] = ((capped_up + 1.0) * capped_gate * sigmoid).astype(BF16)

        def out_block(q):
            span = pl.ds(pl.multiple_of(q * SHARE, SHARE), SHARE)
            return product(hidden[lines, :], weights[2, :, span]) + wide_bias[:, span]

        sent = []
        for y in range(4):
            to_sibling[0, y, lines, :] = out_block(2 * y + 1 - me.core).astype(BF16)
            sent.append(
                send.start(
                    to_sibling.at[0, y, lines], from_sibling.at[0, y, lines], me.sibling()
                )
            )
        for y in range(4):
            sums[0, y, lines, :] = out_block(2 * y + me.core).astype(BF16)
        return sent

    def results_home(h, sent):
        lines = lines_of(h)
        for y in range(4):
            send.arrived(sent[y], from_sibling.at[0, y, lines])
            sums[0, y, lines, :] = (
                sums[0, y, lines, :].astype(F32) + from_sibling[0, y, lines, :].astype(F32)
            ).astype(BF16)
        tickets = []
        for k in range(8 * h, 8 * h + 8):
            span = pl.ds(k * CAP, CAP)
            if k:
                tickets.append(
                    send.start(sums.at[0, :, span], results.at[:, span], me.back_ep(k))
                )
            else:
                tickets.append(None)
                results[:, 0:CAP, :] = sums[0, :, 0:CAP, :]
        return tickets

    complete(R, a[0], 0)
    complete(R, a[1], 1)
    sent_0 = forward(0)
    pass_on(R, a[3], 3)
    pass_far(R, a[2], 2)
    for k in range(1, EXPERTS):
        send.arrived(gates_in[k], gates.at[k])
    gate_rows = jnp.concatenate(
        [gates[:, 0, :], jnp.zeros((128 - EXPERTS, 128), F32)], axis=0
    )
    gate_cols = jnp.transpose(gate_rows)

    def backward(h):
        lines = lines_of(h)
        gate = jnp.concatenate(
            [gate_cols[0:CAP, k : k + 1] for k in range(8 * h, 8 * h + 8)], axis=0
        )
        high = gate.astype(BF16)
        low = (gate - high.astype(F32)).astype(BF16)
        place = lax.broadcasted_iota(jnp.int32, (HALF, 128), 1)
        gate_cols_out[lines, :] = jnp.where(
            place == 0,
            high.astype(F32),
            jnp.where(place == 1, low.astype(F32), 0.0),
        ).astype(BF16)

        def step(y, total):
            block = jnp.concatenate([C[2 * y, lines, :], C[2 * y + 1, lines, :]], axis=1)
            span = pl.ds(pl.multiple_of(y * 2 * SHARE, 2 * SHARE), 2 * SHARE)
            return total + against_rows(block, weights[2, :, span])

        grad_hidden = gate * lax.fori_loop(0, 4, step, jnp.zeros((HALF, FF_LOCAL), F32))
        lowered, capped_gate, tanh, capped_up, sigmoid = activation_parts(
            gate_pre[lines, :], up_pre[lines, :]
        )
        scaled_out[lines, :] = (gate * hidden[lines, :].astype(F32)).astype(BF16)
        slope = (capped_up + 1.0) * (
            sigmoid + ALPHA * capped_gate * sigmoid * (1.0 - sigmoid)
        )
        grad_gate_out[lines, :] = (
            grad_hidden * slope * (1.0 / (1.0 + jnp.exp(-lowered)))
        ).astype(BF16)
        grad_up_out[lines, :] = (
            grad_hidden * capped_gate * sigmoid * (1.0 - tanh * tanh)
        ).astype(BF16)

        def back_block(q):
            span = pl.ds(pl.multiple_of(q * SHARE, SHARE), SHARE)
            return product(grad_gate_out[lines, :], weights[0, :, span]) + product(
                grad_up_out[lines, :], weights[1, :, span]
            )

        sent = []
        for s in (2, 1, 3, 0):
            y = lax.rem(me.y + s, 4)
            to_sibling[1, s, lines, :] = back_block(2 * y + 1 - me.core).astype(BF16)
            sent.append(
                send.start(
                    to_sibling.at[1, s, lines], from_sibling.at[1, s, lines], me.sibling()
                )
            )
        far = []
        for s, n in zip((2, 1, 3, 0), sent):
            y = lax.rem(me.y + s, 4)
            block = back_block(2 * y + me.core)
            send.arrived(n, from_sibling.at[1, s, lines])
            total = block + from_sibling[1, s, lines, :].astype(F32)
            sums[1, s, lines, :] = total.astype(BF16)
            if s == 2:
                for piece, step_y in ((0, 1), (1, 3)):
                    half = pl.ds(h * HALF + piece * QUARTER, QUARTER)
                    far.append(
                        send.start(
                            sums.at[1, 2, half], far_in.at[piece, h], me.along_y(step_y)
                        )
                    )
        return far

    def sums_on(h, far):
        lines = lines_of(h)
        near = []
        for piece, step_y in ((0, 1), (1, 3)):
            half = pl.ds(h * HALF + piece * QUARTER, QUARTER)
            send.arrived(far[piece], far_in.at[piece, h])
            sums[1, step_y, half, :] = (
                sums[1, step_y, half, :].astype(F32) + far_in[piece, h].astype(F32)
            ).astype(BF16)
            near.append(
                send.start(
                    sums.at[1, step_y, lines], near_in.at[piece, lines], me.along_y(step_y)
                )
            )
        return near

    def grads_home(h, near):
        lines = lines_of(h)
        total = sums[1, 0, lines, :].astype(F32)
        for piece in (0, 1):
            send.arrived(near[piece], near_in.at[piece, lines])
            total = total + near_in[piece, lines, :].astype(F32)
        sums[1, 0, lines, :] = total.astype(BF16)
        tickets = []
        for k in range(8 * h, 8 * h + 8):
            span = pl.ds(k * CAP, CAP)
            if k:
                tickets.append(
                    send.start(sums.at[1, 0, span], home.at[span], me.back_ep(k))
                )
            else:
                tickets.append(None)
                home[0:CAP, :] = sums[1, 0, 0:CAP, :]
        return tickets

    back = results_home(0, sent_0)
    pass_far(R, a[3], 3)
    for j in range(4):
        complete(C, b[j], j)
    cots_copy = load(C, cots_out, 12)
    far_0 = backward(0)
    near_0 = sums_on(0, far_0)
    complete(R, a[2], 2)
    complete(R, a[3], 3)
    rows_copy = load(R, rows_out, 13)
    sent_1 = forward(1)
    back = back + results_home(1, sent_1)
    far_1 = backward(1)
    near_1 = sums_on(1, far_1)
    home_in = grads_home(0, near_0)
    all_normed.relay(1)
    all_normed.pass_on(1)
    all_normed.pass_on(3)
    all_heads.meet()
    all_heads.begin(1)
    home_in = home_in + grads_home(1, near_1)

    spread_gates = jnp.concatenate(
        [jnp.broadcast_to(stat[k : k + 1, :], (CAP, 128)) for k in range(EXPERTS)], axis=0
    )
    weighted = selector[...].astype(F32) * spread_gates
    high = weighted.astype(BF16)
    low = (weighted - high.astype(F32)).astype(BF16)
    gain = column_share(settings, SECOND_GAIN, me)
    scale = stat[32:33, :]
    normal = mixed[...] * scale
    for k in range(1, EXPERTS):
        send.arrived(back[k], results.at[:, pl.ds(k * CAP, CAP)])
    pairs = jnp.zeros((SLOTS, ROWS), F32)
    to_y = []
    for s in (2, 1, 3, 0):
        q = lax.rem(me.y + s, 4) * 2 + me.core
        block = results[lax.rem(me.y + s, 4)]
        pairs = pairs + product(
            block, wide_cot[pl.ds(pl.multiple_of(q * SHARE, SHARE), SHARE), :]
        )
        total = contract_rows(block, high) + contract_rows(block, low)
        if s:
            wire[s - 1] = total.astype(BF16)
            to_y.append(send.start(wire.at[s - 1], from_y_small.at[s - 1], me.along_y(s)))
    moe_out = total
    pairs = pairs * selector[...].astype(F32)
    for k in range(EXPERTS):
        stat_own[1, k : k + 1, :] = jnp.sum(pairs[k * CAP : (k + 1) * CAP], axis=0, keepdims=True)
    for k in range(1, EXPERTS):
        send.arrived(home_in[k], home.at[pl.ds(k * CAP, CAP)])
    returned = contract_rows(home[...], selector[...])
    stat_own[1, 16:24, :] = jnp.broadcast_to(
        jnp.sum(returned * gain * normal, axis=0, keepdims=True), (8, ROWS)
    )
    all_normed.meet(1)
    all_normed.pass_on(2)
    total = exchange(me, send, stat_own.at[1], stats.at[7:14])
    gate_share = stat[0:16, :]
    grad_gates = total[0:16, :]
    grad_logits = gate_share * (
        grad_gates - jnp.sum(gate_share * grad_gates, axis=0, keepdims=True)
    )
    inner = total[16:17, :] + jnp.sum(grad_logits * stat[16:32, :], axis=0, keepdims=True)
    grad_second = returned + exact(wide_router[:, mine].astype(F32), grad_logits, 0, 0)
    grad_mixed = wide_cot[mine, :].astype(F32) + scale * (
        gain * grad_second - normal * (inner * (1.0 / D))
    )
    grad_att = grad_mixed.astype(BF16)
    blocks[me.tp] = grad_att
    end_gather = start_gather_shares(me, send, blocks)
    for s, n in zip((2, 1, 3), to_y):
        send.arrived(n, from_y_small.at[s - 1])
        moe_out = moe_out + from_y_small[s - 1].astype(F32)
    layer_out[...] = (mixed[...] + moe_out).astype(BF16)
    small_out[0:16, :] = exact(
        exact(turn, grad_logits, 0, 0), second[...].astype(F32), 1, 1
    )
    small_out[16:24, :] = row_sums(grad_second * normal)
    small_out[24:32, :] = row_sums(grad_att.astype(F32))
    grad_logits_out[...] = exact(turn, grad_logits, 0, 0)
    all_heads.relay(1)
    end_gather()
    for q in range(BLOCKS):
        width = min(SHARE, D - q * SHARE)
        grad_att_out[q * SHARE : q * SHARE + width, :] = blocks[q, 0:width, :]
    all_heads.meet(1)
    for j in range(4):
        all_normed.complete(j)
    rows_copy.wait()
    cots_copy.wait()
    send.finish()


def layer(*operands):
    bf = lambda *dims: pltpu.VMEM(dims, BF16)
    fl = lambda *dims: pltpu.VMEM(dims, F32)
    return pl.pallas_call(
        layer_kernel,
        out_shape=(
            shape((512, ROWS), BF16),
            shape((128, ROWS), BF16),
            shape((8, ROWS), F32),
            shape((8, ROWS), F32),
            shape((64, ROWS), F32),
            shape((ROWS, ROWS), F32),
            shape((SLOTS, FF_LOCAL), BF16),
            shape((SLOTS, FF_LOCAL), BF16),
            shape((SLOTS, FF_LOCAL), BF16),
            shape((SLOTS, 128), BF16),
            shape((D, ROWS), BF16),
            shape((SHARE, ROWS), BF16),
            shape((32, SHARE), F32),
            shape((16, 128), F32),
            shape((8, SLOTS, SHARE), BF16),
            shape((8, SLOTS, SHARE), BF16),
            shape((16, D, ROWS), BF16),
            shape((16, 512, ROWS), BF16),
        ),
        in_specs=[pl.BlockSpec(memory_space=pltpu.SMEM)] + vmem(4) + hbm(9),
        out_specs=tuple(vmem(14) + hbm(4)),
        scratch_shapes=[
            bf(WIDE, ROWS),
            bf(WIDE, ROWS),
            bf(WIDE, ROWS),
            bf(EXPERTS, WIDE),
            bf(D, 512),
            bf(64, D),
            bf(64, D),
            bf(D, 512),
            bf(EXPERTS, D),
            bf(FF_LOCAL, D),
            bf(3, FF_LOCAL, WIDE),
            fl(1, WIDE),
            bf(SLOTS, ROWS),
            bf(512, ROWS),
            fl(SHARE, ROWS),
            bf(SHARE, ROWS),
            fl(40, ROWS),
            bf(8, SHARE, ROWS),
            bf(4, SHARE, ROWS),
            bf(3, SHARE, ROWS),
            bf(3, SHARE, ROWS),
            fl(2, 24, ROWS),
            fl(14, 24, ROWS),
            bf(8, SLOTS, SHARE),
            bf(8, SLOTS, SHARE),
            bf(SLOTS, SHARE),
            bf(SLOTS, SHARE),
            fl(EXPERTS, 8, 128),
            fl(EXPERTS, 8, 128),
            fl(SLOTS, FF_LOCAL),
            fl(SLOTS, FF_LOCAL),
            bf(SLOTS, FF_LOCAL),
            bf(2, 4, SLOTS, SHARE),
            bf(2, 4, SLOTS, SHARE),
            bf(2, 4, SLOTS, SHARE),
            bf(4, SLOTS, SHARE),
            bf(2, 2, QUARTER, SHARE),
            bf(2, SLOTS, SHARE),
            bf(SLOTS, SHARE),
            bf(3, SHARE, ROWS),
            bf(3, SHARE, ROWS),
            bf(8, SHARE, ROWS),
            *semaphores(320),
            pltpu.SemaphoreType.DMA((14,)),
        ],
        compiler_params=params(1, 63),
        name="layer",
    )(*operands)


def expert_grads_kernel(rows, cots, scaled, grad_gate, grad_up, gate_cols, gateup, down, bias, gateup_bias):
    gateup[0] = contract_rows(grad_gate[...], rows[0])
    gateup[1] = contract_rows(grad_up[...], rows[0])
    down[...] = contract_rows(scaled[...], cots[0])
    both = contract_rows(gate_cols[...], cots[0])
    bias[...] = both[0:1] + both[1:2]
    gateup_bias[0:1, :] = jnp.sum(grad_gate[...].astype(F32), axis=0, keepdims=True)
    gateup_bias[1:2, :] = jnp.sum(grad_up[...].astype(F32), axis=0, keepdims=True)


def expert_grads(rows, cots, scaled, grad_gate, grad_up, gate_cols):
    whole = pl.BlockSpec((SLOTS, FF_LOCAL), lambda p: (0, 0))
    block = pl.BlockSpec((1, SLOTS, SHARE), lambda p: (p, 0, 0))
    return pl.pallas_call(
        expert_grads_kernel,
        grid=(BLOCKS,),
        out_shape=(
            shape((2, FF_LOCAL, D), F32),
            shape((FF_LOCAL, D), F32),
            shape((1, D), F32),
            shape((2, FF_LOCAL), F32),
        ),
        in_specs=[block, block, whole, whole, whole, pl.BlockSpec((SLOTS, 128), lambda p: (0, 0))],
        out_specs=(
            pl.BlockSpec((2, FF_LOCAL, SHARE), lambda p: (0, 0, p)),
            pl.BlockSpec((FF_LOCAL, SHARE), lambda p: (0, p)),
            pl.BlockSpec((1, SHARE), lambda p: (0, p)),
            pl.BlockSpec((2, FF_LOCAL), lambda p: (0, 0)),
        ),
        compiler_params=pltpu.CompilerParams(vmem_limit_bytes=40 * 2**20),
        cost_estimate=pl.CostEstimate(
            flops=6 * SLOTS * D * FF_LOCAL, bytes_accessed=22_000_000, transcendentals=0
        ),
        name="expert_grads",
    )(rows, cots, scaled, grad_gate, grad_up, gate_cols)


def back_kernel(
    grad_att, queries, keys_values, log_total, allowed, trig, first_scale, settings, small, grad_logits, layer_share,
    output_weight, query_weight, key_weight, value_weight, tokens, normed_all, heads_all,
    query_grad, key_value_grad, tokens_out, layer_out, small_all, small_own, output_grad,
    N, H, Q, B, O, query_sum, wide_tokens, wide_att, wo, wq, wk, wv,
    part, from_sibling, sums, from_y, stat, stats, blocks, layers, line, lines_in, lines_all,
    send_sems, recv_sems, local_sems,
):
    me = Place()
    send = Sender(me, send_sems, recv_sems)
    all_here = me.greet(True, True)

    def load(source, target, n):
        copy = pltpu.make_async_copy(source, target, local_sems.at[n])
        copy.start()
        return copy

    load_output = load(output_weight, wo, 0)
    load_heads = load(heads_all, H, 1)
    load_weights = [load(query_weight, wq, 2), load(key_weight, wk, 3), load(value_weight, wv, 4)]
    load_tokens = load(tokens, wide_tokens.at[0:D], 5)
    load_normed = load(normed_all, N, 6)
    wide_att[0:D, :] = grad_att[...]
    wide_att[D:, :] = jnp.zeros((WIDE - D, ROWS), BF16)
    wide_tokens[D:, :] = jnp.zeros((WIDE - D, ROWS), BF16)
    mine = pl.ds(pl.multiple_of(me.tp * SHARE, SHARE), SHARE)
    all_here()

    def lines_for(group, core):
        return pl.ds(pl.multiple_of(group * 192 + core * 96, 16), 96)

    own_half = pl.ds(pl.multiple_of(me.core * 96, 16), 96)
    other_half = pl.ds(pl.multiple_of((1 - me.core) * 96, 16), 96)
    att_in = [None]
    for k in range(1, EXPERTS):
        device = me.along_ep(k)
        att_in.append(
            send.start(wide_att.at[lines_for(device[0], me.core)], B.at[k, own_half], device)
        )
    B[0, own_half, :] = wide_att[lines_for(me.ep, me.core), :]
    layers[me.tp] = layer_share[...]
    end_layers = start_gather_shares(me, send, layers)

    load_output.wait()
    head_rows = contract_rows(grad_att[...], wo[...])
    both = keys_values[...].astype(F32)
    row_pair = jnp.transpose(both).astype(BF16)
    key_rows, value_rows = row_pair[:, 0:64], row_pair[:, 64:128]
    included = allowed[...] > 0.5
    sinks = column_of(settings[SINKS : SINKS + 1, :])
    grad_keys = jnp.zeros((64, ROWS), F32)
    grad_values = jnp.zeros((64, ROWS), F32)
    sink_line = jnp.zeros((1, 128), F32)
    place = lax.broadcasted_iota(jnp.int32, (1, 128), 1)
    factor = HEAD_SIZE**-0.5
    for h in range(HEADS):
        if h % 2 == 0:
            pair = jnp.transpose(head_rows[:, h * 64 : h * 64 + 128]).astype(BF16)
        grad_head = pair[0:64] if h % 2 == 0 else pair[64:128]
        query = queries[h * 64 : h * 64 + 64, :]
        scores = jnp.where(included, product(key_rows, query) * factor, NEGATIVE)
        logs = log_total[h : h + 1, :]
        probs = jnp.exp(scores - logs)
        grad_probs = product(value_rows, grad_head)
        delta = jnp.sum(probs * grad_probs, axis=0, keepdims=True)
        grad_scores = (probs * (grad_probs - delta)).astype(BF16)
        sunk = -jnp.sum(jnp.exp(sinks[h : h + 1, :] - logs) * delta, axis=1, keepdims=True)
        sink_line = jnp.where(place == h, sunk, sink_line)
        grad_values = grad_values + against_rows(grad_head, probs.astype(BF16))
        grad_keys = grad_keys + against_rows(query, grad_scores)
        grad_query = product(keys_values[0:64, :], grad_scores) * factor
        Q[0, h * 64 : h * 64 + 64, :] = rotate(grad_query, trig, True).astype(BF16)
    Q[0, 512:576, :] = rotate(grad_keys * factor, trig, True).astype(BF16)
    Q[0, 576:640, :] = grad_values.astype(BF16)
    all_heads = GroupGather(me, send, Q, 640, False)
    all_heads.begin()
    for k in range(1, EXPERTS):
        send.arrived(att_in[k], B.at[k, own_half])
    shared = send.start(B.at[:, own_half], B.at[:, own_half], me.sibling())

    for copy in load_weights:
        copy.wait()

    def grad(lo, width):
        return (
            product(wq[lo : lo + width, :], Q[0, 0:512, :])
            + contract_rows(wk[:, lo : lo + width], Q[0, 512:576, :])
            + contract_rows(wv[:, lo : lo + width], Q[0, 576:640, :])
        )

    def emit(q, block):
        part[q] = block.astype(BF16)

    share_blocks(grad, emit)
    send.arrived(shared, B.at[:, other_half])
    load_heads.wait()
    O[0] = against_rows(
        jnp.concatenate([B[k] for k in range(EXPERTS)], axis=1),
        jnp.concatenate([H[k] for k in range(EXPERTS)], axis=1),
    ).astype(BF16)
    all_blocks = GroupGather(me, send, O, 192, False)
    all_blocks.begin()
    all_heads.relay()
    load_tokens.wait()
    gain = column_share(settings, FIRST_GAIN, me)
    scale = first_scale[0:1, :]
    normal = wide_tokens[mine, :].astype(F32) * scale
    grad_normed = reduce_shares(me, send, part, from_sibling, sums, from_y)
    raised = gain * grad_normed
    stat[...] = jnp.broadcast_to(jnp.sum(raised * normal, axis=0, keepdims=True), (8, ROWS))
    all_heads.meet()
    all_heads.begin(1)
    all_blocks.relay()
    total = exchange(me, send, stat, stats)
    grad_tokens = wide_att[mine, :].astype(F32) + scale * (
        raised - normal * (total[0:1, :] * (1.0 / D))
    )
    blocks[me.tp] = grad_tokens.astype(BF16)
    end_gather = start_gather_shares(me, send, blocks)

    line[0:17, :] = small[0:17, :]
    line[17:18, :] = small[24:25, :]
    line[18:19, :] = row_sums(grad_normed * normal)[0:1]
    router_bias = row_sums(grad_logits[...])[0:1]
    line[19:20, :] = jnp.concatenate([router_bias, jnp.zeros((1, SHARE - 16), F32)], axis=1)
    line[20:21, :] = jnp.concatenate([sink_line, jnp.zeros((1, SHARE - 128), F32)], axis=1)
    head_sums = row_sums(Q[0].astype(F32))
    line[21:22, :] = head_sums[0:1, 0:SHARE]
    line[22:23, :] = jnp.concatenate(
        [head_sums[0:1, SHARE:640], jnp.zeros((1, 2 * SHARE - 640), F32)], axis=1
    )
    line[23:24, :] = jnp.zeros((1, SHARE), F32)
    tickets = [
        send.start(line, lines_in.at[k - 1], me.along_ep(k)) for k in range(1, EXPERTS)
    ]
    all_blocks.meet()
    all_blocks.begin(1)
    end_layers()
    for q in range(BLOCKS):
        width = min(SHARE, D - q * SHARE)
        layer_out[q * SHARE : q * SHARE + width, :] = layers[q, 0:width, :]
    end_gather()
    tokens_out[...] = blocks[...]
    load_normed.wait()

    def head_step(j, first=False):
        for piece in (0, 1):
            half = slice(piece * 320, piece * 320 + 320)
            slots = [4 * j + i if piece == 0 else 4 * i + j for i in range(4)]
            right = jnp.concatenate([Q[k, half, :] for k in slots], axis=1)

            @pl.loop(0, 4)
            def _(r):
                span = pl.ds(pl.multiple_of(r * 720, 16), 720)
                left = jnp.concatenate([N[k, span, :] for k in slots], axis=1)
                value = against_rows(left, right)
                if not first:
                    value = value + query_sum[piece, span, :]
                query_sum[piece, span, :] = value

    head_step(0, True)
    all_heads.relay(1)
    summed = line[...]
    for k, n in enumerate(tickets):
        send.arrived(n, lines_in.at[k])
        summed = summed + lines_in[k]
    lines_all[me.tp] = summed
    small_own[...] = summed
    end_lines = start_gather_shares(me, send, lines_all)
    head_step(1)
    all_blocks.relay(1)
    head_step(3)
    end_lines()
    small_all[...] = lines_all[...]
    all_heads.meet(1)
    head_step(2)
    query_grad[...] = jnp.concatenate(
        [query_sum[0], query_sum[1, :, 0:192]], axis=1
    ).astype(BF16)
    key_value_grad[...] = query_sum[1, :, 192:320].astype(BF16)
    all_blocks.meet(1)
    keep = [load(O.at[k], output_grad.at[me.back_ep(k)[0]], 7 + k) for k in range(EXPERTS)]
    for copy in keep:
        copy.wait()
    send.finish()


def back(*operands):
    bf = lambda *dims: pltpu.VMEM(dims, BF16)
    fl = lambda *dims: pltpu.VMEM(dims, F32)
    return pl.pallas_call(
        back_kernel,
        out_shape=(
            shape((D, 512), BF16),
            shape((D, 128), BF16),
            shape((8, SHARE, ROWS), BF16),
            shape((D, ROWS), BF16),
            shape((8, 24, SHARE), F32),
            shape((24, SHARE), F32),
            shape((16, 192, 512), BF16),
        ),
        in_specs=vmem(11) + hbm(7),
        out_specs=tuple(vmem(6) + hbm(1)),
        scratch_shapes=[
            bf(16, D, ROWS),
            bf(16, 512, ROWS),
            bf(16, 640, ROWS),
            bf(16, 192, ROWS),
            bf(16, 192, 512),
            fl(2, D, 320),
            bf(WIDE, ROWS),
            bf(WIDE, ROWS),
            bf(D, 512),
            bf(D, 512),
            bf(64, D),
            bf(64, D),
            bf(8, SHARE, ROWS),
            bf(4, SHARE, ROWS),
            bf(3, SHARE, ROWS),
            bf(3, SHARE, ROWS),
            fl(8, ROWS),
            fl(7, 8, ROWS),
            bf(8, SHARE, ROWS),
            bf(8, SHARE, ROWS),
            fl(24, SHARE),
            fl(15, 24, SHARE),
            fl(8, 24, SHARE),
            *semaphores(160),
            pltpu.SemaphoreType.DMA((23,)),
        ],
        compiler_params=params(3, 63),
        name="back",
    )(*operands)


def shards(
    tokens,
    seq_lengths,
    expert_ids,
    first_gain,
    query_weight,
    key_matrix,
    value_matrix,
    query_bias,
    key_offset_bias,
    value_offset_bias,
    head_sink_logits,
    output_weight,
    output_bias,
    second_gain,
    router_weight,
    router_bias,
    expert_gateup,
    gateup_bias,
    expert_down,
    down_bias,
    cotangent,
):
    gap = jnp.zeros((WIDE - D,), F32)
    settings = jnp.concatenate(
        [
            output_bias, gap, second_gain, gap, first_gain, gap, query_bias, key_offset_bias, value_offset_bias,
            router_bias, jnp.zeros((112,), F32), head_sink_logits, jnp.zeros((248,), F32),
        ]
    ).reshape(80, 128)
    (
        queries, keys_values, log_total, first_scale, trig, allowed, scaled_hidden, grad_gate, grad_up,
        gate_cols, grad_att, layer_share, small, grad_logits, expert_rows, cot_rows, normed_all, heads_all,
    ) = layer(
        seq_lengths, expert_ids.T, settings, gateup_bias[0], down_bias, tokens.T, cotangent.T, query_weight,
        key_matrix.T, value_matrix.T, output_weight.T, router_weight.T,
        jnp.swapaxes(expert_gateup[0], 1, 2), expert_down[0],
    )
    query_grad, key_value_grad, token_blocks, layer_t, small_all, small_own, output_blocks = back(
        grad_att, queries, keys_values, log_total, allowed, trig, first_scale, settings, small, grad_logits,
        layer_share, output_weight.T, query_weight, key_matrix.T, value_matrix.T, tokens.T, normed_all, heads_all,
    )
    grad_gateup, grad_down, grad_down_bias, grad_gateup_bias = expert_grads(
        expert_rows, cot_rows, scaled_hidden, grad_gate, grad_up, gate_cols
    )
    grad_tokens = token_blocks.reshape(WIDE, ROWS)[:D].astype(F32).T
    output_grad = output_blocks.reshape(WIDE, 512)[:D].astype(F32).T
    across = small_all.transpose(1, 0, 2).reshape(24, WIDE)[:, :D]
    head_sums = small_own[21:23].reshape(2 * SHARE)
    return (
        layer_t.T,
        grad_tokens,
        across[18],
        query_grad.astype(F32),
        key_value_grad[:, 0:64].astype(F32),
        key_value_grad[:, 64:128].astype(F32),
        head_sums[0:512],
        head_sums[512:576],
        head_sums[576:640],
        small_own[20, 0:HEADS],
        output_grad,
        across[17],
        across[16],
        across[:16].T,
        small_own[19, 0:EXPERTS],
        jnp.swapaxes(grad_gateup, 1, 2)[None],
        grad_gateup_bias[None],
        grad_down[None],
        grad_down_bias,
    )


def solution(mesh):
    in_specs = (
        P("ep", None),
        P(),
        P("ep", None),
        P(),
        P(None, "tp"),
        P(None, "tp"),
        P(None, "tp"),
        P("tp"),
        P("tp"),
        P("tp"),
        P("tp"),
        P("tp", None),
        P(),
        P(),
        P(),
        P(),
        P("ep", None, None, "tp"),
        P("ep", None, "tp"),
        P("ep", "tp", None),
        P("ep", None),
        P("ep", None),
    )
    out_specs = (
        P("ep", None),
        P("ep", None),
        P(),
        P(None, "tp"),
        P(None, "tp"),
        P(None, "tp"),
        P("tp"),
        P("tp"),
        P("tp"),
        P("tp"),
        P("tp", None),
        P(),
        P(),
        P(),
        P(),
        P("ep", None, None, "tp"),
        P("ep", None, "tp"),
        P("ep", "tp", None),
        P("ep", None),
    )
    return jax.shard_map(shards, mesh=mesh, in_specs=in_specs, out_specs=out_specs, check_vma=False)
```

```python
import math

import jax
import jax.numpy as jnp
from jax import lax
from jax.experimental import pallas as pl
from jax.experimental.pallas import tpu as pltpu
from jax.sharding import PartitionSpec as P

HEAD_SIZE = 64
EPS = 1e-05
THETA = 150000.0
LIMIT = 7.0
ALPHA = 1.702
NEGATIVE = -1e30

D = 2880
FF_LOCAL = 360
SHARE = 384
BLOCKS = 8
WIDE = SHARE * BLOCKS
ROWS = 128
EXPERTS = 16
CAP = 48
SLOTS = EXPERTS * CAP
HALF = SLOTS // 2
HEADS = 8
FF = 384
QUARTER = SLOTS // 4
MESH = pl.DeviceIdType.MESH
F32 = jnp.float32
BF16 = jnp.bfloat16
HIGHEST = lax.Precision.HIGHEST


def product(left, right):
    return jnp.dot(left, right, preferred_element_type=F32)


def contract_rows(left, right):
    return lax.dot_general(left, right, (((0,), (0,)), ((), ())), preferred_element_type=F32)


def against_rows(left, right):
    return lax.dot_general(left, right, (((1,), (1,)), ((), ())), preferred_element_type=F32)


def exact(left, right, left_dim=1, right_dim=0):
    return lax.dot_general(
        left,
        right,
        (((left_dim,), (right_dim,)), ((), ())),
        preferred_element_type=F32,
        precision=HIGHEST,
    )


def row_sums(columns):
    return exact(jnp.ones((8, columns.shape[1]), F32), columns, 1, 1)


class Place:
    def __init__(self):
        self.ep = lax.axis_index("ep")
        self.tp = lax.axis_index("tp")
        self.z, self.x = self.ep // 4, self.ep % 4
        self.y, self.core = self.tp // 2, self.tp % 2

    def sibling(self):
        return (self.ep, self.y * 2 + (1 - self.core))

    def along_y(self, step):
        return (self.ep, lax.rem(self.y + step, 4) * 2 + self.core)

    def along_tp(self, step):
        return (self.ep, lax.rem(self.tp + step, 8))

    def along_ep(self, k):
        z = lax.rem(self.z + k // 4, 4)
        x = lax.rem(self.x + k % 4, 4)
        return (z * 4 + x, self.tp)

    def back_ep(self, k):
        z = lax.rem(self.z + 4 - k // 4, 4)
        x = lax.rem(self.x + 4 - k % 4, 4)
        return (z * 4 + x, self.tp)

    def greet(self, tp, ep):
        barrier = pltpu.get_barrier_semaphore()
        partners = [self.along_tp(i) for i in range(1, 8) if tp]
        partners += [self.along_ep(k) for k in range(1, 16) if ep]
        for device in partners:
            pl.semaphore_signal(barrier, inc=1, device_id=device, device_id_type=MESH)
        return lambda: pl.semaphore_wait(barrier, len(partners))


class Sender:
    def __init__(self, me, send_sems, recv_sems):
        self.me, self.send_sems, self.recv_sems = me, send_sems, recv_sems
        self.used = 0
        self.open = []

    def start(self, source, target, device):
        n = self.used
        self.used += 1
        copy = pltpu.make_async_remote_copy(
            src_ref=source,
            dst_ref=target,
            send_sem=self.send_sems.at[n],
            recv_sem=self.recv_sems.at[n],
            device_id=device,
            device_id_type=MESH,
        )
        copy.start()
        self.open.append(copy)
        return n

    def arrived(self, n, target):
        pltpu.make_async_remote_copy(
            src_ref=target,
            dst_ref=target,
            send_sem=self.send_sems.at[n],
            recv_sem=self.recv_sems.at[n],
            device_id=self.me.sibling(),
            device_id_type=MESH,
        ).wait_recv()

    def finish(self):
        for copy in self.open:
            copy.wait_send()
        self.open = []


class GroupGather:
    def __init__(self, me, send, buffer, lines, shared, first=None):
        self.me, self.send, self.buffer, self.shared = me, send, buffer, shared
        first = first or lines // (4 if shared else 2)
        self.sizes = (first, lines // (2 if shared else 1) - first)
        self.tickets, self.passed = {}, {}

    def span(self, part, core, piece=None):
        start, size = (0, self.sizes[0])[part], self.sizes[part]
        if self.shared:
            start = core * sum(self.sizes) + start
        cut = size // 32 * 16
        if piece == 0:
            size = cut
        if piece == 1:
            start, size = start + cut, size - cut
        return pl.ds(pl.multiple_of(start, 16), size)

    def groups(self, part, phase, j):
        unit = 1 if (part + phase) % 2 == 0 else 4
        if phase == 0:
            return [j * unit]
        if part == 0:
            return [slice(4 * j, 4 * j + 4)]
        return [4 * i + j for i in range(4)]

    def move(self, name, part, phase, source, target, piece=None):
        unit = 1 if (part + phase) % 2 == 0 else 4
        span = self.span(part, self.me.core, piece)
        step = (target - source) % 4
        self.tickets[name, part, phase] = [
            self.send.start(
                self.buffer.at[a, span], self.buffer.at[b, span], self.me.along_ep(unit * step)
            )
            for a, b in zip(self.groups(part, phase, source), self.groups(part, phase, target))
        ]

    def wait(self, name, part, phase, j, piece=None):
        span = self.span(part, self.me.core, piece)
        for n, slots in zip(self.tickets[name, part, phase], self.groups(part, phase, j)):
            self.send.arrived(n, self.buffer.at[slots, span])

    def begin(self, phase=0):
        for part in (0, 1):
            self.move("right", part, phase, 0, 1)
            self.move("left", part, phase, 0, 3)

    def relay(self, phase=0):
        for part in (0, 1):
            self.wait("right", part, phase, 1)
            self.move("far right", part, phase, 1, 2, 0)
            self.wait("left", part, phase, 3)
            self.move("far left", part, phase, 3, 2, 1)

    def meet(self, phase=0):
        for part in (0, 1):
            self.wait("far right", part, phase, 2, 0)
            self.wait("far left", part, phase, 2, 1)

    def shares(self, j):
        low = 1 if j == 0 else 0
        return [(0, slice(4 * j + low, 4 * j + 4))] + [(1, 4 * i + j) for i in range(low, 4)]

    def pass_on(self, j):
        self.passed[j] = []
        for part, slots in self.shares(j):
            block = self.buffer.at[slots, self.span(part, self.me.core)]
            self.passed[j].append(self.send.start(block, block, self.me.sibling()))

    def complete(self, j):
        for n, (part, slots) in zip(self.passed[j], self.shares(j)):
            self.send.arrived(n, self.buffer.at[slots, self.span(part, 1 - self.me.core)])


def column_of(row):
    return jnp.transpose(jnp.broadcast_to(row, (128, 128)))


def column_share(settings, first, me):
    return jnp.concatenate(
        [column_of(settings[pl.ds(first + me.tp * 3 + j, 1), :]) for j in range(3)], axis=0
    )


def share_blocks(part, emit):
    for q in range(BLOCKS):
        lo = q * SHARE
        width = min(SHARE, D - lo)
        block = part(lo, width)
        if width < SHARE:
            block = jnp.concatenate(
                [block, jnp.zeros((SHARE - width, block.shape[1]), block.dtype)], axis=0
            )
        emit(q, block)


class ReduceShares:
    order = (2, 1, 3, 0)

    def __init__(self, me, send, part, from_sibling, sums, from_y):
        self.me, self.send, self.part = me, send, part
        self.from_sibling, self.sums, self.from_y = from_sibling, sums, from_y
        self.tickets = [
            send.start(part.at[self.at(step) + 1 - me.core], from_sibling.at[i], me.sibling())
            for i, step in enumerate(self.order)
        ]

    def at(self, step):
        return lax.rem(self.me.y + step, 4) * 2

    def pair(self):
        self.landed = []
        for i, step in enumerate(self.order):
            self.send.arrived(self.tickets[i], self.from_sibling.at[i])
            total = self.part[self.at(step) + self.me.core].astype(F32) + self.from_sibling[
                i
            ].astype(F32)
            if step:
                self.sums[i] = total.astype(BF16)
                self.landed.append(
                    self.send.start(self.sums.at[i], self.from_y.at[i], self.me.along_y(step))
                )
        self.total = total

    def end(self):
        for i, n in enumerate(self.landed):
            self.send.arrived(n, self.from_y.at[i])
            self.total = self.total + self.from_y[i].astype(F32)
        return self.total


class Exchange:
    def __init__(self, me, send, own, others):
        self.send, self.own, self.others = send, own, others
        self.tickets = [send.start(own, others.at[i - 1], me.along_tp(i)) for i in range(1, 8)]

    def end(self):
        total = self.own[...]
        for i, n in enumerate(self.tickets):
            self.send.arrived(n, self.others.at[i])
            total = total + self.others[i]
        return total


def start_gather_shares(me, send, blocks):
    own = blocks.at[me.tp]
    to_y = [send.start(own, own, me.along_y(step)) for step in (2, 1, 3)]
    to_sibling = [send.start(own, own, me.sibling())]

    def end():
        for n, step in zip(to_y, (2, 1, 3)):
            block = blocks.at[lax.rem(me.y + 4 - step, 4) * 2 + me.core]
            send.arrived(n, block)
            to_sibling.append(send.start(block, block, me.sibling()))
        for n, step in zip(to_sibling, (0, 2, 1, 3)):
            send.arrived(n, blocks.at[lax.rem(me.y + 4 - step, 4) * 2 + 1 - me.core])

    return end


def vmem(count):
    return [pl.BlockSpec(memory_space=pltpu.VMEM)] * count


def hbm(count):
    return [pl.BlockSpec(memory_space=pl.ANY)] * count


def semaphores(count):
    return [pltpu.SemaphoreType.DMA((count,)), pltpu.SemaphoreType.DMA((count,))]


def params(number, megabytes):
    return pltpu.CompilerParams(
        collective_id=number, has_side_effects=True, vmem_limit_bytes=megabytes * 2**20
    )


shape = jax.ShapeDtypeStruct


OUTPUT_BIAS, SECOND_GAIN, FIRST_GAIN, HEAD_BIASES, ROUTER_BIAS, SINKS = 0, 24, 48, 72, 77, 78


def turned(me):
    k = lax.broadcasted_iota(jnp.int32, (EXPERTS, EXPERTS), 0)
    e = lax.broadcasted_iota(jnp.int32, (EXPERTS, EXPERTS), 1)
    name = ((me.z + (k >> 2)) & 3) * 4 + ((me.x + (k & 3)) & 3)
    return (name == e).astype(F32)


def rotate(pair, trig, back=False):
    first, last = pair[0:32], pair[32:64]
    cosine, sine = trig[0:32, :], trig[32:64, :]
    if back:
        sine = -sine
    return jnp.concatenate([first * cosine - last * sine, last * cosine + first * sine], axis=0)


def documents(index, first_end, second_end):
    return (index >= first_end).astype(jnp.int32) + (index >= second_end).astype(jnp.int32)


def activation_parts(gate_pre, up_pre):
    lowered = LIMIT - gate_pre
    cap = jnp.maximum(lowered, 0.0) + jnp.log(1.0 + jnp.exp(-jnp.abs(lowered)))
    capped_gate = LIMIT - cap
    tanh = jnp.tanh(up_pre * (1.0 / LIMIT))
    capped_up = LIMIT * tanh
    sigmoid = 1.0 / (1.0 + jnp.exp(-ALPHA * capped_gate))
    return lowered, capped_gate, tanh, capped_up, sigmoid


def layer_kernel(
    lengths, ids, settings, gateup_bias, down_bias,
    tokens, cotangent, query_weight, key_weight, value_weight, output_weight, router, gateup, down,
    queries, keys_values, log_total, first_scale, trig, allowed, bias_sums,
    grad_att_out, layer_out, small_out, grad_logits_out,
    scaled_out, grad_pre_out, rows_out, cots_out, normed_all, heads_all,
    wide_tokens, wide_cot, wide_normed, wide_router, wq, wk, wv, wo, router_in, unpadded, wide_gateup, wide_down,
    wide_bias,
    selector, heads, mixed, second, stat, part, part_sibling, part_sums, part_y, stat_own, stats,
    R, C, staged, staged_c, staged_near, gates_send, gates, gate_sums_send, gate_sums, pre, hidden, grad_pre,
    to_sibling, from_sibling, sums, far_in, near_in, home, scaled, scaled_grad, blocks,
    send_sems, recv_sems, local_sems,
):
    me = Place()
    send = Sender(me, send_sems, recv_sems)
    all_here = me.greet(True, True)

    def load(source, target, n):
        copy = pltpu.make_async_copy(source, target, local_sems.at[n])
        copy.start()
        return copy

    load_cot = load(cotangent, wide_cot.at[0:D], 0)
    load_tokens = load(tokens, wide_tokens.at[0:D], 1)
    load_query = load(query_weight, wq, 2)
    load_pair = [load(key_weight, wk, 3), load(value_weight, wv, 4)]
    load_output = load(output_weight, wo, 5)
    load_router = load(router, router_in, 6)
    load_expert = load(gateup.at[0], unpadded, 7)

    def place_weights(target, first):
        for q in range(BLOCKS):
            width = min(SHARE, D - q * SHARE)
            to = (q % 2 * 4 + q // 2) * SHARE
            target[first : first + FF_LOCAL, to : to + width] = unpadded[
                :, q * SHARE : q * SHARE + width
            ]

    def block_at(core, y):
        return core * 4 + y

    mine = pl.ds(pl.multiple_of(me.tp * SHARE, SHARE), SHARE)
    own = block_at(me.core, me.y)
    for buffer in (wide_cot, wide_tokens):
        buffer[D:, :] = jnp.zeros((WIDE - D, ROWS), BF16)

    k = lax.broadcasted_iota(jnp.int32, (EXPERTS, ROWS), 0)
    name = ((me.z + (k >> 2)) & 3) * 4 + ((me.x + (k & 3)) & 3)
    chosen = jnp.zeros((EXPERTS, ROWS), F32)
    for j in range(4):
        chosen = chosen + (name == ids[j : j + 1, :]).astype(F32)
    taken = chosen > 0.5
    column = lax.broadcasted_iota(jnp.int32, (ROWS, ROWS), 0)
    row = lax.broadcasted_iota(jnp.int32, (ROWS, ROWS), 1)
    rank = product(chosen.astype(BF16), (column < row).astype(F32).astype(BF16))
    rank = jnp.where(taken, rank, -1.0)
    place = lax.broadcasted_iota(jnp.int32, (CAP, ROWS), 0).astype(F32)
    for k in range(EXPERTS):
        selector[k * CAP : (k + 1) * CAP, :] = (
            (place == rank[k : k + 1, :]).astype(F32).astype(BF16)
        )
    load_cot.wait()
    staged_c[...] = against_rows(selector[HALF:, :], wide_cot[mine, :]).astype(BF16)
    for y in range(4):
        span = pl.ds(pl.multiple_of((2 * y + me.core) * SHARE, SHARE), SHARE)
        staged_near[y] = against_rows(selector[0:HALF, :], wide_cot[span, :]).astype(BF16)
    all_here()

    def lines_at(j, piece=None):
        if piece is None:
            return pl.ds(j * QUARTER, QUARTER)
        return pl.ds(j * QUARTER + piece * (QUARTER // 2), QUARTER // 2)

    def back_y(buffer, step, lines, core):
        return buffer.at[block_at(core, lax.rem(me.y + 4 - step, 4)), lines]

    def spread(buffer, tickets, j):
        for k in range(4 * j, 4 * j + 4):
            if k:
                send.arrived(tickets[k], buffer.at[own, pl.ds(k * CAP, CAP)])
        source = buffer.at[own, lines_at(j)]
        return {
            1: send.start(source, source, me.along_y(1)),
            3: send.start(source, source, me.along_y(3)),
            "sibling": [send.start(source, source, me.sibling())],
        }

    def pass_on(buffer, tickets, j):
        for step, piece in ((1, 0), (3, 1)):
            block = back_y(buffer, step, lines_at(j), me.core)
            send.arrived(tickets[step], block)
            block_half = back_y(buffer, step, lines_at(j, piece), me.core)
            tickets[2, piece] = send.start(block_half, block_half, me.along_y(step))
            tickets["sibling"].append(send.start(block, block, me.sibling()))

    def pass_far(buffer, tickets, j):
        for piece in (0, 1):
            send.arrived(tickets[2, piece], back_y(buffer, 2, lines_at(j, piece), me.core))
        block = back_y(buffer, 2, lines_at(j), me.core)
        tickets["sibling"].append(send.start(block, block, me.sibling()))

    def complete(buffer, tickets, j):
        for n, step in zip(tickets["sibling"], (0, 1, 3, 2)):
            send.arrived(n, back_y(buffer, step, lines_at(j), 1 - me.core))

    half_blocks = pl.ds(me.core * 4, 4)
    other_blocks = pl.ds((1 - me.core) * 4, 4)
    cots_in = [None] * EXPERTS
    for k in range(8, EXPERTS):
        cots_in[k] = send.start(
            staged_c.at[(k - 8) * CAP : (k - 7) * CAP],
            C.at[own, k * CAP : (k + 1) * CAP],
            me.along_ep(k),
        )
    for k in range(1, 8):
        lines = slice(k * CAP, (k + 1) * CAP)
        cots_in[k] = send.start(
            staged_near.at[:, lines], C.at[half_blocks, lines], me.along_ep(k)
        )
    C[half_blocks, 0:CAP, :] = staged_near[:, 0:CAP, :]

    load_tokens.wait()

    def squares(j, total):
        lines = wide_tokens[pl.ds(pl.multiple_of(j * 96, 96), 96), :].astype(F32)
        return total + jnp.sum(lines * lines, axis=0, keepdims=True)

    scale = lax.rsqrt(lax.fori_loop(0, 30, squares, jnp.zeros((1, ROWS), F32)) * (1.0 / D) + EPS)
    first_scale[...] = jnp.broadcast_to(scale, (8, ROWS))

    @pl.loop(0, 24)
    def _(j):
        span = pl.ds(pl.multiple_of(j * 128, 128), 128)
        gain = column_of(settings[pl.ds(FIRST_GAIN + j, 1), :])
        wide_normed[span, :] = (wide_tokens[span, :].astype(F32) * scale * gain).astype(BF16)

    keep_normed = load(wide_normed.at[0:D], normed_all.at[0], 10)
    first_end = lengths[me.ep, 0]
    second_end = first_end + lengths[me.ep, 1]
    index = lax.broadcasted_iota(jnp.int32, (1, ROWS), 1)
    document = documents(index, first_end, second_end)
    start = jnp.where(document == 0, 0, jnp.where(document == 1, first_end, second_end))
    positions = (index - start).astype(F32)
    exponent = lax.broadcasted_iota(jnp.int32, (32, ROWS), 0).astype(F32)
    angles = jnp.exp(exponent * (-math.log(THETA) / 32.0)) * positions
    trig[0:32, :] = jnp.cos(angles)
    trig[32:64, :] = jnp.sin(angles)
    included = (
        documents(column, first_end, second_end) == documents(row, first_end, second_end)
    ) & (column <= row)
    allowed[...] = included.astype(F32)
    load_query.wait()
    query_rows = contract_rows(wide_normed[0:D, :], wq[...])
    for copy in load_pair:
        copy.wait()
    both = jnp.concatenate(
        [product(wk[...], wide_normed[0:D, :]), product(wv[...], wide_normed[0:D, :])], axis=0
    ) + column_of(settings[HEAD_BIASES + 4 : HEAD_BIASES + 5, :])
    both = jnp.concatenate([rotate(both[0:64], trig), both[64:128]], axis=0)
    keys_values[...] = both.astype(BF16)
    key_rows = jnp.transpose(both)[:, 0:64].astype(BF16)
    for j in range(4):
        pair = jnp.transpose(query_rows[:, j * 128 : (j + 1) * 128]) + column_of(
            settings[HEAD_BIASES + j : HEAD_BIASES + j + 1, :]
        )
        queries[j * 128 : j * 128 + 64, :] = rotate(pair[0:64], trig).astype(BF16)
        queries[j * 128 + 64 : j * 128 + 128, :] = rotate(pair[64:128], trig).astype(BF16)
    b = [None] * 4
    b[2] = spread(C, cots_in, 2)
    b[3] = spread(C, cots_in, 3)
    keep_normed.wait()
    all_normed = GroupGather(me, send, normed_all, D, True)
    all_normed.begin()
    sinks = column_of(settings[SINKS : SINKS + 1, :])

    def attend(h):
        scores = product(key_rows, queries[h * 64 : h * 64 + 64, :]) * (HEAD_SIZE**-0.5)
        scores = jnp.where(included, scores, NEGATIVE)
        sink = sinks[h : h + 1, :]
        highest = jnp.maximum(jnp.max(scores, axis=0, keepdims=True), sink)
        total = jnp.exp(sink - highest) + jnp.sum(
            jnp.exp(scores - highest), axis=0, keepdims=True
        )
        logs = highest + jnp.log(total)
        log_total[h : h + 1, :] = logs
        probs = jnp.exp(scores - logs).astype(BF16)
        heads[h * 64 : h * 64 + 64, :] = product(keys_values[64:128, :], probs).astype(BF16)

    for h in range(4):
        attend(h)
    pass_on(C, b[2], 2)
    for h in range(4, HEADS):
        attend(h)
    pass_on(C, b[3], 3)
    keep_heads = load(heads, heads_all.at[0], 11)
    load_output.wait()

    def emit(q, block):
        part[q] = block.astype(BF16)

    share_blocks(lambda lo, width: product(wo[lo : lo + width, :], heads[...]), emit)
    reduction = ReduceShares(me, send, part, part_sibling, part_sums, part_y)
    turn = turned(me)
    load_router.wait()
    wide_router[:, 0:D] = product(turn.astype(BF16), router_in[...]).astype(BF16)
    wide_router[:, D:] = jnp.zeros((EXPERTS, WIDE - D), BF16)
    router_share = wide_router[:, mine]
    base = wide_tokens[mine, :].astype(F32) + column_share(settings, OUTPUT_BIAS, me)
    gain = column_share(settings, SECOND_GAIN, me)
    reduction.pair()
    all_normed.relay()
    wide_gateup[...] = jnp.zeros((2 * FF, WIDE), BF16)
    wide_down[...] = jnp.zeros((FF, WIDE), BF16)
    load_expert.wait()
    place_weights(wide_gateup, 0)
    load_expert = load(gateup.at[1], unpadded, 7)
    mixed[...] = base + reduction.end()

    raised = (mixed[...] * gain).astype(BF16)
    second[...] = raised
    staged[...] = against_rows(selector[...], raised).astype(BF16)
    rows_in = [None]
    for k in range(1, EXPERTS):
        lines = pl.ds(k * CAP, CAP)
        rows_in.append(send.start(staged.at[lines], R.at[own, lines], me.along_ep(k)))
    R[own, 0:CAP, :] = staged[0:CAP, :]
    stat_own[0, 0:16, :] = product(router_share, raised)
    stat_own[0, 16:24, :] = jnp.broadcast_to(
        jnp.sum(mixed[...] * mixed[...], axis=0, keepdims=True), (8, ROWS)
    )
    exchanged = Exchange(me, send, stat_own.at[0], stats.at[0:7])
    pass_far(C, b[2], 2)
    pass_far(C, b[3], 3)
    load_expert.wait()
    place_weights(wide_gateup, FF)
    load_expert = load(down, unpadded, 7)
    a = [None] * 4
    a[0] = spread(R, rows_in, 0)
    a[1] = spread(R, rows_in, 1)
    total = exchanged.end()
    scale = lax.rsqrt(total[16:17, :] * (1.0 / D) + EPS)
    plain = total[0:16, :] * scale
    logits = plain + exact(
        turn, column_of(settings[ROUTER_BIAS : ROUTER_BIAS + 1, :])[0:EXPERTS]
    )
    highest = jnp.max(jnp.where(taken, logits, NEGATIVE), axis=0, keepdims=True)
    lifted = jnp.where(taken, jnp.exp(jnp.where(taken, logits, highest) - highest), 0.0)
    stat[0:16, :] = lifted / jnp.sum(lifted, axis=0, keepdims=True)
    stat[16:32, :] = plain
    stat[32:40, :] = jnp.broadcast_to(scale, (8, ROWS))
    a[2] = spread(R, rows_in, 2)
    pass_on(R, a[0], 0)
    a[3] = spread(R, rows_in, 3)
    chosen_rows = selector[...].astype(F32)
    spread_gates = jnp.concatenate(
        [jnp.broadcast_to(stat[k : k + 1, :], (CAP, 128)) for k in range(EXPERTS)], axis=0
    )
    slot_gates = row_sums(spread_gates * chosen_rows)
    slot_scales = exact(jnp.broadcast_to(scale, (8, ROWS)), chosen_rows, 1, 1)
    gates_in = [None]
    for k in range(EXPERTS):
        lines = slice(k * CAP, (k + 1) * CAP)
        pair = jnp.concatenate([slot_gates[0:4, lines], slot_scales[0:4, lines]], axis=0)
        gates_send[k] = jnp.concatenate([pair, jnp.zeros((8, 128 - CAP), F32)], axis=1)
        if k:
            gates_in.append(send.start(gates_send.at[k], gates.at[k], me.along_ep(k)))
    gates[0] = gates_send[0]
    keep_heads.wait()
    all_heads = GroupGather(me, send, heads_all, 512, False)
    all_heads.begin()
    all_normed.meet()
    all_normed.begin(1)
    pass_on(R, a[1], 1)
    for k in range(1, 8):
        send.arrived(cots_in[k], C.at[half_blocks, k * CAP : (k + 1) * CAP])
    near_cots = C.at[half_blocks, 0:HALF]
    near_shared = send.start(near_cots, near_cots, me.sibling())
    pass_far(R, a[0], 0)
    pass_on(R, a[2], 2)
    pass_far(R, a[1], 1)
    pass_on(R, a[3], 3)
    all_heads.relay()
    load_expert.wait()
    place_weights(wide_down, 0)
    bias_row = down_bias[...] * jnp.where(me.tp == 0, 1.0, 0.0)
    bias_high = bias_row.astype(BF16)
    bias_low = (bias_row - bias_high.astype(F32)).astype(BF16)
    line = lax.broadcasted_iota(jnp.int32, (16, D), 0)
    bias_lines = jnp.where(
        line == 8,
        jnp.broadcast_to(bias_high.astype(F32), (16, D)),
        jnp.where(line == 9, jnp.broadcast_to(bias_low.astype(F32), (16, D)), 0.0),
    ).astype(BF16)
    for q in range(BLOCKS):
        width = min(SHARE, D - q * SHARE)
        to = (q % 2 * 4 + q // 2) * SHARE
        lines = bias_lines[:, q * SHARE : q * SHARE + width]
        old = wide_down[352:368, to : to + width]
        wide_down[352:368, to : to + width] = (old.astype(F32) + lines.astype(F32)).astype(BF16)
    wide_bias[...] = jnp.zeros((1, 2 * FF), F32)
    wide_bias[:, 0:FF_LOCAL] = gateup_bias[0:1, :]
    wide_bias[:, FF : FF + FF_LOCAL] = gateup_bias[1:2, :]

    def lines_of(h):
        return pl.ds(h * HALF, HALF)

    def wide_rows(buffer, lines, first, count):
        return jnp.concatenate([buffer[q, lines, :] for q in range(first, first + count)], axis=1)

    def columns_of(what, h):
        return jnp.concatenate(
            [what[0:CAP, k : k + 1] for k in range(8 * h, 8 * h + 8)], axis=0
        )

    unit = lax.broadcasted_iota(jnp.int32, (1, FF), 1)

    def forward(h):
        lines = lines_of(h)
        pre[lines, :] = against_rows(wide_rows(R, lines, 0, 4), wide_gateup[:, 0 : 4 * SHARE])
        pre[lines, :] = (
            pre[lines, :]
            + against_rows(wide_rows(R, lines, 4, 4), wide_gateup[:, 4 * SHARE :])
        ) * columns_of(scale_cols, h) + wide_bias[...]
        _, capped_gate, _, capped_up, sigmoid = activation_parts(
            pre[lines, 0:FF], pre[lines, FF:]
        )
        value = (capped_up + 1.0) * capped_gate * sigmoid
        hidden[lines, :] = jnp.where(
            unit < FF_LOCAL, value, jnp.where(unit < FF_LOCAL + 2, 1.0, 0.0)
        ).astype(BF16)

    def to_home(n, h, left, weights):
        lines = lines_of(h)
        theirs = pl.ds(pl.multiple_of((1 - me.core) * 4 * SHARE, SHARE), 4 * SHARE)
        ours = pl.ds(pl.multiple_of(me.core * 4 * SHARE, SHARE), 4 * SHARE)
        value = product(left, weights[:, theirs]).astype(BF16)
        for y in range(4):
            to_sibling[n // 2, y, lines, :] = value[:, y * SHARE : (y + 1) * SHARE]
        sent = []
        for s in (2, 1, 3, 0):
            block = (n // 2, lax.rem(me.y + s, 4), lines)
            sent.append(
                send.start(to_sibling.at[block], from_sibling.at[block], me.sibling())
            )
        value = product(left, weights[:, ours]).astype(BF16)
        for y in range(4):
            sums[n // 2, y, lines, :] = value[:, y * SHARE : (y + 1) * SHARE]
        return sent

    def add_sibling(n, h, sent):
        lines = lines_of(h)
        for s, ticket in zip((2, 1, 3, 0), sent):
            y = lax.rem(me.y + s, 4)
            send.arrived(ticket, from_sibling.at[n // 2, y, lines])
            sums[n // 2, y, lines, :] = (
                sums[n // 2, y, lines, :].astype(F32) + from_sibling[n // 2, y, lines, :].astype(F32)
            ).astype(BF16)
            yield s, y

    def piece_of(h, piece):
        return pl.ds(h * HALF + piece * QUARTER, QUARTER)

    def near_part(n, h, y, piece, step_y, direction):
        return send.start(
            sums.at[n // 2, y, piece_of(h, piece)],
            near_in.at[n + h, direction, pl.ds(piece * QUARTER, QUARTER)],
            me.along_y(step_y),
        )

    def pair_up(n, h, sent):
        far, early = [], []
        for s, y in add_sibling(n, h, sent):
            if s == 2:
                for piece, step_y in ((0, 1), (1, 3)):
                    far.append(
                        send.start(
                            sums.at[n // 2, y, piece_of(h, piece)],
                            far_in.at[n + h, piece],
                            me.along_y(step_y),
                        )
                    )
            elif s:
                direction = 0 if s == 1 else 1
                early.append(near_part(n, h, y, 1 - direction, s, direction))
        return far, early

    def sums_on(n, h, far):
        far, early = far
        late = []
        for piece, step_y in ((0, 1), (1, 3)):
            y = lax.rem(me.y + step_y, 4)
            half = piece_of(h, piece)
            send.arrived(far[piece], far_in.at[n + h, piece])
            sums[n // 2, y, half, :] = (
                sums[n // 2, y, half, :].astype(F32) + far_in[n + h, piece].astype(F32)
            ).astype(BF16)
            late.append(near_part(n, h, y, piece, step_y, piece))
        return early, late

    def go_home(n, h, near):
        lines = lines_of(h)
        total = sums[n // 2, me.y, lines, :].astype(F32)
        early, late = near
        for direction in (0, 1):
            for ticket, piece in ((early[direction], 1 - direction), (late[direction], direction)):
                send.arrived(
                    ticket, near_in.at[n + h, direction, pl.ds(piece * QUARTER, QUARTER)]
                )
            total = total + near_in[n + h, direction].astype(F32)
        sums[n // 2, me.y, lines, :] = total.astype(BF16)
        tickets = []
        for k in range(8):
            span = pl.ds((8 * h + k) * CAP, CAP)
            place = pl.ds(k * CAP, CAP)
            if 8 * h + k:
                tickets.append(
                    send.start(
                        sums.at[n // 2, me.y, span], home.at[n + h, place], me.back_ep(8 * h + k)
                    )
                )
            else:
                tickets.append(None)
                home[n + h, 0:CAP, :] = sums[n // 2, me.y, 0:CAP, :]
        return tickets

    def is_home(n, h, tickets):
        for k, ticket in enumerate(tickets):
            if ticket is not None:
                send.arrived(ticket, home.at[n + h, pl.ds(k * CAP, CAP)])

    def backward(h):
        lines = lines_of(h)
        gate = columns_of(gate_cols, h)
        raw = against_rows(wide_rows(C, lines, 0, 8), wide_down[...])
        lowered, capped_gate, tanh, capped_up, sigmoid = activation_parts(
            pre[lines, 0:FF], pre[lines, FF:]
        )
        units = hidden[lines, :].astype(F32)
        slot_sums = row_sums(units * raw)
        grad_hidden = jnp.where(unit < FF_LOCAL, gate * raw, 0.0)
        high = gate.astype(BF16).astype(F32)
        scaled[lines, :] = jnp.where(
            unit < FF_LOCAL,
            gate * units,
            jnp.where(unit == FF_LOCAL, high, jnp.where(unit == FF_LOCAL + 1, gate - high, 0.0)),
        ).astype(BF16)
        slope = (capped_up + 1.0) * (
            sigmoid + ALPHA * capped_gate * sigmoid * (1.0 - sigmoid)
        )
        grad_gate = (grad_hidden * slope * (1.0 / (1.0 + jnp.exp(-lowered)))).astype(BF16)
        grad_up = (grad_hidden * capped_gate * sigmoid * (1.0 - tanh * tanh)).astype(BF16)
        grad_pre[lines, 0:FF] = grad_gate
        grad_pre[lines, FF:] = grad_up
        sent = to_home(2, h, grad_pre[lines, :], wide_gateup)
        row_scale = columns_of(scale_cols, h)
        values = grad_pre[lines, :].astype(F32)
        scaled_grad[lines, :] = (values * row_scale).astype(BF16)
        total = jnp.sum(values, axis=0, keepdims=True)
        if h == 0:
            bias_sums[0:1, :] = total
        else:
            bias_sums[0:1, :] = bias_sums[0:1, :] + total
        tickets = []
        for k in range(8 * h, 8 * h + 8):
            first = (k - 8 * h) * CAP
            gate_sums_send[k] = jnp.concatenate(
                [slot_sums[:, first : first + CAP], jnp.zeros((8, 128 - CAP), F32)], axis=1
            )
            if k:
                tickets.append(
                    send.start(gate_sums_send.at[k], gate_sums.at[k], me.back_ep(k))
                )
            else:
                tickets.append(None)
                gate_sums[0] = gate_sums_send[0]
        return sent, tickets

    bias_sums[...] = jnp.zeros((8, 2 * FF), F32)
    for k in range(1, EXPERTS):
        send.arrived(gates_in[k], gates.at[k])
    spare = jnp.zeros((128 - EXPERTS, 128), F32)
    gate_cols = jnp.transpose(jnp.concatenate([gates[:, 0, :], spare], axis=0))
    scale_cols = jnp.transpose(jnp.concatenate([gates[:, 4, :], spare], axis=0))
    complete(R, a[0], 0)
    complete(R, a[1], 1)
    forward(0)
    pass_far(R, a[2], 2)
    send.arrived(near_shared, C.at[other_blocks, 0:HALF])
    sent_0, sums_in = backward(0)
    pass_far(R, a[3], 3)
    far_0 = pair_up(2, 0, sent_0)
    results_0 = to_home(0, 0, hidden[lines_of(0), :], wide_down)
    complete(R, a[2], 2)
    complete(R, a[3], 3)
    rows_copy = load(R, rows_out, 13)
    all_normed.relay(1)
    all_heads.meet()
    all_heads.begin(1)
    forward(1)
    near_0 = sums_on(2, 0, far_0)
    complete(C, b[2], 2)
    complete(C, b[3], 3)
    cots_copy = load(C, cots_out, 12)
    sent_1, more = backward(1)
    sums_in = sums_in + more
    far_1 = pair_up(2, 1, sent_1)
    home_0 = go_home(2, 0, near_0)
    all_normed.pass_on(0)
    all_normed.pass_on(1)
    all_normed.pass_on(3)
    keep_scaled = [load(scaled, scaled_out, 14), load(scaled_grad, grad_pre_out, 15)]
    near_1 = sums_on(2, 1, far_1)
    results_1 = to_home(0, 1, hidden[lines_of(1), :], wide_down)
    weighted = chosen_rows * spread_gates
    high = weighted.astype(BF16)
    low = (weighted - high.astype(F32)).astype(BF16)
    home_1 = go_home(2, 1, near_1)
    res_far_0 = pair_up(0, 0, results_0)
    res_far_1 = pair_up(0, 1, results_1)

    gain = column_share(settings, SECOND_GAIN, me)
    scale = stat[32:33, :]
    normal = mixed[...] * scale
    for k in range(1, EXPERTS):
        send.arrived(sums_in[k], gate_sums.at[k])
    slots = jnp.transpose(jnp.concatenate([gate_sums[:, 0, :], spare], axis=0))
    for k in range(EXPERTS):
        stat_own[1, k : k + 1, :] = jnp.sum(
            chosen_rows[k * CAP : (k + 1) * CAP] * slots[0:CAP, k : k + 1], axis=0, keepdims=True
        )
    is_home(2, 0, home_0)
    returned = contract_rows(home[2], selector[0:HALF, :])
    is_home(2, 1, home_1)
    returned = returned + contract_rows(home[3], selector[HALF:, :])
    stat_own[1, 16:24, :] = jnp.broadcast_to(
        jnp.sum(returned * gain * normal, axis=0, keepdims=True), (8, ROWS)
    )
    exchanged = Exchange(me, send, stat_own.at[1], stats.at[7:14])
    res_near_0 = sums_on(0, 0, res_far_0)
    res_near_1 = sums_on(0, 1, res_far_1)
    all_normed.meet(1)
    all_normed.pass_on(2)
    total = exchanged.end()
    gate_share = stat[0:16, :]
    grad_gates = total[0:16, :]
    grad_logits = gate_share * (
        grad_gates - jnp.sum(gate_share * grad_gates, axis=0, keepdims=True)
    )
    inner = total[16:17, :] + jnp.sum(grad_logits * stat[16:32, :], axis=0, keepdims=True)
    grad_second = returned + exact(wide_router[:, mine].astype(F32), grad_logits, 0, 0)
    grad_mixed = wide_cot[mine, :].astype(F32) + scale * (
        gain * grad_second - normal * (inner * (1.0 / D))
    )
    grad_att = grad_mixed.astype(BF16)
    blocks[me.tp] = grad_att
    end_gather = start_gather_shares(me, send, blocks)
    all_heads.relay(1)
    results_in_0 = go_home(0, 0, res_near_0)
    results_in_1 = go_home(0, 1, res_near_1)
    grad_logits = exact(turn, grad_logits, 0, 0)
    small_out[0:16, :] = exact(grad_logits, second[...].astype(F32) * scale, 1, 1)
    small_out[16:24, :] = row_sums(grad_second * normal)
    small_out[24:32, :] = row_sums(grad_att.astype(F32))
    grad_logits_out[...] = grad_logits
    end_gather()
    for q in range(BLOCKS):
        width = min(SHARE, D - q * SHARE)
        grad_att_out[q * SHARE : q * SHARE + width, :] = blocks[q, 0:width, :]
    is_home(0, 0, results_in_0)
    is_home(0, 1, results_in_1)
    moe_out = jnp.zeros((SHARE, ROWS), F32)
    for h, lines in ((0, slice(0, HALF)), (1, slice(HALF, SLOTS))):
        moe_out = moe_out + contract_rows(home[h], high[lines]) + contract_rows(home[h], low[lines])
    layer_out[...] = (mixed[...] + moe_out).astype(BF16)
    for copy in keep_scaled:
        copy.wait()
    all_heads.meet(1)
    for j in range(4):
        all_normed.complete(j)
    rows_copy.wait()
    cots_copy.wait()
    send.finish()


def layer(*operands):
    bf = lambda *dims: pltpu.VMEM(dims, BF16)
    fl = lambda *dims: pltpu.VMEM(dims, F32)
    return pl.pallas_call(
        layer_kernel,
        out_shape=(
            shape((512, ROWS), BF16),
            shape((128, ROWS), BF16),
            shape((8, ROWS), F32),
            shape((8, ROWS), F32),
            shape((64, ROWS), F32),
            shape((ROWS, ROWS), F32),
            shape((8, 2 * FF), F32),
            shape((D, ROWS), BF16),
            shape((SHARE, ROWS), BF16),
            shape((32, SHARE), F32),
            shape((16, 128), F32),
            shape((SLOTS, FF), BF16),
            shape((SLOTS, 2 * FF), BF16),
            shape((8, SLOTS, SHARE), BF16),
            shape((8, SLOTS, SHARE), BF16),
            shape((16, D, ROWS), BF16),
            shape((16, 512, ROWS), BF16),
        ),
        in_specs=[pl.BlockSpec(memory_space=pltpu.SMEM)] + vmem(4) + hbm(9),
        out_specs=tuple(vmem(11) + hbm(6)),
        scratch_shapes=[
            bf(WIDE, ROWS),
            bf(WIDE, ROWS),
            bf(WIDE, ROWS),
            bf(EXPERTS, WIDE),
            bf(D, 512),
            bf(64, D),
            bf(64, D),
            bf(D, 512),
            bf(EXPERTS, D),
            bf(FF_LOCAL, D),
            bf(2 * FF, WIDE),
            bf(FF, WIDE),
            fl(1, 2 * FF),
            bf(SLOTS, ROWS),
            bf(512, ROWS),
            fl(SHARE, ROWS),
            bf(SHARE, ROWS),
            fl(40, ROWS),
            bf(8, SHARE, ROWS),
            bf(4, SHARE, ROWS),
            bf(3, SHARE, ROWS),
            bf(3, SHARE, ROWS),
            fl(2, 24, ROWS),
            fl(14, 24, ROWS),
            bf(8, SLOTS, SHARE),
            bf(8, SLOTS, SHARE),
            bf(SLOTS, SHARE),
            bf(HALF, SHARE),
            bf(4, HALF, SHARE),
            fl(EXPERTS, 8, 128),
            fl(EXPERTS, 8, 128),
            fl(EXPERTS, 8, 128),
            fl(EXPERTS, 8, 128),
            fl(SLOTS, 2 * FF),
            bf(SLOTS, FF),
            bf(SLOTS, 2 * FF),
            bf(2, 4, SLOTS, SHARE),
            bf(2, 4, SLOTS, SHARE),
            bf(2, 4, SLOTS, SHARE),
            bf(4, 2, QUARTER, SHARE),
            bf(4, 2, HALF, SHARE),
            bf(4, HALF, SHARE),
            bf(SLOTS, FF),
            bf(SLOTS, 2 * FF),
            bf(8, SHARE, ROWS),
            *semaphores(320),
            pltpu.SemaphoreType.DMA((16,)),
        ],
        compiler_params=params(1, 63),
        name="layer",
    )(*operands)


def finish_kernel(
    rows, cots, scaled, grad_pre, output_grad, query_grad, key_value_grad, tokens, layer_in, small,
    gateup_out, down_out, bias_out, output_out, query_out, key_out, value_out, tokens_out, layer_out, router_out,
    gains_out,
):
    gateup = contract_rows(grad_pre[...], rows[0])
    gateup_out[0] = gateup[0:FF_LOCAL]
    gateup_out[1] = gateup[FF : FF + FF_LOCAL]
    both = contract_rows(scaled[...], cots[0])
    down_out[...] = both[0:FF_LOCAL]
    bias_out[...] = both[FF_LOCAL : FF_LOCAL + 1] + both[FF_LOCAL + 1 : FF_LOCAL + 2]
    output_out[...] = output_grad[...].astype(F32)
    query_out[...] = query_grad[...].astype(F32)
    turned_back = jnp.concatenate(
        [
            jnp.transpose(key_value_grad[j : j + 128, :].astype(F32))
            for j in range(0, SHARE, 128)
        ],
        axis=1,
    )
    key_out[...] = turned_back[0:64]
    value_out[...] = turned_back[64:128]
    tokens_out[...] = tokens[...].astype(F32)
    layer_out[...] = layer_in[...]
    router_out[...] = small[0, 0:16, :]
    gains_out[...] = small[0, 16:24, :]


def finish(*operands):
    def whole(*dims):
        return pl.BlockSpec(dims, lambda p: (0,) * len(dims))

    def lines(columns):
        return pl.BlockSpec((SHARE, columns), lambda p: (p, 0))

    def columns(count):
        return pl.BlockSpec((count, SHARE), lambda p: (0, p))

    block = pl.BlockSpec((1, SLOTS, SHARE), lambda p: (p % 2 * 4 + p // 2, 0, 0))
    return pl.pallas_call(
        finish_kernel,
        grid=(BLOCKS,),
        out_shape=(
            shape((2, FF_LOCAL, D), F32),
            shape((FF_LOCAL, D), F32),
            shape((1, D), F32),
            shape((D, 512), F32),
            shape((D, 512), F32),
            shape((64, D), F32),
            shape((64, D), F32),
            shape((D, ROWS), F32),
            shape((D, ROWS), BF16),
            shape((16, D), F32),
            shape((8, D), F32),
        ),
        in_specs=[
            block, block, whole(SLOTS, FF), whole(SLOTS, 2 * FF), lines(512), lines(512), lines(128), lines(ROWS),
            lines(ROWS), pl.BlockSpec((1, 24, SHARE), lambda p: (p, 0, 0)),
        ],
        out_specs=(
            pl.BlockSpec((2, FF_LOCAL, SHARE), lambda p: (0, 0, p)),
            columns(FF_LOCAL), columns(1), lines(512), lines(512), columns(64), columns(64), lines(ROWS),
            lines(ROWS), columns(16), columns(8),
        ),
        compiler_params=pltpu.CompilerParams(vmem_limit_bytes=60 * 2**20),
        cost_estimate=pl.CostEstimate(
            flops=6 * SLOTS * D * FF, bytes_accessed=44_000_000, transcendentals=0
        ),
        name="finish",
    )(*operands)


def back_kernel(
    grad_att, queries, keys_values, log_total, allowed, trig, first_scale, settings, small, grad_logits, layer_share,
    output_weight, query_weight, key_weight, value_weight, tokens, normed_all, heads_all,
    query_grad, key_value_grad, tokens_out, layer_out, small_all, small_own, output_grad,
    N, H, Q, B, O, query_sum, rest_sum, wide_tokens, wide_att, wo, wq, wk, wv,
    part, from_sibling, sums, from_y, stat, stats, blocks, layers, line, line_x, lines_in, lines_all,
    send_sems, recv_sems, local_sems,
):
    me = Place()
    send = Sender(me, send_sems, recv_sems)
    all_here = me.greet(True, True)

    def load(source, target, n):
        copy = pltpu.make_async_copy(source, target, local_sems.at[n])
        copy.start()
        return copy

    load_output = load(output_weight, wo, 0)
    load_heads = load(heads_all, H, 1)
    load_weights = [load(query_weight, wq, 2), load(key_weight, wk, 3), load(value_weight, wv, 4)]
    load_tokens = load(tokens, wide_tokens.at[0:D], 5)
    load_normed = load(normed_all, N, 6)
    wide_att[0:D, :] = grad_att[...]
    wide_att[D:, :] = jnp.zeros((WIDE - D, ROWS), BF16)
    wide_tokens[D:, :] = jnp.zeros((WIDE - D, ROWS), BF16)
    mine = pl.ds(pl.multiple_of(me.tp * SHARE, SHARE), SHARE)
    all_here()

    def lines_for(group, core):
        return pl.ds(pl.multiple_of(group * 192 + core * 96, 16), 96)

    own_half = pl.ds(pl.multiple_of(me.core * 96, 16), 96)
    other_half = pl.ds(pl.multiple_of((1 - me.core) * 96, 16), 96)
    att_in = [None]
    for k in range(1, EXPERTS):
        device = me.along_ep(k)
        att_in.append(
            send.start(wide_att.at[lines_for(device[0], me.core)], B.at[k, own_half], device)
        )
    B[0, own_half, :] = wide_att[lines_for(me.ep, me.core), :]
    layers[me.tp] = layer_share[...]
    end_layers = start_gather_shares(me, send, layers)

    load_output.wait()
    head_rows = contract_rows(grad_att[...], wo[...])
    both = keys_values[...].astype(F32)
    row_pair = jnp.transpose(both).astype(BF16)
    key_rows, value_rows = row_pair[:, 0:64], row_pair[:, 64:128]
    included = allowed[...] > 0.5
    sinks = column_of(settings[SINKS : SINKS + 1, :])
    grad_keys = jnp.zeros((64, ROWS), F32)
    grad_values = jnp.zeros((64, ROWS), F32)
    sink_line = jnp.zeros((1, 128), F32)
    place = lax.broadcasted_iota(jnp.int32, (1, 128), 1)
    factor = HEAD_SIZE**-0.5
    for h in range(HEADS):
        if h % 2 == 0:
            pair = jnp.transpose(head_rows[:, h * 64 : h * 64 + 128]).astype(BF16)
        grad_head = pair[0:64] if h % 2 == 0 else pair[64:128]
        query = queries[h * 64 : h * 64 + 64, :]
        scores = jnp.where(included, product(key_rows, query) * factor, NEGATIVE)
        logs = log_total[h : h + 1, :]
        probs = jnp.exp(scores - logs)
        grad_probs = product(value_rows, grad_head)
        delta = jnp.sum(probs * grad_probs, axis=0, keepdims=True)
        grad_scores = (probs * (grad_probs - delta)).astype(BF16)
        sunk = -jnp.sum(jnp.exp(sinks[h : h + 1, :] - logs) * delta, axis=1, keepdims=True)
        sink_line = jnp.where(place == h, sunk, sink_line)
        grad_values = grad_values + against_rows(grad_head, probs.astype(BF16))
        grad_keys = grad_keys + against_rows(query, grad_scores)
        grad_query = product(keys_values[0:64, :], grad_scores) * factor
        Q[0, h * 64 : h * 64 + 64, :] = rotate(grad_query, trig, True).astype(BF16)
    Q[0, 512:576, :] = rotate(grad_keys * factor, trig, True).astype(BF16)
    Q[0, 576:640, :] = grad_values.astype(BF16)
    all_heads = GroupGather(me, send, Q, 640, False, 256)
    all_heads.begin()
    for k in range(1, EXPERTS):
        send.arrived(att_in[k], B.at[k, own_half])
    shared = send.start(B.at[:, own_half], B.at[:, own_half], me.sibling())

    for copy in load_weights:
        copy.wait()
    all_heads.relay()

    def grad(lo, width):
        return (
            product(wq[lo : lo + width, :], Q[0, 0:512, :])
            + contract_rows(wk[:, lo : lo + width], Q[0, 512:576, :])
            + contract_rows(wv[:, lo : lo + width], Q[0, 576:640, :])
        )

    def emit(q, block):
        part[q] = block.astype(BF16)

    share_blocks(grad, emit)
    reduction = ReduceShares(me, send, part, from_sibling, sums, from_y)
    send.arrived(shared, B.at[:, other_half])
    load_heads.wait()
    O[0] = against_rows(
        jnp.concatenate([B[k] for k in range(EXPERTS)], axis=1),
        jnp.concatenate([H[k] for k in range(EXPERTS)], axis=1),
    ).astype(BF16)
    all_blocks = GroupGather(me, send, O, 192, False)
    all_blocks.begin()
    all_heads.meet()
    all_heads.begin(1)
    reduction.pair()
    all_blocks.relay()
    load_normed.wait()

    def head_step(j, first=False):
        for piece, half, total in ((0, slice(0, 256), query_sum), (1, slice(256, 640), rest_sum)):
            slots = [4 * j + i if piece == 0 else 4 * i + j for i in range(4)]
            right = jnp.concatenate([Q[k, half, :] for k in slots], axis=1)

            @pl.loop(0, 4)
            def _(r):
                span = pl.ds(pl.multiple_of(r * 720, 16), 720)
                left = jnp.concatenate([N[k, span, :] for k in slots], axis=1)
                value = against_rows(left, right)
                if not first:
                    value = value + total[span, :]
                total[span, :] = value

    head_step(0, True)
    load_tokens.wait()
    gain = column_share(settings, FIRST_GAIN, me)
    scale = first_scale[0:1, :]
    normal = wide_tokens[mine, :].astype(F32) * scale
    grad_normed = reduction.end()
    raised = gain * grad_normed
    stat[...] = jnp.broadcast_to(jnp.sum(raised * normal, axis=0, keepdims=True), (8, ROWS))
    exchanged = Exchange(me, send, stat, stats)

    line[0:17, :] = small[0:17, :]
    line[17:18, :] = small[24:25, :]
    line[18:19, :] = row_sums(grad_normed * normal)[0:1]
    router_bias = row_sums(grad_logits[...])[0:1]
    line[19:20, :] = jnp.concatenate([router_bias, jnp.zeros((1, SHARE - 16), F32)], axis=1)
    line[20:21, :] = jnp.concatenate([sink_line, jnp.zeros((1, SHARE - 128), F32)], axis=1)
    head_sums = row_sums(Q[0].astype(F32))
    line[21:22, :] = head_sums[0:1, 0:SHARE]
    line[22:23, :] = jnp.concatenate(
        [head_sums[0:1, SHARE:640], jnp.zeros((1, 2 * SHARE - 640), F32)], axis=1
    )
    line[23:24, :] = jnp.zeros((1, SHARE), F32)
    tickets = [send.start(line, lines_in.at[d - 1], me.along_ep(d)) for d in (1, 2, 3)]
    total = exchanged.end()
    grad_tokens = wide_att[mine, :].astype(F32) + scale * (
        raised - normal * (total[0:1, :] * (1.0 / D))
    )
    blocks[me.tp] = grad_tokens.astype(BF16)
    end_gather = start_gather_shares(me, send, blocks)
    all_blocks.meet()
    all_blocks.begin(1)
    summed = line[...]
    for k, n in enumerate(tickets):
        send.arrived(n, lines_in.at[k])
        summed = summed + lines_in[k]
    line_x[...] = summed
    tickets = [send.start(line_x, lines_in.at[2 + d], me.along_ep(4 * d)) for d in (1, 2, 3)]

    all_heads.relay(1)
    head_step(1)
    end_gather()
    tokens_out[...] = blocks[...]
    all_blocks.relay(1)
    end_layers()
    for q in range(BLOCKS):
        width = min(SHARE, D - q * SHARE)
        layer_out[q * SHARE : q * SHARE + width, :] = layers[q, 0:width, :]
    head_step(3)
    summed = line_x[...]
    for k, n in enumerate(tickets):
        send.arrived(n, lines_in.at[3 + k])
        summed = summed + lines_in[3 + k]
    lines_all[me.tp] = summed
    for j in range(3):
        small_own[j : j + 1, :] = summed[21:22, j * 128 : (j + 1) * 128]
    for j in range(2):
        small_own[3 + j : 4 + j, :] = summed[22:23, j * 128 : (j + 1) * 128]
    small_own[5:6, :] = summed[19:20, 0:128]
    small_own[6:7, :] = summed[20:21, 0:128]
    small_own[7:8, :] = jnp.zeros((1, 128), F32)
    end_lines = start_gather_shares(me, send, lines_all)
    all_heads.meet(1)
    head_step(2)
    query_grad[...] = jnp.concatenate([query_sum[...], rest_sum[:, 0:256]], axis=1).astype(BF16)
    key_value_grad[...] = rest_sum[:, 256:384].astype(BF16)
    end_lines()
    small_all[...] = lines_all[...]
    all_blocks.meet(1)
    keep = [load(O.at[k], output_grad.at[me.back_ep(k)[0]], 7 + k) for k in range(EXPERTS)]
    for copy in keep:
        copy.wait()
    send.finish()


def back(*operands):
    bf = lambda *dims: pltpu.VMEM(dims, BF16)
    fl = lambda *dims: pltpu.VMEM(dims, F32)
    return pl.pallas_call(
        back_kernel,
        out_shape=(
            shape((D, 512), BF16),
            shape((D, 128), BF16),
            shape((8, SHARE, ROWS), BF16),
            shape((D, ROWS), BF16),
            shape((8, 24, SHARE), F32),
            shape((8, 128), F32),
            shape((16, 192, 512), BF16),
        ),
        in_specs=vmem(11) + hbm(7),
        out_specs=tuple(vmem(6) + hbm(1)),
        scratch_shapes=[
            bf(16, D, ROWS),
            bf(16, 512, ROWS),
            bf(16, 640, ROWS),
            bf(16, 192, ROWS),
            bf(16, 192, 512),
            fl(D, 256),
            fl(D, 384),
            bf(WIDE, ROWS),
            bf(WIDE, ROWS),
            bf(D, 512),
            bf(D, 512),
            bf(64, D),
            bf(64, D),
            bf(8, SHARE, ROWS),
            bf(4, SHARE, ROWS),
            bf(3, SHARE, ROWS),
            bf(3, SHARE, ROWS),
            fl(8, ROWS),
            fl(7, 8, ROWS),
            bf(8, SHARE, ROWS),
            bf(8, SHARE, ROWS),
            fl(24, SHARE),
            fl(24, SHARE),
            fl(6, 24, SHARE),
            fl(8, 24, SHARE),
            *semaphores(160),
            pltpu.SemaphoreType.DMA((23,)),
        ],
        compiler_params=params(3, 63),
        name="back",
    )(*operands)


def shards(
    tokens,
    seq_lengths,
    expert_ids,
    first_gain,
    query_weight,
    key_matrix,
    value_matrix,
    query_bias,
    key_offset_bias,
    value_offset_bias,
    head_sink_logits,
    output_weight,
    output_bias,
    second_gain,
    router_weight,
    router_bias,
    expert_gateup,
    gateup_bias,
    expert_down,
    down_bias,
    cotangent,
):
    gap = jnp.zeros((WIDE - D,), F32)
    settings = jnp.concatenate(
        [
            output_bias, gap, second_gain, gap, first_gain, gap, query_bias, key_offset_bias, value_offset_bias,
            router_bias, jnp.zeros((112,), F32), head_sink_logits, jnp.zeros((248,), F32),
        ]
    ).reshape(80, 128)
    (
        queries, keys_values, log_total, first_scale, trig, allowed, bias_sums,
        grad_att, layer_share, small, grad_logits, scaled_hidden, grad_pre, expert_rows, cot_rows, normed_all, heads_all,
    ) = layer(
        seq_lengths, expert_ids.T, settings, gateup_bias[0], down_bias, tokens.T, cotangent.T, query_weight,
        key_matrix.T, value_matrix.T, output_weight.T, router_weight.T,
        jnp.swapaxes(expert_gateup[0], 1, 2), expert_down[0],
    )
    query_grad, key_value_grad, token_blocks, layer_t, small_all, small_own, output_blocks = back(
        grad_att, queries, keys_values, log_total, allowed, trig, first_scale, settings, small, grad_logits,
        layer_share, output_weight.T, query_weight, key_matrix.T, value_matrix.T, tokens.T, normed_all, heads_all,
    )
    (
        grad_gateup, grad_down, grad_down_bias, output_grad, query_out, key_out, value_out, tokens_out, layer_out,
        router_out, gains,
    ) = finish(
        expert_rows, cot_rows, scaled_hidden, grad_pre, output_blocks.reshape(WIDE, 512), query_grad,
        key_value_grad, token_blocks.reshape(WIDE, ROWS), layer_t, small_all,
    )
    lines = small_own.reshape(1024)
    return (
        layer_out.T,
        tokens_out.T,
        gains[2],
        query_out,
        key_out.T,
        value_out.T,
        lines[0:512],
        lines[512:576],
        lines[576:640],
        lines[768 : 768 + HEADS],
        output_grad.T,
        gains[1],
        gains[0],
        router_out.T,
        lines[640 : 640 + EXPERTS],
        jnp.swapaxes(grad_gateup, 1, 2)[None],
        jnp.stack([bias_sums[0, 0:FF_LOCAL], bias_sums[0, FF : FF + FF_LOCAL]])[None],
        grad_down[None],
        grad_down_bias,
    )


def solution(mesh):
    in_specs = (
        P("ep", None),
        P(),
        P("ep", None),
        P(),
        P(None, "tp"),
        P(None, "tp"),
        P(None, "tp"),
        P("tp"),
        P("tp"),
        P("tp"),
        P("tp"),
        P("tp", None),
        P(),
        P(),
        P(),
        P(),
        P("ep", None, None, "tp"),
        P("ep", None, "tp"),
        P("ep", "tp", None),
        P("ep", None),
        P("ep", None),
    )
    out_specs = (
        P("ep", None),
        P("ep", None),
        P(),
        P(None, "tp"),
        P(None, "tp"),
        P(None, "tp"),
        P("tp"),
        P("tp"),
        P("tp"),
        P("tp"),
        P("tp", None),
        P(),
        P(),
        P(),
        P(),
        P("ep", None, None, "tp"),
        P("ep", None, "tp"),
        P("ep", "tp", None),
        P("ep", None),
    )
    return jax.shard_map(shards, mesh=mesh, in_specs=in_specs, out_specs=out_specs, check_vma=False)
```

```python
import math

import jax
import jax.numpy as jnp
from jax import lax
from jax.experimental import pallas as pl
from jax.experimental.pallas import tpu as pltpu
from jax.sharding import PartitionSpec as P

HEAD_SIZE = 64
EPS = 1e-05
THETA = 150000.0
LIMIT = 7.0
ALPHA = 1.702
NEGATIVE = -1e30

D = 2880
FF_LOCAL = 360
SHARE = 384
BLOCKS = 8
WIDE = SHARE * BLOCKS
ROWS = 128
EXPERTS = 16
CAP = 48
SLOTS = EXPERTS * CAP
HALF = SLOTS // 2
HEADS = 8
FF = 384
QUARTER = SLOTS // 4
MESH = pl.DeviceIdType.MESH
F32 = jnp.float32
BF16 = jnp.bfloat16
HIGHEST = lax.Precision.HIGHEST


def product(left, right):
    return jnp.dot(left, right, preferred_element_type=F32)


def contract_rows(left, right):
    return lax.dot_general(left, right, (((0,), (0,)), ((), ())), preferred_element_type=F32)


def against_rows(left, right):
    return lax.dot_general(left, right, (((1,), (1,)), ((), ())), preferred_element_type=F32)


def exact(left, right, left_dim=1, right_dim=0):
    return lax.dot_general(
        left,
        right,
        (((left_dim,), (right_dim,)), ((), ())),
        preferred_element_type=F32,
        precision=HIGHEST,
    )


def row_sums(columns):
    return exact(jnp.ones((8, columns.shape[1]), F32), columns, 1, 1)


class Place:
    def __init__(self):
        self.ep = lax.axis_index("ep")
        self.tp = lax.axis_index("tp")
        self.z, self.x = self.ep // 4, self.ep % 4
        self.y, self.core = self.tp // 2, self.tp % 2

    def sibling(self):
        return (self.ep, self.y * 2 + (1 - self.core))

    def along_y(self, step):
        return (self.ep, lax.rem(self.y + step, 4) * 2 + self.core)

    def along_tp(self, step):
        return (self.ep, lax.rem(self.tp + step, 8))

    def along_ep(self, k):
        z = lax.rem(self.z + k // 4, 4)
        x = lax.rem(self.x + k % 4, 4)
        return (z * 4 + x, self.tp)

    def back_ep(self, k):
        z = lax.rem(self.z + 4 - k // 4, 4)
        x = lax.rem(self.x + 4 - k % 4, 4)
        return (z * 4 + x, self.tp)

    def greet(self, tp, ep):
        barrier = pltpu.get_barrier_semaphore()
        partners = [self.along_tp(i) for i in range(1, 8) if tp]
        partners += [self.along_ep(k) for k in range(1, 16) if ep]
        for device in partners:
            pl.semaphore_signal(barrier, inc=1, device_id=device, device_id_type=MESH)
        return lambda: pl.semaphore_wait(barrier, len(partners))


class Sender:
    def __init__(self, me, send_sems, recv_sems):
        self.me, self.send_sems, self.recv_sems = me, send_sems, recv_sems
        self.used = 0
        self.open = []

    def start(self, source, target, device):
        n = self.used
        self.used += 1
        copy = pltpu.make_async_remote_copy(
            src_ref=source,
            dst_ref=target,
            send_sem=self.send_sems.at[n],
            recv_sem=self.recv_sems.at[n],
            device_id=device,
            device_id_type=MESH,
        )
        copy.start()
        self.open.append(copy)
        return n

    def arrived(self, n, target):
        pltpu.make_async_remote_copy(
            src_ref=target,
            dst_ref=target,
            send_sem=self.send_sems.at[n],
            recv_sem=self.recv_sems.at[n],
            device_id=self.me.sibling(),
            device_id_type=MESH,
        ).wait_recv()

    def finish(self):
        for copy in self.open:
            copy.wait_send()
        self.open = []


class GroupGather:
    def __init__(self, me, send, buffer, lines, shared, first=None):
        self.me, self.send, self.buffer, self.shared = me, send, buffer, shared
        first = first or lines // (4 if shared else 2)
        self.sizes = (first, lines // (2 if shared else 1) - first)
        self.tickets, self.passed = {}, {}

    def span(self, part, core, piece=None):
        start, size = (0, self.sizes[0])[part], self.sizes[part]
        if self.shared:
            start = core * sum(self.sizes) + start
        cut = size // 32 * 16
        if piece == 0:
            size = cut
        if piece == 1:
            start, size = start + cut, size - cut
        return pl.ds(pl.multiple_of(start, 16), size)

    def groups(self, part, phase, j):
        unit = 1 if (part + phase) % 2 == 0 else 4
        if phase == 0:
            return [j * unit]
        if part == 0:
            return [slice(4 * j, 4 * j + 4)]
        return [4 * i + j for i in range(4)]

    def move(self, name, part, phase, source, target, piece=None):
        unit = 1 if (part + phase) % 2 == 0 else 4
        span = self.span(part, self.me.core, piece)
        step = (target - source) % 4
        self.tickets[name, part, phase] = [
            self.send.start(
                self.buffer.at[a, span], self.buffer.at[b, span], self.me.along_ep(unit * step)
            )
            for a, b in zip(self.groups(part, phase, source), self.groups(part, phase, target))
        ]

    def wait(self, name, part, phase, j, piece=None):
        span = self.span(part, self.me.core, piece)
        for n, slots in zip(self.tickets[name, part, phase], self.groups(part, phase, j)):
            self.send.arrived(n, self.buffer.at[slots, span])

    def begin(self, phase=0):
        for part in (0, 1):
            self.move("right", part, phase, 0, 1)
            self.move("left", part, phase, 0, 3)

    def near(self, phase=0):
        for part in (0, 1):
            self.wait("right", part, phase, 1)
            self.wait("left", part, phase, 3)

    def relay(self, phase=0, waited=False):
        if not waited:
            self.near(phase)
        for part in (0, 1):
            self.move("far right", part, phase, 1, 2, 0)
            self.move("far left", part, phase, 3, 2, 1)

    def meet(self, phase=0):
        for part in (0, 1):
            self.wait("far right", part, phase, 2, 0)
            self.wait("far left", part, phase, 2, 1)

    def shares(self, j):
        low = 1 if j == 0 else 0
        return [(0, slice(4 * j + low, 4 * j + 4))] + [(1, 4 * i + j) for i in range(low, 4)]

    def pass_on(self, j):
        self.passed[j] = []
        for part, slots in self.shares(j):
            block = self.buffer.at[slots, self.span(part, self.me.core)]
            self.passed[j].append(self.send.start(block, block, self.me.sibling()))

    def complete(self, j):
        for n, (part, slots) in zip(self.passed[j], self.shares(j)):
            self.send.arrived(n, self.buffer.at[slots, self.span(part, 1 - self.me.core)])


def column_of(row):
    return jnp.transpose(jnp.broadcast_to(row, (128, 128)))


def column_share(settings, first, me):
    return jnp.concatenate(
        [column_of(settings[pl.ds(first + me.tp * 3 + j, 1), :]) for j in range(3)], axis=0
    )


def share_blocks(part, emit):
    for q in range(BLOCKS):
        lo = q * SHARE
        width = min(SHARE, D - lo)
        block = part(lo, width)
        if width < SHARE:
            block = jnp.concatenate(
                [block, jnp.zeros((SHARE - width, block.shape[1]), block.dtype)], axis=0
            )
        emit(q, block)


class ReduceShares:
    order = (2, 1, 3, 0)

    def __init__(self, me, send, part, from_sibling, sums, from_y):
        self.me, self.send, self.part = me, send, part
        self.from_sibling, self.sums, self.from_y = from_sibling, sums, from_y
        self.tickets = [
            send.start(part.at[self.at(step) + 1 - me.core], from_sibling.at[i], me.sibling())
            for i, step in enumerate(self.order)
        ]

    def at(self, step):
        return lax.rem(self.me.y + step, 4) * 2

    def pair(self):
        self.landed = []
        for i, step in enumerate(self.order):
            self.send.arrived(self.tickets[i], self.from_sibling.at[i])
            total = self.part[self.at(step) + self.me.core].astype(F32) + self.from_sibling[
                i
            ].astype(F32)
            if step:
                self.sums[i] = total.astype(BF16)
                self.landed.append(
                    self.send.start(self.sums.at[i], self.from_y.at[i], self.me.along_y(step))
                )
        self.total = total

    def end(self):
        for i, n in enumerate(self.landed):
            self.send.arrived(n, self.from_y.at[i])
            self.total = self.total + self.from_y[i].astype(F32)
        return self.total


class Exchange:
    def __init__(self, me, send, own, others):
        self.send, self.own, self.others = send, own, others
        self.tickets = [send.start(own, others.at[i - 1], me.along_tp(i)) for i in range(1, 8)]

    def end(self):
        total = self.own[...]
        for i, n in enumerate(self.tickets):
            self.send.arrived(n, self.others.at[i])
            total = total + self.others[i]
        return total


def start_gather_shares(me, send, blocks):
    own = blocks.at[me.tp]
    to_y = [send.start(own, own, me.along_y(step)) for step in (2, 1, 3)]
    to_sibling = [send.start(own, own, me.sibling())]

    def end():
        for n, step in zip(to_y, (2, 1, 3)):
            block = blocks.at[lax.rem(me.y + 4 - step, 4) * 2 + me.core]
            send.arrived(n, block)
            to_sibling.append(send.start(block, block, me.sibling()))
        for n, step in zip(to_sibling, (0, 2, 1, 3)):
            send.arrived(n, blocks.at[lax.rem(me.y + 4 - step, 4) * 2 + 1 - me.core])

    return end


class RowsHome:
    def __init__(self, me, send, sums, far_in, near_in, home):
        self.me, self.send, self.sums = me, send, sums
        self.far_in, self.near_in, self.home = far_in, near_in, home
        self.far, self.early, self.late, self.tickets = {}, {}, {}, {}

    def piece_of(self, h, piece):
        return pl.ds(h * HALF + piece * QUARTER, QUARTER)

    def near_part(self, h, y, piece, step_y, direction):
        return self.send.start(
            self.sums.at[y, self.piece_of(h, piece)],
            self.near_in.at[h, direction, pl.ds(piece * QUARTER, QUARTER)],
            self.me.along_y(step_y),
        )

    def begin(self, h, s, y):
        if s == 2:
            self.far[h] = [
                self.send.start(
                    self.sums.at[y, self.piece_of(h, piece)],
                    self.far_in.at[h, piece],
                    self.me.along_y(step_y),
                )
                for piece, step_y in ((0, 1), (1, 3))
            ]
        elif s:
            direction = 0 if s == 1 else 1
            self.early[h, direction] = self.near_part(h, y, 1 - direction, s, direction)

    def sums_on(self, h):
        for piece, step_y in ((0, 1), (1, 3)):
            y = lax.rem(self.me.y + step_y, 4)
            half = self.piece_of(h, piece)
            self.send.arrived(self.far[h][piece], self.far_in.at[h, piece])
            self.sums[y, half, :] = (
                self.sums[y, half, :].astype(F32) + self.far_in[h, piece].astype(F32)
            ).astype(BF16)
            self.late[h, piece] = self.near_part(h, y, piece, step_y, piece)

    def go_home(self, h):
        me, lines = self.me, pl.ds(h * HALF, HALF)
        total = self.sums[me.y, lines, :].astype(F32)
        for direction in (0, 1):
            for ticket, piece in (
                (self.early[h, direction], 1 - direction),
                (self.late[h, direction], direction),
            ):
                self.send.arrived(
                    ticket, self.near_in.at[h, direction, pl.ds(piece * QUARTER, QUARTER)]
                )
            total = total + self.near_in[h, direction].astype(F32)
        self.sums[me.y, lines, :] = total.astype(BF16)
        for k in range(8):
            span = pl.ds((8 * h + k) * CAP, CAP)
            place = pl.ds(k * CAP, CAP)
            if 8 * h + k:
                self.tickets[h, k] = self.send.start(
                    self.sums.at[me.y, span], self.home.at[h, place], me.back_ep(8 * h + k)
                )
            else:
                self.home[0, 0:CAP, :] = self.sums[me.y, 0:CAP, :]

    def is_home(self, h):
        for k in range(8):
            if 8 * h + k:
                self.send.arrived(self.tickets[h, k], self.home.at[h, pl.ds(k * CAP, CAP)])


def vmem(count):
    return [pl.BlockSpec(memory_space=pltpu.VMEM)] * count


def hbm(count):
    return [pl.BlockSpec(memory_space=pl.ANY)] * count


def semaphores(count):
    return [pltpu.SemaphoreType.DMA((count,)), pltpu.SemaphoreType.DMA((count,))]


def params(number, megabytes):
    return pltpu.CompilerParams(
        collective_id=number, has_side_effects=True, vmem_limit_bytes=megabytes * 2**20
    )


shape = jax.ShapeDtypeStruct


OUTPUT_BIAS, SECOND_GAIN, FIRST_GAIN, HEAD_BIASES, ROUTER_BIAS, SINKS = 0, 24, 48, 72, 77, 78


def turned(me):
    k = lax.broadcasted_iota(jnp.int32, (EXPERTS, EXPERTS), 0)
    e = lax.broadcasted_iota(jnp.int32, (EXPERTS, EXPERTS), 1)
    name = ((me.z + (k >> 2)) & 3) * 4 + ((me.x + (k & 3)) & 3)
    return (name == e).astype(F32)


def rotate(pair, trig, back=False):
    first, last = pair[0:32], pair[32:64]
    cosine, sine = trig[0:32, :], trig[32:64, :]
    if back:
        sine = -sine
    return jnp.concatenate([first * cosine - last * sine, last * cosine + first * sine], axis=0)


def documents(index, first_end, second_end):
    return (index >= first_end).astype(jnp.int32) + (index >= second_end).astype(jnp.int32)


def activation_parts(gate_pre, up_pre):
    lowered = LIMIT - gate_pre
    cap = jnp.maximum(lowered, 0.0) + jnp.log(1.0 + jnp.exp(-jnp.abs(lowered)))
    capped_gate = LIMIT - cap
    tanh = jnp.tanh(up_pre * (1.0 / LIMIT))
    capped_up = LIMIT * tanh
    sigmoid = 1.0 / (1.0 + jnp.exp(-ALPHA * capped_gate))
    return lowered, capped_gate, tanh, capped_up, sigmoid


def layer_kernel(
    lengths, ids, output_bias, second_gain, first_gain, query_bias, key_bias, value_bias, router_bias, sink_logits,
    gateup_bias, down_bias,
    tokens, cotangent, query_weight, key_weight, value_weight, output_weight, router, gateup, down,
    queries, keys_values, log_total, first_scale, trig, allowed, bias_sums,
    grad_att_out, mixed_out, high_out, low_out, small_out, grad_logits_out,
    settings, results_out, scaled_out, grad_pre_out, rows_out, cots_out, normed_all, heads_all,
    wide_tokens, wide_cot, wide_normed, wide_router, wq, wk, wv, wo, router_in, unpadded, wide_gateup, wide_down,
    wide_bias,
    selector, heads, mixed, second, stat, part, part_sibling, part_sums, part_y, stat_own, stats,
    R, C, staged, staged_c, staged_near, gates_send, gates, gate_sums_send, gate_sums, pre, hidden, raw_sums, grad_pre,
    to_sibling, from_sibling, sums, far_in, near_in, home, scaled, scaled_grad, blocks,
    send_sems, recv_sems, local_sems,
):
    me = Place()
    send = Sender(me, send_sems, recv_sems)
    all_here = me.greet(True, True)

    def load(source, target, n):
        copy = pltpu.make_async_copy(source, target, local_sems.at[n])
        copy.start()
        return copy

    load_cot = load(cotangent, wide_cot.at[0:D], 0)
    load_tokens = load(tokens, wide_tokens.at[0:D], 1)
    load_query = load(query_weight, wq, 2)
    load_pair = [load(key_weight, wk, 3), load(value_weight, wv, 4)]
    load_output = load(output_weight, wo, 5)
    load_router = load(router, router_in, 6)
    def place_weights(target, first):
        for q in range(BLOCKS):
            width = min(SHARE, D - q * SHARE)
            to = (q % 2 * 4 + q // 2) * SHARE
            target[first : first + FF_LOCAL, to : to + width] = unpadded[
                :, q * SHARE : q * SHARE + width
            ]

    def block_at(core, y):
        return core * 4 + y

    settings[...] = jnp.zeros((80, 128), F32)
    for first, vector in (
        (OUTPUT_BIAS, output_bias), (SECOND_GAIN, second_gain), (FIRST_GAIN, first_gain), (HEAD_BIASES, query_bias),
        (ROUTER_BIAS, router_bias), (SINKS, sink_logits),
    ):
        count = vector.shape[0]
        for j in range(0, count, 128):
            width = min(128, count - j)
            settings[first + j // 128, 0:width] = vector[j : j + width]
    settings[HEAD_BIASES + 4, 0:64] = key_bias[...]
    settings[HEAD_BIASES + 4, 64:128] = value_bias[...]
    mine = pl.ds(pl.multiple_of(me.tp * SHARE, SHARE), SHARE)
    own = block_at(me.core, me.y)
    for buffer in (wide_cot, wide_tokens):
        buffer[D:, :] = jnp.zeros((WIDE - D, ROWS), BF16)

    k = lax.broadcasted_iota(jnp.int32, (EXPERTS, ROWS), 0)
    name = ((me.z + (k >> 2)) & 3) * 4 + ((me.x + (k & 3)) & 3)
    chosen = jnp.zeros((EXPERTS, ROWS), F32)
    for j in range(4):
        chosen = chosen + (name == ids[j : j + 1, :]).astype(F32)
    taken = chosen > 0.5
    column = lax.broadcasted_iota(jnp.int32, (ROWS, ROWS), 0)
    row = lax.broadcasted_iota(jnp.int32, (ROWS, ROWS), 1)
    rank = product(chosen.astype(BF16), (column < row).astype(F32).astype(BF16))
    rank = jnp.where(taken, rank, -1.0)
    place = lax.broadcasted_iota(jnp.int32, (CAP, ROWS), 0).astype(F32)
    for k in range(EXPERTS):
        selector[k * CAP : (k + 1) * CAP, :] = (
            (place == rank[k : k + 1, :]).astype(F32).astype(BF16)
        )
    load_cot.wait()
    staged_c[...] = against_rows(selector[HALF:, :], wide_cot[mine, :]).astype(BF16)
    for y in range(4):
        span = pl.ds(pl.multiple_of((2 * y + me.core) * SHARE, SHARE), SHARE)
        staged_near[y] = against_rows(selector[0:HALF, :], wide_cot[span, :]).astype(BF16)
    all_here()

    def lines_at(j, piece=None):
        if piece is None:
            return pl.ds(j * QUARTER, QUARTER)
        return pl.ds(j * QUARTER + piece * (QUARTER // 2), QUARTER // 2)

    def back_y(buffer, step, lines, core):
        return buffer.at[block_at(core, lax.rem(me.y + 4 - step, 4)), lines]

    def spread(buffer, tickets, j):
        for k in range(4 * j, 4 * j + 4):
            if k:
                send.arrived(tickets[k], buffer.at[own, pl.ds(k * CAP, CAP)])
        source = buffer.at[own, lines_at(j)]
        return {
            1: send.start(source, source, me.along_y(1)),
            3: send.start(source, source, me.along_y(3)),
            "sibling": [send.start(source, source, me.sibling())],
        }

    def pass_on(buffer, tickets, j):
        for step, piece in ((1, 0), (3, 1)):
            block = back_y(buffer, step, lines_at(j), me.core)
            send.arrived(tickets[step], block)
            block_half = back_y(buffer, step, lines_at(j, piece), me.core)
            tickets[2, piece] = send.start(block_half, block_half, me.along_y(step))
            tickets["sibling"].append(send.start(block, block, me.sibling()))

    def pass_far(buffer, tickets, j):
        for piece in (0, 1):
            send.arrived(tickets[2, piece], back_y(buffer, 2, lines_at(j, piece), me.core))
        block = back_y(buffer, 2, lines_at(j), me.core)
        tickets["sibling"].append(send.start(block, block, me.sibling()))

    def complete(buffer, tickets, j):
        for n, step in zip(tickets["sibling"], (0, 1, 3, 2)):
            send.arrived(n, back_y(buffer, step, lines_at(j), 1 - me.core))

    half_blocks = pl.ds(me.core * 4, 4)
    other_blocks = pl.ds((1 - me.core) * 4, 4)
    cots_in = [None] * EXPERTS
    for k in range(8, EXPERTS):
        cots_in[k] = send.start(
            staged_c.at[(k - 8) * CAP : (k - 7) * CAP],
            C.at[own, k * CAP : (k + 1) * CAP],
            me.along_ep(k),
        )
    for k in range(1, 8):
        lines = slice(k * CAP, (k + 1) * CAP)
        cots_in[k] = send.start(
            staged_near.at[:, lines], C.at[half_blocks, lines], me.along_ep(k)
        )
    C[half_blocks, 0:CAP, :] = staged_near[:, 0:CAP, :]

    load_tokens.wait()

    def squares(j, total):
        lines = wide_tokens[pl.ds(pl.multiple_of(j * 96, 96), 96), :].astype(F32)
        return total + jnp.sum(lines * lines, axis=0, keepdims=True)

    scale = lax.rsqrt(lax.fori_loop(0, 30, squares, jnp.zeros((1, ROWS), F32)) * (1.0 / D) + EPS)
    first_scale[...] = jnp.broadcast_to(scale, (8, ROWS))

    @pl.loop(0, 24)
    def _(j):
        span = pl.ds(pl.multiple_of(j * 128, 128), 128)
        gain = column_of(settings[pl.ds(FIRST_GAIN + j, 1), :])
        wide_normed[span, :] = (wide_tokens[span, :].astype(F32) * scale * gain).astype(BF16)

    keep_normed = load(wide_normed.at[0:D], normed_all.at[0], 10)
    first_end = lengths[0, me.ep]
    second_end = first_end + lengths[1, me.ep]
    index = lax.broadcasted_iota(jnp.int32, (1, ROWS), 1)
    document = documents(index, first_end, second_end)
    start = jnp.where(document == 0, 0, jnp.where(document == 1, first_end, second_end))
    positions = (index - start).astype(F32)
    exponent = lax.broadcasted_iota(jnp.int32, (32, ROWS), 0).astype(F32)
    angles = jnp.exp(exponent * (-math.log(THETA) / 32.0)) * positions
    trig[0:32, :] = jnp.cos(angles)
    trig[32:64, :] = jnp.sin(angles)
    included = (
        documents(column, first_end, second_end) == documents(row, first_end, second_end)
    ) & (column <= row)
    allowed[...] = included.astype(F32)
    load_query.wait()
    query_rows = contract_rows(wide_normed[0:D, :], wq[...])
    for copy in load_pair:
        copy.wait()
    both = jnp.concatenate(
        [product(wk[...], wide_normed[0:D, :]), product(wv[...], wide_normed[0:D, :])], axis=0
    ) + column_of(settings[HEAD_BIASES + 4 : HEAD_BIASES + 5, :])
    both = jnp.concatenate([rotate(both[0:64], trig), both[64:128]], axis=0)
    keys_values[...] = both.astype(BF16)
    key_rows = jnp.transpose(both)[:, 0:64].astype(BF16)
    for j in range(4):
        pair = jnp.transpose(query_rows[:, j * 128 : (j + 1) * 128]) + column_of(
            settings[HEAD_BIASES + j : HEAD_BIASES + j + 1, :]
        )
        queries[j * 128 : j * 128 + 64, :] = rotate(pair[0:64], trig).astype(BF16)
        queries[j * 128 + 64 : j * 128 + 128, :] = rotate(pair[64:128], trig).astype(BF16)
    b = [None] * 4
    b[2] = spread(C, cots_in, 2)
    b[3] = spread(C, cots_in, 3)
    keep_normed.wait()
    all_normed = GroupGather(me, send, normed_all, D, True)
    all_normed.begin()
    sinks = column_of(settings[SINKS : SINKS + 1, :])

    def attend(h):
        scores = product(key_rows, queries[h * 64 : h * 64 + 64, :]) * (HEAD_SIZE**-0.5)
        scores = jnp.where(included, scores, NEGATIVE)
        sink = sinks[h : h + 1, :]
        highest = jnp.maximum(jnp.max(scores, axis=0, keepdims=True), sink)
        total = jnp.exp(sink - highest) + jnp.sum(
            jnp.exp(scores - highest), axis=0, keepdims=True
        )
        logs = highest + jnp.log(total)
        log_total[h : h + 1, :] = logs
        probs = jnp.exp(scores - logs).astype(BF16)
        heads[h * 64 : h * 64 + 64, :] = product(keys_values[64:128, :], probs).astype(BF16)

    for h in range(4):
        attend(h)
    pass_on(C, b[2], 2)
    for h in range(4, HEADS):
        attend(h)
    pass_on(C, b[3], 3)
    keep_heads = load(heads, heads_all.at[0], 11)
    load_output.wait()
    load_expert = load(gateup.at[0], unpadded, 7)

    def emit(q, block):
        part[q] = block.astype(BF16)

    share_blocks(lambda lo, width: product(wo[lo : lo + width, :], heads[...]), emit)
    reduction = ReduceShares(me, send, part, part_sibling, part_sums, part_y)
    turn = turned(me)
    load_router.wait()
    wide_router[:, 0:D] = product(turn.astype(BF16), router_in[...]).astype(BF16)
    wide_router[:, D:] = jnp.zeros((EXPERTS, WIDE - D), BF16)
    router_share = wide_router[:, mine]
    base = wide_tokens[mine, :].astype(F32) + column_share(settings, OUTPUT_BIAS, me)
    gain = column_share(settings, SECOND_GAIN, me)
    reduction.pair()
    wide_gateup[...] = jnp.zeros((2 * FF, WIDE), BF16)
    wide_down[...] = jnp.zeros((FF, WIDE), BF16)
    load_expert.wait()
    place_weights(wide_gateup, 0)
    load_expert = load(gateup.at[1], unpadded, 7)
    mixed[...] = base + reduction.end()

    raised = (mixed[...] * gain).astype(BF16)
    second[...] = raised
    staged[...] = against_rows(selector[...], raised).astype(BF16)
    rows_in = [None]
    for k in range(1, EXPERTS):
        lines = pl.ds(k * CAP, CAP)
        rows_in.append(send.start(staged.at[lines], R.at[own, lines], me.along_ep(k)))
    R[own, 0:CAP, :] = staged[0:CAP, :]
    stat_own[0, 0:16, :] = product(router_share, raised)
    stat_own[0, 16:24, :] = jnp.broadcast_to(
        jnp.sum(mixed[...] * mixed[...], axis=0, keepdims=True), (8, ROWS)
    )
    exchanged = Exchange(me, send, stat_own.at[0], stats.at[0:7])
    pass_far(C, b[2], 2)
    pass_far(C, b[3], 3)
    load_expert.wait()
    place_weights(wide_gateup, FF)
    load_expert = load(down, unpadded, 7)
    a = [None] * 4
    a[0] = spread(R, rows_in, 0)
    def lines_of(h):
        return pl.ds(h * HALF, HALF)

    def wide_rows(buffer, lines, first, count):
        return jnp.concatenate([buffer[q, lines, :] for q in range(first, first + count)], axis=1)

    def raw_rows(h):
        raw_sums[lines_of(h), :] = against_rows(wide_rows(C, lines_of(h), 0, 8), wide_down[...])

    a[1] = spread(R, rows_in, 1)
    total = exchanged.end()
    scale = lax.rsqrt(total[16:17, :] * (1.0 / D) + EPS)
    plain = total[0:16, :] * scale
    logits = plain + exact(
        turn, column_of(settings[ROUTER_BIAS : ROUTER_BIAS + 1, :])[0:EXPERTS]
    )
    highest = jnp.max(jnp.where(taken, logits, NEGATIVE), axis=0, keepdims=True)
    lifted = jnp.where(taken, jnp.exp(jnp.where(taken, logits, highest) - highest), 0.0)
    stat[0:16, :] = lifted / jnp.sum(lifted, axis=0, keepdims=True)
    stat[16:32, :] = plain
    stat[32:40, :] = jnp.broadcast_to(scale, (8, ROWS))
    a[2] = spread(R, rows_in, 2)
    pass_on(R, a[0], 0)
    a[3] = spread(R, rows_in, 3)
    pass_on(R, a[1], 1)
    load_expert.wait()
    place_weights(wide_down, 0)
    bias_row = down_bias[...] * jnp.where(me.tp == 0, 1.0, 0.0)
    bias_high = bias_row.astype(BF16)
    bias_low = (bias_row - bias_high.astype(F32)).astype(BF16)
    line = lax.broadcasted_iota(jnp.int32, (16, D), 0)
    bias_lines = jnp.where(
        line == 8,
        jnp.broadcast_to(bias_high.astype(F32), (16, D)),
        jnp.where(line == 9, jnp.broadcast_to(bias_low.astype(F32), (16, D)), 0.0),
    ).astype(BF16)
    for q in range(BLOCKS):
        width = min(SHARE, D - q * SHARE)
        to = (q % 2 * 4 + q // 2) * SHARE
        lines = bias_lines[:, q * SHARE : q * SHARE + width]
        old = wide_down[352:368, to : to + width]
        wide_down[352:368, to : to + width] = (old.astype(F32) + lines.astype(F32)).astype(BF16)
    all_normed.relay()
    chosen_rows = selector[...].astype(F32)
    spread_gates = jnp.concatenate(
        [jnp.broadcast_to(stat[k : k + 1, :], (CAP, 128)) for k in range(EXPERTS)], axis=0
    )
    slot_gates = row_sums(spread_gates * chosen_rows)
    slot_scales = exact(jnp.broadcast_to(scale, (8, ROWS)), chosen_rows, 1, 1)
    gates_in = [None]
    for k in range(EXPERTS):
        lines = slice(k * CAP, (k + 1) * CAP)
        pair = jnp.concatenate([slot_gates[0:4, lines], slot_scales[0:4, lines]], axis=0)
        gates_send[k] = jnp.concatenate([pair, jnp.zeros((8, 128 - CAP), F32)], axis=1)
        if k:
            gates_in.append(send.start(gates_send.at[k], gates.at[k], me.along_ep(k)))
    gates[0] = gates_send[0]
    keep_heads.wait()
    all_heads = GroupGather(me, send, heads_all, 512, False)
    all_heads.begin()
    for k in range(1, 8):
        send.arrived(cots_in[k], C.at[half_blocks, k * CAP : (k + 1) * CAP])
    near_cots = C.at[half_blocks, 0:HALF]
    near_shared = send.start(near_cots, near_cots, me.sibling())
    complete(C, b[2], 2)
    complete(C, b[3], 3)
    raw_rows(1)
    pass_on(R, a[2], 2)
    pass_far(R, a[0], 0)
    all_normed.meet()
    all_normed.begin(1)
    pass_on(R, a[3], 3)
    pass_far(R, a[1], 1)
    all_heads.relay()
    send.arrived(near_shared, C.at[other_blocks, 0:HALF])
    cots_copy = load(C, cots_out, 12)
    raw_rows(0)
    wide_bias[...] = jnp.zeros((1, 2 * FF), F32)
    wide_bias[:, 0:FF_LOCAL] = gateup_bias[0:1, :]
    wide_bias[:, FF : FF + FF_LOCAL] = gateup_bias[1:2, :]

    def columns_of(what, h):
        return jnp.concatenate(
            [what[0:CAP, k : k + 1] for k in range(8 * h, 8 * h + 8)], axis=0
        )

    unit = lax.broadcasted_iota(jnp.int32, (1, FF), 1)

    def forward(h):
        lines = lines_of(h)
        pre[lines, :] = against_rows(wide_rows(R, lines, 0, 4), wide_gateup[:, 0 : 4 * SHARE])
        pre[lines, :] = (
            pre[lines, :]
            + against_rows(wide_rows(R, lines, 4, 4), wide_gateup[:, 4 * SHARE :])
        ) * columns_of(scale_cols, h) + wide_bias[...]
        _, capped_gate, _, capped_up, sigmoid = activation_parts(
            pre[lines, 0:FF], pre[lines, FF:]
        )
        value = (capped_up + 1.0) * capped_gate * sigmoid
        hidden[lines, :] = jnp.where(
            unit < FF_LOCAL, value, jnp.where(unit < FF_LOCAL + 2, 1.0, 0.0)
        ).astype(BF16)

    def to_home(n, h, left, weights):
        lines = lines_of(h)
        theirs = pl.ds(pl.multiple_of((1 - me.core) * 4 * SHARE, SHARE), 4 * SHARE)
        ours = pl.ds(pl.multiple_of(me.core * 4 * SHARE, SHARE), 4 * SHARE)
        value = product(left, weights[:, theirs]).astype(BF16)
        for y in range(4):
            to_sibling[n // 2, y, lines, :] = value[:, y * SHARE : (y + 1) * SHARE]
        sent = []
        for s in (2, 1, 3, 0):
            block = (n // 2, lax.rem(me.y + s, 4), lines)
            sent.append(
                send.start(to_sibling.at[block], from_sibling.at[block], me.sibling())
            )
        value = product(left, weights[:, ours]).astype(BF16)
        for y in range(4):
            sums[n // 2, y, lines, :] = value[:, y * SHARE : (y + 1) * SHARE]
        return sent

    def add_sibling(n, h, sent):
        lines = lines_of(h)
        for s, ticket in zip((2, 1, 3, 0), sent):
            y = lax.rem(me.y + s, 4)
            send.arrived(ticket, from_sibling.at[n // 2, y, lines])
            sums[n // 2, y, lines, :] = (
                sums[n // 2, y, lines, :].astype(F32) + from_sibling[n // 2, y, lines, :].astype(F32)
            ).astype(BF16)
            yield s, y

    def pair_up(h, sent):
        for s, y in add_sibling(2, h, sent):
            grads.begin(h, s, y)

    def backward(h):
        lines = lines_of(h)
        gate = columns_of(gate_cols, h)
        raw = raw_sums[lines, :]
        lowered, capped_gate, tanh, capped_up, sigmoid = activation_parts(
            pre[lines, 0:FF], pre[lines, FF:]
        )
        units = hidden[lines, :].astype(F32)
        slot_sums = row_sums(units * raw)
        grad_hidden = jnp.where(unit < FF_LOCAL, gate * raw, 0.0)
        high = gate.astype(BF16).astype(F32)
        scaled[lines, :] = jnp.where(
            unit < FF_LOCAL,
            gate * units,
            jnp.where(unit == FF_LOCAL, high, jnp.where(unit == FF_LOCAL + 1, gate - high, 0.0)),
        ).astype(BF16)
        slope = (capped_up + 1.0) * (
            sigmoid + ALPHA * capped_gate * sigmoid * (1.0 - sigmoid)
        )
        grad_gate = (grad_hidden * slope * (1.0 / (1.0 + jnp.exp(-lowered)))).astype(BF16)
        grad_up = (grad_hidden * capped_gate * sigmoid * (1.0 - tanh * tanh)).astype(BF16)
        grad_pre[lines, 0:FF] = grad_gate
        grad_pre[lines, FF:] = grad_up
        sent = to_home(2, h, grad_pre[lines, :], wide_gateup)
        row_scale = columns_of(scale_cols, h)
        values = grad_pre[lines, :].astype(F32)
        scaled_grad[lines, :] = (values * row_scale).astype(BF16)
        total = jnp.sum(values, axis=0, keepdims=True)
        if h == 0:
            bias_sums[0:1, :] = total
        else:
            bias_sums[0:1, :] = bias_sums[0:1, :] + total
        tickets = []
        for k in range(8 * h, 8 * h + 8):
            first = (k - 8 * h) * CAP
            gate_sums_send[k] = jnp.concatenate(
                [slot_sums[:, first : first + CAP], jnp.zeros((8, 128 - CAP), F32)], axis=1
            )
            if k:
                tickets.append(
                    send.start(gate_sums_send.at[k], gate_sums.at[k], me.back_ep(k))
                )
            else:
                tickets.append(None)
                gate_sums[0] = gate_sums_send[0]
        return sent, tickets

    grads = RowsHome(me, send, sums.at[1], far_in, near_in, home)
    bias_sums[...] = jnp.zeros((8, 2 * FF), F32)
    for k in range(1, EXPERTS):
        send.arrived(gates_in[k], gates.at[k])
    spare = jnp.zeros((128 - EXPERTS, 128), F32)
    gate_cols = jnp.transpose(jnp.concatenate([gates[:, 0, :], spare], axis=0))
    scale_cols = jnp.transpose(jnp.concatenate([gates[:, 4, :], spare], axis=0))
    complete(R, a[0], 0)
    complete(R, a[1], 1)
    forward(0)
    pass_far(R, a[2], 2)
    pass_far(R, a[3], 3)
    sent_0, sums_in = backward(0)
    pair_up(0, sent_0)
    complete(R, a[2], 2)
    complete(R, a[3], 3)
    rows_copy = load(R, rows_out, 13)
    forward(1)
    all_heads.meet()
    all_heads.begin(1)
    grads.sums_on(0)
    sent_1, more = backward(1)
    sums_in = sums_in + more
    pair_up(1, sent_1)
    grads.go_home(0)
    all_heads.relay(1)
    all_normed.near(1)
    all_normed.pass_on(0)
    all_normed.pass_on(1)
    all_normed.pass_on(3)
    keep_scaled = [load(scaled, scaled_out, 14), load(scaled_grad, grad_pre_out, 15)]
    results_0 = to_home(0, 0, hidden[lines_of(0), :], wide_down)
    grads.sums_on(1)
    results_1 = to_home(0, 1, hidden[lines_of(1), :], wide_down)
    weighted = chosen_rows * spread_gates
    high = weighted.astype(BF16)
    high_out[...] = high
    low_out[...] = (weighted - high.astype(F32)).astype(BF16)
    mixed_out[...] = mixed[...]
    for h, sent in ((0, results_0), (1, results_1)):
        for _ in add_sibling(0, h, sent):
            pass
    grads.go_home(1)
    keep_scaled.append(load(sums.at[0], results_out, 16))

    gain = column_share(settings, SECOND_GAIN, me)
    scale = stat[32:33, :]
    normal = mixed[...] * scale
    for k in range(1, EXPERTS):
        send.arrived(sums_in[k], gate_sums.at[k])
    slots = jnp.transpose(jnp.concatenate([gate_sums[:, 0, :], spare], axis=0))
    for k in range(EXPERTS):
        stat_own[1, k : k + 1, :] = jnp.sum(
            chosen_rows[k * CAP : (k + 1) * CAP] * slots[0:CAP, k : k + 1], axis=0, keepdims=True
        )
    grads.is_home(0)
    returned = contract_rows(home[0], selector[0:HALF, :])
    grads.is_home(1)
    all_normed.relay(1, True)
    returned = returned + contract_rows(home[1], selector[HALF:, :])
    stat_own[1, 16:24, :] = jnp.broadcast_to(
        jnp.sum(returned * gain * normal, axis=0, keepdims=True), (8, ROWS)
    )
    exchanged = Exchange(me, send, stat_own.at[1], stats.at[7:14])
    total = exchanged.end()
    gate_share = stat[0:16, :]
    grad_gates = total[0:16, :]
    grad_logits = gate_share * (
        grad_gates - jnp.sum(gate_share * grad_gates, axis=0, keepdims=True)
    )
    inner = total[16:17, :] + jnp.sum(grad_logits * stat[16:32, :], axis=0, keepdims=True)
    grad_second = returned + exact(wide_router[:, mine].astype(F32), grad_logits, 0, 0)
    grad_mixed = wide_cot[mine, :].astype(F32) + scale * (
        gain * grad_second - normal * (inner * (1.0 / D))
    )
    grad_att = grad_mixed.astype(BF16)
    blocks[me.tp] = grad_att
    end_gather = start_gather_shares(me, send, blocks)
    grad_logits = exact(turn, grad_logits, 0, 0)
    small_out[0:16, :] = exact(grad_logits, second[...].astype(F32) * scale, 1, 1)
    small_out[16:24, :] = row_sums(grad_second * normal)
    small_out[24:32, :] = row_sums(grad_att.astype(F32))
    grad_logits_out[...] = grad_logits
    end_gather()
    all_normed.meet(1)
    all_normed.pass_on(2)
    for q in range(BLOCKS):
        width = min(SHARE, D - q * SHARE)
        grad_att_out[q * SHARE : q * SHARE + width, :] = blocks[q, 0:width, :]
    for copy in keep_scaled:
        copy.wait()
    all_heads.meet(1)
    for j in range(4):
        all_normed.complete(j)
    rows_copy.wait()
    cots_copy.wait()
    send.finish()


def layer(*operands):
    bf = lambda *dims: pltpu.VMEM(dims, BF16)
    fl = lambda *dims: pltpu.VMEM(dims, F32)
    return pl.pallas_call(
        layer_kernel,
        out_shape=(
            shape((512, ROWS), BF16),
            shape((128, ROWS), BF16),
            shape((8, ROWS), F32),
            shape((8, ROWS), F32),
            shape((64, ROWS), F32),
            shape((ROWS, ROWS), F32),
            shape((8, 2 * FF), F32),
            shape((D, ROWS), BF16),
            shape((SHARE, ROWS), F32),
            shape((SLOTS, ROWS), BF16),
            shape((SLOTS, ROWS), BF16),
            shape((32, SHARE), F32),
            shape((16, 128), F32),
            shape((80, 128), F32),
            shape((4, SLOTS, SHARE), BF16),
            shape((SLOTS, FF), BF16),
            shape((SLOTS, 2 * FF), BF16),
            shape((8, SLOTS, SHARE), BF16),
            shape((8, SLOTS, SHARE), BF16),
            shape((16, D, ROWS), BF16),
            shape((16, 512, ROWS), BF16),
        ),
        in_specs=[pl.BlockSpec(memory_space=pltpu.SMEM)] + vmem(11) + hbm(9),
        out_specs=tuple(vmem(14) + hbm(7)),
        scratch_shapes=[
            bf(WIDE, ROWS),
            bf(WIDE, ROWS),
            bf(WIDE, ROWS),
            bf(EXPERTS, WIDE),
            bf(D, 512),
            bf(64, D),
            bf(64, D),
            bf(D, 512),
            bf(EXPERTS, D),
            bf(FF_LOCAL, D),
            bf(2 * FF, WIDE),
            bf(FF, WIDE),
            fl(1, 2 * FF),
            bf(SLOTS, ROWS),
            bf(512, ROWS),
            fl(SHARE, ROWS),
            bf(SHARE, ROWS),
            fl(40, ROWS),
            bf(8, SHARE, ROWS),
            bf(4, SHARE, ROWS),
            bf(3, SHARE, ROWS),
            bf(3, SHARE, ROWS),
            fl(2, 24, ROWS),
            fl(14, 24, ROWS),
            bf(8, SLOTS, SHARE),
            bf(8, SLOTS, SHARE),
            bf(SLOTS, SHARE),
            bf(HALF, SHARE),
            bf(4, HALF, SHARE),
            fl(EXPERTS, 8, 128),
            fl(EXPERTS, 8, 128),
            fl(EXPERTS, 8, 128),
            fl(EXPERTS, 8, 128),
            fl(SLOTS, 2 * FF),
            bf(SLOTS, FF),
            fl(SLOTS, FF),
            bf(SLOTS, 2 * FF),
            bf(2, 4, SLOTS, SHARE),
            bf(2, 4, SLOTS, SHARE),
            bf(2, 4, SLOTS, SHARE),
            bf(2, 2, QUARTER, SHARE),
            bf(2, 2, HALF, SHARE),
            bf(2, HALF, SHARE),
            bf(SLOTS, FF),
            bf(SLOTS, 2 * FF),
            bf(8, SHARE, ROWS),
            *semaphores(320),
            pltpu.SemaphoreType.DMA((17,)),
        ],
        compiler_params=params(1, 63),
        name="layer",
    )(*operands)


def finish_kernel(
    rows, cots, scaled, grad_pre, output_grad, query_grad, key_value_grad, tokens, layer_in, small, sums, own,
    gateup_out, down_out, bias_out, output_out, query_out, key_out, value_out, tokens_out, layer_out, router_out,
    second_gain_out, output_bias_out, first_gain_out, gateup_bias_out, query_bias_out, key_bias_out, value_bias_out,
    sinks_out, router_bias_out,
):
    gateup = contract_rows(grad_pre[...], rows[0])
    gateup_out[0] = gateup[0:FF_LOCAL]
    gateup_out[1] = gateup[FF : FF + FF_LOCAL]
    both = contract_rows(scaled[...], cots[0])
    down_out[...] = both[0:FF_LOCAL]
    bias_out[...] = both[FF_LOCAL : FF_LOCAL + 1] + both[FF_LOCAL + 1 : FF_LOCAL + 2]
    output_out[...] = output_grad[...].astype(F32)
    query_out[...] = query_grad[...].astype(F32)
    turned_back = jnp.concatenate(
        [
            jnp.transpose(key_value_grad[j : j + 128, :].astype(F32))
            for j in range(0, SHARE, 128)
        ],
        axis=1,
    )
    key_out[...] = turned_back[0:64]
    value_out[...] = turned_back[64:128]
    tokens_out[...] = tokens[...].astype(F32)
    layer_out[...] = layer_in[...]
    router_out[...] = small[0, 0:16, :]
    step = pl.program_id(0)
    for line, vector in ((16, second_gain_out), (17, output_bias_out), (18, first_gain_out)):

        @pl.when(step < BLOCKS - 1)
        def _():
            vector[pl.ds(pl.multiple_of(step * SHARE, SHARE), SHARE)] = small[0, line, :]

        @pl.when(step == BLOCKS - 1)
        def _():
            vector[(BLOCKS - 1) * SHARE : D] = small[0, line, 0 : D - (BLOCKS - 1) * SHARE]

    @pl.when(step == 0)
    def _():
        gateup_bias_out[0:1, :] = sums[0:1, 0:FF_LOCAL]
        gateup_bias_out[1:2, :] = sums[0:1, FF : FF + FF_LOCAL]
        for j in range(4):
            query_bias_out[j * 128 : (j + 1) * 128] = own[j, :]
        key_bias_out[...] = own[4, 0:64]
        value_bias_out[...] = own[4, 64:128]
        router_bias_out[...] = own[5, 0:EXPERTS]
        sinks_out[...] = own[6, 0:HEADS]


def finish(*operands):
    def whole(*dims):
        return pl.BlockSpec(dims, lambda p: (0,) * len(dims))

    def lines(columns):
        return pl.BlockSpec((SHARE, columns), lambda p: (p, 0))

    def columns(count):
        return pl.BlockSpec((count, SHARE), lambda p: (0, p))

    block = pl.BlockSpec((1, SLOTS, SHARE), lambda p: (p % 2 * 4 + p // 2, 0, 0))
    return pl.pallas_call(
        finish_kernel,
        grid=(BLOCKS,),
        out_shape=(
            shape((2, FF_LOCAL, D), F32),
            shape((FF_LOCAL, D), F32),
            shape((1, D), F32),
            shape((D, 512), F32),
            shape((D, 512), F32),
            shape((64, D), F32),
            shape((64, D), F32),
            shape((D, ROWS), F32),
            shape((D, ROWS), BF16),
            shape((16, D), F32),
            shape((D,), F32),
            shape((D,), F32),
            shape((D,), F32),
            shape((2, FF_LOCAL), F32),
            shape((512,), F32),
            shape((64,), F32),
            shape((64,), F32),
            shape((HEADS,), F32),
            shape((EXPERTS,), F32),
        ),
        in_specs=[
            block, block, whole(SLOTS, FF), whole(SLOTS, 2 * FF), lines(512), lines(512), lines(128), lines(ROWS),
            lines(ROWS), pl.BlockSpec((1, 24, SHARE), lambda p: (p, 0, 0)), whole(8, 2 * FF), whole(8, 128),
        ],
        out_specs=(
            pl.BlockSpec((2, FF_LOCAL, SHARE), lambda p: (0, 0, p)),
            columns(FF_LOCAL), columns(1), lines(512), lines(512), columns(64), columns(64), lines(ROWS),
            lines(ROWS), columns(16), whole(D), whole(D), whole(D), whole(2, FF_LOCAL), whole(512), whole(64), whole(64),
            whole(HEADS), whole(EXPERTS),
        ),
        compiler_params=pltpu.CompilerParams(vmem_limit_bytes=60 * 2**20),
        cost_estimate=pl.CostEstimate(
            flops=6 * SLOTS * D * FF, bytes_accessed=44_000_000, transcendentals=0
        ),
        name="finish",
    )(*operands)


def back_kernel(
    grad_att, queries, keys_values, log_total, allowed, trig, first_scale, settings, small, grad_logits, mixed, high, low,
    results, output_weight, query_weight, key_weight, value_weight, tokens, normed_all, heads_all,
    query_grad, key_value_grad, tokens_out, layer_out, small_all, small_own, output_grad,
    N, H, Q, B, O, S, far_in, near_in, home, query_sum, rest_sum, wide_tokens, wide_att, wo, wq, wk, wv,
    part, from_sibling, sums, from_y, stat, stats, blocks, layers, line, line_x, lines_in, lines_all,
    send_sems, recv_sems, local_sems,
):
    me = Place()
    send = Sender(me, send_sems, recv_sems)
    all_here = me.greet(True, True)

    def load(source, target, n):
        copy = pltpu.make_async_copy(source, target, local_sems.at[n])
        copy.start()
        return copy

    load_results = load(results, S, 23)
    load_output = load(output_weight, wo, 0)
    load_heads = load(heads_all, H, 1)
    load_weights = [load(query_weight, wq, 2), load(key_weight, wk, 3), load(value_weight, wv, 4)]
    load_tokens = load(tokens, wide_tokens.at[0:D], 5)
    load_normed = load(normed_all, N, 6)
    wide_att[0:D, :] = grad_att[...]
    wide_att[D:, :] = jnp.zeros((WIDE - D, ROWS), BF16)
    wide_tokens[D:, :] = jnp.zeros((WIDE - D, ROWS), BF16)
    mine = pl.ds(pl.multiple_of(me.tp * SHARE, SHARE), SHARE)
    all_here()

    def lines_for(group, core):
        return pl.ds(pl.multiple_of(group * 192 + core * 96, 16), 96)

    own_half = pl.ds(pl.multiple_of(me.core * 96, 16), 96)
    other_half = pl.ds(pl.multiple_of((1 - me.core) * 96, 16), 96)
    att_in = [None]
    for k in range(1, EXPERTS):
        device = me.along_ep(k)
        att_in.append(
            send.start(wide_att.at[lines_for(device[0], me.core)], B.at[k, own_half], device)
        )
    B[0, own_half, :] = wide_att[lines_for(me.ep, me.core), :]
    load_results.wait()
    moe = RowsHome(me, send, S, far_in, near_in, home)
    for h in (0, 1):
        for step in (2, 1, 3):
            moe.begin(h, step, lax.rem(me.y + step, 4))

    load_output.wait()
    head_rows = contract_rows(grad_att[...], wo[...])
    both = keys_values[...].astype(F32)
    row_pair = jnp.transpose(both).astype(BF16)
    key_rows, value_rows = row_pair[:, 0:64], row_pair[:, 64:128]
    included = allowed[...] > 0.5
    sinks = column_of(settings[SINKS : SINKS + 1, :])
    grad_keys = jnp.zeros((64, ROWS), F32)
    grad_values = jnp.zeros((64, ROWS), F32)
    sink_line = jnp.zeros((1, 128), F32)
    place = lax.broadcasted_iota(jnp.int32, (1, 128), 1)
    factor = HEAD_SIZE**-0.5
    for h in range(HEADS):
        if h % 2 == 0:
            pair = jnp.transpose(head_rows[:, h * 64 : h * 64 + 128]).astype(BF16)
        grad_head = pair[0:64] if h % 2 == 0 else pair[64:128]
        query = queries[h * 64 : h * 64 + 64, :]
        scores = jnp.where(included, product(key_rows, query) * factor, NEGATIVE)
        logs = log_total[h : h + 1, :]
        probs = jnp.exp(scores - logs)
        grad_probs = product(value_rows, grad_head)
        delta = jnp.sum(probs * grad_probs, axis=0, keepdims=True)
        grad_scores = (probs * (grad_probs - delta)).astype(BF16)
        sunk = -jnp.sum(jnp.exp(sinks[h : h + 1, :] - logs) * delta, axis=1, keepdims=True)
        sink_line = jnp.where(place == h, sunk, sink_line)
        grad_values = grad_values + against_rows(grad_head, probs.astype(BF16))
        grad_keys = grad_keys + against_rows(query, grad_scores)
        grad_query = product(keys_values[0:64, :], grad_scores) * factor
        Q[0, h * 64 : h * 64 + 64, :] = rotate(grad_query, trig, True).astype(BF16)
    Q[0, 512:576, :] = rotate(grad_keys * factor, trig, True).astype(BF16)
    Q[0, 576:640, :] = grad_values.astype(BF16)
    all_heads = GroupGather(me, send, Q, 640, False, 256)
    all_heads.begin()
    for k in range(1, EXPERTS):
        send.arrived(att_in[k], B.at[k, own_half])
    shared = send.start(B.at[:, own_half], B.at[:, own_half], me.sibling())

    for copy in load_weights:
        copy.wait()
    all_heads.relay()
    moe.sums_on(0)
    moe.sums_on(1)

    def grad(lo, width):
        return (
            product(wq[lo : lo + width, :], Q[0, 0:512, :])
            + contract_rows(wk[:, lo : lo + width], Q[0, 512:576, :])
            + contract_rows(wv[:, lo : lo + width], Q[0, 576:640, :])
        )

    def emit(q, block):
        part[q] = block.astype(BF16)

    share_blocks(grad, emit)
    reduction = ReduceShares(me, send, part, from_sibling, sums, from_y)
    send.arrived(shared, B.at[:, other_half])
    load_heads.wait()
    O[0] = against_rows(
        jnp.concatenate([B[k] for k in range(EXPERTS)], axis=1),
        jnp.concatenate([H[k] for k in range(EXPERTS)], axis=1),
    ).astype(BF16)
    all_blocks = GroupGather(me, send, O, 192, False)
    all_blocks.begin()
    all_heads.meet()
    all_heads.begin(1)
    reduction.pair()
    all_blocks.relay()
    moe.go_home(0)
    load_normed.wait()

    def head_step(j, first=False):
        for piece, half, total in ((0, slice(0, 256), query_sum), (1, slice(256, 640), rest_sum)):
            slots = [4 * j + i if piece == 0 else 4 * i + j for i in range(4)]
            right = jnp.concatenate([Q[k, half, :] for k in slots], axis=1)

            @pl.loop(0, 4)
            def _(r):
                span = pl.ds(pl.multiple_of(r * 720, 16), 720)
                left = jnp.concatenate([N[k, span, :] for k in slots], axis=1)
                value = against_rows(left, right)
                if not first:
                    value = value + total[span, :]
                total[span, :] = value

    head_step(0, True)
    moe.go_home(1)
    all_heads.relay(1)
    load_tokens.wait()
    gain = column_share(settings, FIRST_GAIN, me)
    scale = first_scale[0:1, :]
    normal = wide_tokens[mine, :].astype(F32) * scale
    grad_normed = reduction.end()
    raised = gain * grad_normed
    stat[...] = jnp.broadcast_to(jnp.sum(raised * normal, axis=0, keepdims=True), (8, ROWS))
    exchanged = Exchange(me, send, stat, stats)

    line[0:17, :] = small[0:17, :]
    line[17:18, :] = small[24:25, :]
    line[18:19, :] = row_sums(grad_normed * normal)[0:1]
    router_bias = row_sums(grad_logits[...])[0:1]
    line[19:20, :] = jnp.concatenate([router_bias, jnp.zeros((1, SHARE - 16), F32)], axis=1)
    line[20:21, :] = jnp.concatenate([sink_line, jnp.zeros((1, SHARE - 128), F32)], axis=1)
    head_sums = row_sums(Q[0].astype(F32))
    line[21:22, :] = head_sums[0:1, 0:SHARE]
    line[22:23, :] = jnp.concatenate(
        [head_sums[0:1, SHARE:640], jnp.zeros((1, 2 * SHARE - 640), F32)], axis=1
    )
    line[23:24, :] = jnp.zeros((1, SHARE), F32)
    tickets = [send.start(line, lines_in.at[d - 1], me.along_ep(d)) for d in (1, 2, 3)]
    all_blocks.meet()
    all_blocks.begin(1)
    head_step(1)
    total = exchanged.end()
    grad_tokens = wide_att[mine, :].astype(F32) + scale * (
        raised - normal * (total[0:1, :] * (1.0 / D))
    )
    blocks[me.tp] = grad_tokens.astype(BF16)
    end_gather = start_gather_shares(me, send, blocks)
    moe.is_home(0)
    moe.is_home(1)
    share = mixed[...]
    for h, lines in ((0, slice(0, HALF)), (1, slice(HALF, SLOTS))):
        share = share + contract_rows(home[h], high[lines, :]) + contract_rows(home[h], low[lines, :])
    layers[me.tp] = share.astype(BF16)
    end_layers = start_gather_shares(me, send, layers)
    head_step(3)
    summed = line[...]
    for k, n in enumerate(tickets):
        send.arrived(n, lines_in.at[k])
        summed = summed + lines_in[k]
    line_x[...] = summed
    tickets = [send.start(line_x, lines_in.at[2 + d], me.along_ep(4 * d)) for d in (1, 2, 3)]
    all_heads.meet(1)
    head_step(2)
    all_blocks.relay(1)
    end_gather()
    tokens_out[...] = blocks[...]
    summed = line_x[...]
    for k, n in enumerate(tickets):
        send.arrived(n, lines_in.at[3 + k])
        summed = summed + lines_in[3 + k]
    lines_all[me.tp] = summed
    for j in range(3):
        small_own[j : j + 1, :] = summed[21:22, j * 128 : (j + 1) * 128]
    for j in range(2):
        small_own[3 + j : 4 + j, :] = summed[22:23, j * 128 : (j + 1) * 128]
    small_own[5:6, :] = summed[19:20, 0:128]
    small_own[6:7, :] = summed[20:21, 0:128]
    small_own[7:8, :] = jnp.zeros((1, 128), F32)
    end_lines = start_gather_shares(me, send, lines_all)
    query_grad[...] = jnp.concatenate([query_sum[...], rest_sum[:, 0:256]], axis=1).astype(BF16)
    key_value_grad[...] = rest_sum[:, 256:384].astype(BF16)
    end_layers()
    for q in range(BLOCKS):
        width = min(SHARE, D - q * SHARE)
        layer_out[q * SHARE : q * SHARE + width, :] = layers[q, 0:width, :]
    end_lines()
    small_all[...] = lines_all[...]
    all_blocks.meet(1)
    keep = [load(O.at[k], output_grad.at[me.back_ep(k)[0]], 7 + k) for k in range(EXPERTS)]
    for copy in keep:
        copy.wait()
    send.finish()


def back(*operands):
    bf = lambda *dims: pltpu.VMEM(dims, BF16)
    fl = lambda *dims: pltpu.VMEM(dims, F32)
    return pl.pallas_call(
        back_kernel,
        out_shape=(
            shape((D, 512), BF16),
            shape((D, 128), BF16),
            shape((8, SHARE, ROWS), BF16),
            shape((D, ROWS), BF16),
            shape((8, 24, SHARE), F32),
            shape((8, 128), F32),
            shape((16, 192, 512), BF16),
        ),
        in_specs=vmem(13) + hbm(8),
        out_specs=tuple(vmem(6) + hbm(1)),
        scratch_shapes=[
            bf(16, D, ROWS),
            bf(16, 512, ROWS),
            bf(16, 640, ROWS),
            bf(16, 192, ROWS),
            bf(16, 192, 512),
            bf(4, SLOTS, SHARE),
            bf(2, 2, QUARTER, SHARE),
            bf(2, 2, HALF, SHARE),
            bf(2, HALF, SHARE),
            fl(D, 256),
            fl(D, 384),
            bf(WIDE, ROWS),
            bf(WIDE, ROWS),
            bf(D, 512),
            bf(D, 512),
            bf(64, D),
            bf(64, D),
            bf(8, SHARE, ROWS),
            bf(4, SHARE, ROWS),
            bf(3, SHARE, ROWS),
            bf(3, SHARE, ROWS),
            fl(8, ROWS),
            fl(7, 8, ROWS),
            bf(8, SHARE, ROWS),
            bf(8, SHARE, ROWS),
            fl(24, SHARE),
            fl(24, SHARE),
            fl(6, 24, SHARE),
            fl(8, 24, SHARE),
            *semaphores(200),
            pltpu.SemaphoreType.DMA((24,)),
        ],
        compiler_params=params(3, 63),
        name="back",
    )(*operands)


def shards(
    tokens,
    seq_lengths,
    expert_ids,
    first_gain,
    query_weight,
    key_matrix,
    value_matrix,
    query_bias,
    key_offset_bias,
    value_offset_bias,
    head_sink_logits,
    output_weight,
    output_bias,
    second_gain,
    router_weight,
    router_bias,
    expert_gateup,
    gateup_bias,
    expert_down,
    down_bias,
    cotangent,
):
    (
        queries, keys_values, log_total, first_scale, trig, allowed, bias_sums,
        grad_att, mixed, high, low, small, grad_logits, settings, results, scaled_hidden, grad_pre, expert_rows, cot_rows, normed_all, heads_all,
    ) = layer(
        seq_lengths.T, expert_ids.T, output_bias, second_gain, first_gain, query_bias, key_offset_bias,
        value_offset_bias, router_bias, head_sink_logits, gateup_bias[0], down_bias, tokens.T, cotangent.T, query_weight,
        key_matrix.T, value_matrix.T, output_weight.T, router_weight.T,
        jnp.swapaxes(expert_gateup[0], 1, 2), expert_down[0],
    )
    query_grad, key_value_grad, token_blocks, layer_t, small_all, small_own, output_blocks = back(
        grad_att, queries, keys_values, log_total, allowed, trig, first_scale, settings, small, grad_logits,
        mixed, high, low, results, output_weight.T, query_weight, key_matrix.T, value_matrix.T, tokens.T, normed_all, heads_all,
    )
    (
        grad_gateup, grad_down, grad_down_bias, output_grad, query_out, key_out, value_out, tokens_out, layer_out,
        router_out, second_gain_out, output_bias_out, first_gain_out, gateup_bias_out, query_bias_out, key_bias_out,
        value_bias_out, sinks_out, router_bias_out,
    ) = finish(
        expert_rows, cot_rows, scaled_hidden, grad_pre, output_blocks.reshape(WIDE, 512), query_grad,
        key_value_grad, token_blocks.reshape(WIDE, ROWS), layer_t, small_all, bias_sums, small_own,
    )
    return (
        layer_out.T,
        tokens_out.T,
        first_gain_out,
        query_out,
        key_out.T,
        value_out.T,
        query_bias_out,
        key_bias_out,
        value_bias_out,
        sinks_out,
        output_grad.T,
        output_bias_out,
        second_gain_out,
        router_out.T,
        router_bias_out,
        jnp.swapaxes(grad_gateup, 1, 2)[None],
        gateup_bias_out[None],
        grad_down[None],
        grad_down_bias,
    )


def solution(mesh):
    in_specs = (
        P("ep", None),
        P(),
        P("ep", None),
        P(),
        P(None, "tp"),
        P(None, "tp"),
        P(None, "tp"),
        P("tp"),
        P("tp"),
        P("tp"),
        P("tp"),
        P("tp", None),
        P(),
        P(),
        P(),
        P(),
        P("ep", None, None, "tp"),
        P("ep", None, "tp"),
        P("ep", "tp", None),
        P("ep", None),
        P("ep", None),
    )
    out_specs = (
        P("ep", None),
        P("ep", None),
        P(),
        P(None, "tp"),
        P(None, "tp"),
        P(None, "tp"),
        P("tp"),
        P("tp"),
        P("tp"),
        P("tp"),
        P("tp", None),
        P(),
        P(),
        P(),
        P(),
        P("ep", None, None, "tp"),
        P("ep", None, "tp"),
        P("ep", "tp", None),
        P("ep", None),
    )
    return jax.shard_map(shards, mesh=mesh, in_specs=in_specs, out_specs=out_specs, check_vma=False)
```
